32 devices in a mesh: dp: 8 (over y, x, core), seq: 4 (over z).
Axes of the slice: x: 2, y: 2, z: 4, core: 2. Of those that a mesh axis runs over, the one named last changes fastest.
Arguments:
- tokens: bfloat16 [32, 1024, 576], P('dp', 'seq'), may hold values from -6 to 6
- lengths: int32 [32], P('dp'), may hold values from 256 to 1024, as said below
- w_query: bfloat16 [576, 576], replicated, may hold values from -0.25 to 0.25
- w_key: bfloat16 [576, 192], replicated, may hold values from -0.25 to 0.25
- w_value: bfloat16 [576, 192], replicated, may hold values from -0.25 to 0.25
- w_out: bfloat16 [576, 576], replicated, may hold values from -1 to 1
- w_gate: bfloat16 [576, 1536], replicated, may hold values from -0.25 to 0.25
- w_up: bfloat16 [576, 1536], replicated, may hold values from -0.25 to 0.25
- w_down: bfloat16 [1536, 576], replicated, may hold values from -0.15625 to 0.15625
- gain_attn: float32 [576], replicated, may hold values from 0.1 to 1.9
- gain_ffn: float32 [576], replicated, may hold values from 0.1 to 1.9
- cotangent: bfloat16 [32, 1024, 576], P('dp', 'seq'), may hold values from -6 to 6
Outputs:
- mixed: bfloat16 [32, 1024, 576], P('dp', 'seq')
- tokens_grad: bfloat16 [32, 1024, 576], P('dp', 'seq')
- w_query_grad: float32 [576, 576], replicated
- w_key_grad: float32 [576, 192], replicated
- w_value_grad: float32 [576, 192], replicated
- w_out_grad: float32 [576, 576], replicated
- w_gate_grad: float32 [576, 1536], replicated
- w_up_grad: float32 [576, 1536], replicated
- w_down_grad: float32 [1536, 576], replicated
- gain_attn_grad: float32 [576], replicated
- gain_ffn_grad: float32 [576], replicated
The draws below stay inside these ranges and needn't reach their ends.
Inputs may be any that keep to these rules, and one draw needn't show every extreme that they name: A row's real tokens are its first lengths entries; among the 4 rows of each index of dp one row has exactly 1024.
All inputs are finite; a program needn't handle non-finite values.
Results may differ from the reference program's by a relative error of at most 0.03.
Values may be sent and summed in bfloat16 or wider, within the bound.
No kernel may reach another device: no remote copies, remote signals or barrier semaphores. Data moves between devices by JAX's collectives and lax.ppermute only.
A program may use at most 128 MiB of HBM per device.

```python
import math
import jax
import jax.numpy as jnp
from jax import lax

D = 576
HQ = 9
HK = 3
DH = 64
FF = 1536
ROWS = 4
BLK = 256
BATCH = 32
SEQ_LEN = 1024


def draw_lengths(key, part):
    key = jax.random.fold_in(key, 7)
    first_key, second_key = jax.random.split(key)
    drawn_len = jax.random.randint(first_key, (BATCH,), BLK, SEQ_LEN + 1)
    chosen_row = jax.random.randint(second_key, (BATCH // ROWS,), 0, ROWS)
    row_index = jnp.arange(BATCH, dtype=jnp.int32)
    longest = row_index % ROWS == jnp.repeat(chosen_row, ROWS)
    return jnp.where(longest, SEQ_LEN, drawn_len).astype(jnp.int32)


def steps_of(key, extent, pieces, low, top_value):
    level, own = 1.0, jax.random.fold_in(key, 6)
    for axis_at, blocks in pieces:
        heights = jnp.exp(jax.random.uniform(jax.random.fold_in(own, axis_at), (blocks,), jnp.float32, low / len(pieces), top_value / len(pieces)))
        level = level * jnp.repeat(heights, extent[axis_at] // blocks).reshape([-1 if axis == axis_at else 1 for axis in range(len(extent))])
    return level


def noise(key, extent, deviation, reach, cuts=(), held_as=jnp.bfloat16):
    loudness = steps_of(key, extent, cuts, -0.22, 0.18) if cuts else 1.0
    array = jax.random.normal(key, extent, jnp.float32) * deviation * loudness
    return jnp.minimum(jnp.maximum(array, -reach), reach).astype(held_as)


def setup_inputs(seed: int = 0) -> dict:
    streams_of = jax.random.split(jax.random.key(seed), 13)
    tokens = noise(streams_of[0], (BATCH, SEQ_LEN, D), 1.0, 6.0, ((0, 8), (1, 4)))
    lengths = draw_lengths(jax.random.fold_in(streams_of[12], 71), 0)
    w_query = noise(streams_of[2], (D, HQ * DH), D ** -0.5, 0.25)
    w_key = noise(streams_of[3], (D, HK * DH), D ** -0.5, 0.25)
    w_value = noise(streams_of[4], (D, HK * DH), D ** -0.5, 0.25)
    w_out = noise(streams_of[5], (HQ * DH, D), (HQ * DH // 16) ** -0.5, 1.0)
    w_gate = noise(streams_of[6], (D, FF), D ** -0.5, 0.25)
    w_up = noise(streams_of[7], (D, FF), D ** -0.5, 0.25)
    w_down = noise(streams_of[8], (FF, D), FF ** -0.5, 0.15625)
    gain_attn = jnp.clip(1.0 + 0.18 * jax.random.normal(streams_of[9], (D,), jnp.float32), 0.1, 1.9)
    gain_ffn = jnp.clip(1.0 + 0.18 * jax.random.normal(streams_of[10], (D,), jnp.float32), 0.1, 1.9)
    cotangent = noise(streams_of[11], (BATCH, SEQ_LEN, D), 1.0, 6.0, ((0, 8), (1, 4)))
    return dict(tokens=tokens, lengths=lengths, w_query=w_query, w_key=w_key, w_value=w_value, w_out=w_out, w_gate=w_gate, w_up=w_up, w_down=w_down, gain_attn=gain_attn, gain_ffn=gain_ffn, cotangent=cotangent)


@jax.custom_vjp
def low(v):
    return lax.optimization_barrier(v.astype(jnp.bfloat16)).astype(jnp.float32)

@jax.custom_vjp
def low_back(v):
    return v

def low_keep(v):
    return (low(v), None)

def low_pass(kept, grad):
    return (grad,)

def back_keep(v):
    return (v, None)

def back_low(kept, grad):
    return (low(grad),)
low.defvjp(low_keep, low_pass)
low_back.defvjp(back_keep, back_low)
eps_norm = 1e-05
rope_base = 100000.0
neg_large = -1e+30

def matmul(left, right):
    return jnp.dot(left, right, precision=lax.Precision.HIGHEST)

def norm_rows(values, gain_vec):
    return values * lax.rsqrt(lax.optimization_barrier(jnp.mean(values * values, axis=-1, keepdims=True)) + eps_norm) * gain_vec

def rotate(values, positions):
    half_dim = values.shape[-1] // 2
    frequency = rope_base ** (-jnp.arange(half_dim, dtype=jnp.float32) / half_dim)
    angles = positions.astype(jnp.float32)[:, None] * frequency[None, :]
    cosine = jnp.cos(angles)[:, None, :]
    sine_part = jnp.sin(angles)[:, None, :]
    first_half = values[..., :half_dim]
    second_half = values[..., half_dim:]
    return jnp.concatenate([first_half * cosine - second_half * sine_part, second_half * cosine + first_half * sine_part], axis=-1)

def attention(query_heads, key_heads, value_heads, lengths):
    row_count, seq_len = (query_heads.shape[0], query_heads.shape[1])
    group_size = HQ // HK
    block_len = math.gcd(512, seq_len)
    query_blocks = query_heads.reshape(row_count, seq_len // block_len, block_len, HK, group_size, DH)
    starts = jnp.arange(seq_len // block_len, dtype=jnp.int32) * block_len
    key_pos = jnp.arange(seq_len, dtype=jnp.int32)

    def one_block(block_items):
        query_block, block_start = block_items
        query_pos = block_start + jnp.arange(block_len, dtype=jnp.int32)
        scores = jnp.einsum('rqhgd,rkhd->rhgqk', query_block, key_heads, precision=lax.Precision.HIGHEST) / math.sqrt(DH)
        scores = low_back(scores)
        allowed = (key_pos[None, None, :] <= query_pos[None, :, None]) & (key_pos[None, None, :] < lengths[:, None, None])
        scores = jnp.where(allowed[:, None, None], scores, neg_large)
        row_max = lax.optimization_barrier(jnp.max(scores, axis=-1, keepdims=True))
        exp_scores = jnp.exp(scores - row_max)
        probabilities = exp_scores / lax.optimization_barrier(jnp.sum(exp_scores, axis=-1, keepdims=True))
        block_out = jnp.einsum('rhgqk,rkhd->rqhgd', low(probabilities), value_heads, precision=lax.Precision.HIGHEST)
        live_rows = query_pos[None, :] < lengths[:, None]
        return jnp.where(live_rows[:, :, None, None, None], block_out, 0.0)
    block_outs = lax.map(jax.checkpoint(one_block), (jnp.moveaxis(query_blocks, 1, 0), starts))
    return jnp.moveaxis(block_outs, 0, 1).reshape(row_count, seq_len, HQ * DH)

def block_layer(inputs, lengths, weights):
    w_query, w_key, w_value, w_out, w_gate, w_up, w_down, gain_attn, gain_ffn = weights
    row_count, seq_len, model_width = inputs.shape
    positions = jnp.arange(seq_len, dtype=jnp.int32)
    attn_in = low(norm_rows(inputs, gain_attn)).reshape(-1, model_width)
    query_pre = low_back(matmul(attn_in, w_query)).reshape(row_count, seq_len, HQ, DH)
    query_heads = low(rotate(query_pre, positions)).reshape(row_count, seq_len, HK, HQ // HK, DH)
    key_pre = low_back(matmul(attn_in, w_key)).reshape(row_count, seq_len, HK, DH)
    key_heads = low(rotate(key_pre, positions))
    value_heads = low(low_back(matmul(attn_in, w_value))).reshape(row_count, seq_len, HK, DH)
    attended = attention(query_heads, key_heads, value_heads, lengths)
    attn_low = low(low_back(attended)).reshape(-1, HQ * DH)
    residual = inputs + low_back(matmul(attn_low, w_out)).reshape(row_count, seq_len, model_width)
    ffn_in = low(norm_rows(residual, gain_ffn)).reshape(-1, model_width)
    gate_proj = low_back(matmul(ffn_in, w_gate))
    up_proj = low_back(matmul(ffn_in, w_up))
    hidden = low(jax.nn.silu(gate_proj) * up_proj)
    branch = low_back(matmul(hidden, w_down)).reshape(row_count, seq_len, model_width)
    return residual + branch

def reference(tokens, lengths, w_query, w_key, w_value, w_out, w_gate, w_up, w_down, gain_attn, gain_ffn, cotangent):
    weights = tuple((weight_item.astype(jnp.float32) for weight_item in (w_query, w_key, w_value, w_out, w_gate, w_up, w_down, gain_attn, gain_ffn)))
    groups = BATCH // ROWS
    token_groups = tokens.astype(jnp.float32).reshape(groups, ROWS, SEQ_LEN, D)
    length_groups = lengths.reshape(groups, ROWS)
    cot_groups = cotangent.astype(jnp.float32).reshape(groups, ROWS, SEQ_LEN, D)

    def one_group(totals, group_items):
        group_tokens, group_lengths, group_cot = group_items
        result, pullback = jax.vjp(lambda inputs, params: block_layer(inputs, group_lengths, params), group_tokens, weights)
        grad_in, grad_params = pullback(group_cot)
        totals = tuple((total_item + new_item for total_item, new_item in zip(totals, grad_params)))
        return (totals, (result.astype(jnp.bfloat16), grad_in.astype(jnp.bfloat16)))
    start_totals = tuple((jnp.zeros_like(weight_item) for weight_item in weights))
    totals, (mixed, input_grad) = lax.scan(one_group, start_totals, (token_groups, length_groups, cot_groups))
    return (mixed.reshape(BATCH, SEQ_LEN, D), input_grad.reshape(BATCH, SEQ_LEN, D), totals[0], totals[1], totals[2], totals[3], totals[4], totals[5], totals[6], totals[7], totals[8])
```

```python
from functools import partial
import math

import jax
import jax.numpy as jnp
from jax import lax
from jax.experimental import pallas as pl
from jax.experimental.pallas import tpu as pltpu
from jax.sharding import PartitionSpec as P

HQ = 9
HK = 3
DH = 64


eps_norm = 1e-05
rope_base = 100000.0
neg_large = -1e30


def norm_rows(values, gain_vec):
    return (
        values * lax.rsqrt(jnp.mean(values * values, axis=-1, keepdims=True) + eps_norm) * gain_vec
    )


def rotate(values, positions, turn_sign):
    half_dim = values.shape[-1] // 2
    frequency = rope_base ** (-jnp.arange(half_dim, dtype=jnp.float32) / half_dim)
    angles = turn_sign * positions.astype(jnp.float32)[:, None] * frequency[None, :]
    cosine = jnp.cos(angles)[:, None, :]
    sine_part = jnp.sin(angles)[:, None, :]
    first_half = values[..., :half_dim]
    second_half = values[..., half_dim:]
    return jnp.concatenate(
        [
            first_half * cosine - second_half * sine_part,
            second_half * cosine + first_half * sine_part,
        ],
        axis=-1,
    )


def inner_rows(left, right):
    return lax.dot_general(
        left, right, (((0,), (0,)), ((), ())), preferred_element_type=jnp.float32
    )


def times_t(left, right):
    return lax.dot_general(
        left, right, (((1,), (1,)), ((), ())), preferred_element_type=jnp.float32
    )


def fold_piece(block_len, step_fn, carry, pieces):
    piece_count = pieces.shape[1] // block_len

    def inner_step(index_step, state):
        part_piece = lax.dynamic_slice_in_dim(pieces, index_step * block_len, block_len, 1)
        return step_fn(state, part_piece, index_step * block_len)

    return lax.fori_loop(0, piece_count, inner_step, carry)


def local_general(
    tokens,
    lengths,
    w_query,
    w_key,
    w_value,
    w_out,
    w_gate,
    w_up,
    w_down,
    gain_attn,
    gain_ffn,
    cotangent,
):
    row_count, block_len, model_width = tokens.shape
    group_size = HQ // HK
    kv_width = HK * DH
    score_scale = 1.0 / math.sqrt(DH)
    seq_devices = lax.axis_size("seq")
    my_start = lax.axis_index("seq") * block_len
    positions = my_start + jnp.arange(block_len, dtype=jnp.int32)
    longest = jnp.max(lengths)
    live_rows = positions[None, :] < lengths[:, None]
    query_active = my_start < longest
    inputs = tokens.reshape(-1, model_width).astype(jnp.float32)
    attn_norm, attn_pull = jax.vjp(norm_rows, inputs, gain_attn)
    attn_in = attn_norm.astype(jnp.bfloat16)
    query_pre = jnp.dot(attn_in, w_query, preferred_element_type=jnp.float32)
    query_heads = rotate(query_pre.reshape(row_count, block_len, HQ, DH), positions, 1.0).astype(
        jnp.bfloat16
    )
    query_heads = query_heads.reshape(row_count, block_len, HK, group_size, DH)
    key_pre = jnp.dot(attn_in, w_key, preferred_element_type=jnp.float32)
    key_heads = rotate(key_pre.reshape(row_count, block_len, HK, DH), positions, 1.0).astype(
        jnp.bfloat16
    )
    value_heads = jnp.dot(attn_in, w_value, preferred_element_type=jnp.float32).astype(jnp.bfloat16)
    key_value = jnp.concatenate(
        [
            key_heads.reshape(row_count, block_len, kv_width),
            value_heads.reshape(row_count, block_len, kv_width),
        ],
        axis=-1,
    )

    def allowed_for(piece_start):
        key_pos = piece_start + jnp.arange(block_len, dtype=jnp.int32)
        causal = key_pos[None, None, :] <= positions[None, :, None]
        inside = key_pos[None, None, :] < lengths[:, None, None]
        return causal & inside

    def needed_for(piece_start):
        return (piece_start <= my_start) & (piece_start < longest) & query_active

    def split_piece(pieces):
        key_part = pieces[..., :kv_width].reshape(row_count, block_len, HK, DH)
        value_part = pieces[..., kv_width:].reshape(row_count, block_len, HK, DH)
        return (key_part, value_part)

    def forward_block(carry, pieces, piece_start):

        def forward_compute_block(state):
            row_max, row_total, weighted = state
            key_part, value_part = split_piece(pieces)
            scores = (
                jnp.einsum(
                    "rqhgd,rkhd->rhgqk", query_heads, key_part, preferred_element_type=jnp.float32
                )
                * score_scale
            )
            allowed = allowed_for(piece_start)[:, None, None]
            scores = jnp.where(allowed, scores, neg_large)
            new_max = jnp.maximum(row_max, jnp.max(scores, axis=-1))
            shrink = jnp.exp(row_max - new_max)
            exp_scores = jnp.where(allowed, jnp.exp(scores - new_max[..., None]), 0.0)
            row_total = row_total * shrink + jnp.sum(exp_scores, axis=-1)
            update = jnp.einsum(
                "rhgqk,rkhd->rqhgd",
                exp_scores.astype(jnp.bfloat16),
                value_part,
                preferred_element_type=jnp.float32,
            )
            weighted = weighted * jnp.moveaxis(shrink, 3, 1)[..., None] + update
            return (new_max, row_total, weighted)

        return lax.cond(needed_for(piece_start), forward_compute_block, lambda state: state, carry)

    stat_shape = (row_count, HK, group_size, block_len)
    forward_init = (
        jnp.full(stat_shape, neg_large, jnp.float32),
        jnp.zeros(stat_shape, jnp.float32),
        jnp.zeros((row_count, block_len, HK, group_size, DH), jnp.float32),
    )
    forward_state = fold_piece(
        block_len, forward_block, forward_init, lax.all_gather(key_value, "seq", axis=1, tiled=True)
    )
    row_max, row_total, weighted = forward_state
    safe_total = jnp.where(row_total > 0, row_total, 1.0)
    attn_heads = weighted / jnp.moveaxis(safe_total, 3, 1)[..., None]
    attn_heads = jnp.where(live_rows[:, :, None, None, None], attn_heads, 0.0)
    log_sum = jnp.where(live_rows[:, None, None, :], row_max + jnp.log(safe_total), 0.0)
    attn_low = attn_heads.reshape(-1, HQ * DH).astype(jnp.bfloat16)
    residual = inputs + jnp.dot(attn_low, w_out, preferred_element_type=jnp.float32)
    ffn_norm, ffn_pull = jax.vjp(norm_rows, residual, gain_ffn)
    ffn_in = ffn_norm.astype(jnp.bfloat16)
    gate_proj = jnp.dot(ffn_in, w_gate, preferred_element_type=jnp.float32)
    up_proj = jnp.dot(ffn_in, w_up, preferred_element_type=jnp.float32)
    product, swiglu_pull = jax.vjp(
        lambda gate_in, up_in: jax.nn.silu(gate_in) * up_in, gate_proj, up_proj
    )
    hidden = product.astype(jnp.bfloat16)
    branch = jnp.dot(hidden, w_down, preferred_element_type=jnp.float32)
    mixed = (residual + branch).astype(jnp.bfloat16).reshape(row_count, block_len, model_width)
    out_low = cotangent.reshape(-1, model_width)
    out_grad = out_low.astype(jnp.float32)
    w_down_grad = inner_rows(hidden, out_low)
    hidden_grad = times_t(out_low, w_down)
    gate_grad, up_grad = swiglu_pull(hidden_grad)
    gate_low = gate_grad.astype(jnp.bfloat16)
    up_low = up_grad.astype(jnp.bfloat16)
    w_gate_grad = inner_rows(ffn_in, gate_low)
    w_up_grad = inner_rows(ffn_in, up_low)
    ffn_in_grad = times_t(gate_low, w_gate) + times_t(up_low, w_up)
    residual_part, gain_ffn_grad = ffn_pull(ffn_in_grad)
    residual_grad = out_grad + residual_part
    residual_low = residual_grad.astype(jnp.bfloat16)
    w_out_grad = inner_rows(attn_low, residual_low)
    attended_grad = times_t(residual_low, w_out).reshape(row_count, block_len, HK, group_size, DH)
    attended_grad = jnp.where(live_rows[:, :, None, None, None], attended_grad, 0.0).astype(
        jnp.bfloat16
    )
    grad_dot = jnp.moveaxis(jnp.sum(attended_grad.astype(jnp.float32) * attn_heads, axis=-1), 1, 3)

    def backward_block(with_kv, carry, pieces, piece_start):

        def backward_compute_block(state):
            key_part, value_part = split_piece(pieces)
            scores = (
                jnp.einsum(
                    "rqhgd,rkhd->rhgqk", query_heads, key_part, preferred_element_type=jnp.float32
                )
                * score_scale
            )
            allowed = allowed_for(piece_start)[:, None, None]
            weights_now = jnp.where(allowed, jnp.exp(scores - log_sum[..., None]), 0.0)
            weights_grad = jnp.einsum(
                "rqhgd,rkhd->rhgqk", attended_grad, value_part, preferred_element_type=jnp.float32
            )
            score_grad = (weights_now * (weights_grad - grad_dot[..., None])).astype(jnp.bfloat16)
            query_grad = (
                state[0]
                + jnp.einsum(
                    "rhgqk,rkhd->rqhgd", score_grad, key_part, preferred_element_type=jnp.float32
                )
                * score_scale
            )
            kv_grad = state[1]
            values_grad = jnp.einsum(
                "rhgqk,rqhgd->rkhd",
                weights_now.astype(jnp.bfloat16),
                attended_grad,
                preferred_element_type=jnp.float32,
            )
            keys_grad = (
                jnp.einsum(
                    "rhgqk,rqhgd->rkhd", score_grad, query_heads, preferred_element_type=jnp.float32
                )
                * score_scale
            )
            local_kv = jnp.concatenate(
                [
                    keys_grad.reshape(row_count, block_len, kv_width),
                    values_grad.reshape(row_count, block_len, kv_width),
                ],
                axis=-1,
            )
            current = lax.dynamic_slice_in_dim(kv_grad, piece_start, block_len, 1)
            kv_grad = lax.dynamic_update_slice_in_dim(kv_grad, current + local_kv, piece_start, 1)
            return (query_grad, kv_grad)

        return lax.cond(needed_for(piece_start), backward_compute_block, lambda state: state, carry)

    query_zero = jnp.zeros((row_count, block_len, HK, group_size, DH), jnp.float32)
    backward_init = (
        query_zero,
        jnp.zeros((row_count, block_len * seq_devices, 2 * kv_width), jnp.float32),
    )
    step_back = partial(backward_block, True)
    backward_state = fold_piece(
        block_len, step_back, backward_init, lax.all_gather(key_value, "seq", axis=1, tiled=True)
    )
    query_grad = backward_state[0]
    own_kv_grad = lax.psum_scatter(
        backward_state[1].astype(jnp.bfloat16), "seq", scatter_dimension=1, tiled=True
    ).astype(jnp.float32)
    query_low = (
        rotate(query_grad.reshape(row_count, block_len, HQ, DH), positions, -1.0)
        .astype(jnp.bfloat16)
        .reshape(-1, HQ * DH)
    )
    key_low = (
        rotate(own_kv_grad[..., :kv_width].reshape(row_count, block_len, HK, DH), positions, -1.0)
        .astype(jnp.bfloat16)
        .reshape(-1, kv_width)
    )
    value_low = own_kv_grad[..., kv_width:].astype(jnp.bfloat16).reshape(-1, kv_width)
    w_query_grad = inner_rows(attn_in, query_low)
    w_key_grad = inner_rows(attn_in, key_low)
    w_value_grad = inner_rows(attn_in, value_low)
    attn_in_grad = (
        times_t(query_low, w_query) + times_t(key_low, w_key) + times_t(value_low, w_value)
    )
    inputs_part, gain_attn_grad = attn_pull(attn_in_grad)
    tokens_grad = (
        (residual_grad + inputs_part)
        .astype(jnp.bfloat16)
        .reshape(row_count, block_len, model_width)
    )
    (
        w_query_grad,
        w_key_grad,
        w_value_grad,
        w_out_grad,
        w_gate_grad,
        w_up_grad,
        w_down_grad,
        gain_attn_grad,
        gain_ffn_grad,
    ) = lax.psum(
        (
            w_query_grad,
            w_key_grad,
            w_value_grad,
            w_out_grad,
            w_gate_grad,
            w_up_grad,
            w_down_grad,
            gain_attn_grad,
            gain_ffn_grad,
        ),
        ("dp", "seq"),
    )
    return (
        mixed,
        tokens_grad,
        w_query_grad,
        w_key_grad,
        w_value_grad,
        w_out_grad,
        w_gate_grad,
        w_up_grad,
        w_down_grad,
        gain_attn_grad,
        gain_ffn_grad,
    )


GROUP = HQ // HK
QBLK = 256


def mul_nt(left, right):
    return lax.dot_general(
        left, right, (((1,), (1,)), ((), ())), preferred_element_type=jnp.float32
    )


def mul_nn(left, right):
    return lax.dot_general(
        left, right, (((1,), (0,)), ((), ())), preferred_element_type=jnp.float32
    )


def turn(values, cosine, sine_part):
    first_half, second_half = values[: DH // 2], values[DH // 2 :]
    return jnp.concatenate(
        [
            first_half * cosine - second_half * sine_part,
            second_half * cosine + first_half * sine_part,
        ],
        axis=0,
    )


def causal_mask():
    key_at = lax.broadcasted_iota(jnp.int32, (QBLK, QBLK), 0)
    query_at = lax.broadcasted_iota(jnp.int32, (QBLK, QBLK), 1)
    return jnp.concatenate([key_at <= query_at] * GROUP, axis=1)


def heads_of(ref, cols):
    return jnp.concatenate([ref[j * DH : (j + 1) * DH, cols] for j in range(GROUP)], axis=1)


def attend_kernel(
    length_ref,
    attn_in_ref,
    weights_ref,
    cos_ref,
    sin_ref,
    query_ref,
    key_ref,
    value_ref,
    out_ref,
    lse_ref,
    key_rows,
):
    seq_len = attn_in_ref.shape[0]
    attn_in = attn_in_ref[...]
    cosine, sine_part = cos_ref[...], sin_ref[...]
    for j in range(GROUP):
        pre = mul_nt(weights_ref[0, j * DH : (j + 1) * DH], attn_in)
        query_ref[j * DH : (j + 1) * DH] = (turn(pre, cosine, sine_part) * DH**-0.5).astype(
            jnp.bfloat16
        )
    pre = mul_nt(weights_ref[0, GROUP * DH : (GROUP + 1) * DH], attn_in)
    keys = turn(pre, cosine, sine_part).astype(jnp.bfloat16)
    key_ref[...] = keys
    key_rows[...] = keys.T
    value_ref[...] = mul_nt(weights_ref[0, (GROUP + 1) * DH :], attn_in).astype(jnp.bfloat16)
    mask = causal_mask()
    for at in range(seq_len // QBLK):
        cols = slice(at * QBLK, (at + 1) * QBLK)
        queries = heads_of(query_ref, cols)
        scores, top = [], None
        for k in range(at + 1):
            part = mul_nn(key_rows[k * QBLK : (k + 1) * QBLK], queries)
            if k == at:
                part = jnp.where(mask, part, neg_large)
            scores.append(part)
            part_top = jnp.max(part, axis=0, keepdims=True)
            top = part_top if top is None else jnp.maximum(top, part_top)
        total, weighted = 0.0, 0.0
        for k in range(at + 1):
            weights_now = jnp.exp(scores[k] - top)
            total = total + jnp.sum(weights_now, axis=0, keepdims=True)
            weighted = weighted + mul_nn(
                value_ref[:, k * QBLK : (k + 1) * QBLK], weights_now.astype(jnp.bfloat16)
            )
        weighted = weighted * (1.0 / total)
        log_sum = top + jnp.log(total)
        place = at * QBLK + lax.broadcasted_iota(jnp.int32, (1, QBLK), 1)
        for j in range(GROUP):
            mine = slice(j * QBLK, (j + 1) * QBLK)
            out_ref[j * DH : (j + 1) * DH, cols] = jnp.where(
                place < length_ref[0], weighted[:, mine], 0.0
            ).astype(jnp.bfloat16)
            lse_ref[0, j : j + 1, cols] = log_sum[:, mine]


def attend_back_kernel(
    query_ref,
    key_ref,
    value_ref,
    out_ref,
    out_grad_ref,
    lse_ref,
    cos_ref,
    sin_ref,
    query_grad_ref,
    key_grad_ref,
    value_grad_ref,
    key_rows,
    value_rows,
    key_sum,
    value_sum,
):
    key_rows[...] = key_ref[...].T
    value_rows[...] = value_ref[...].T
    blocks = query_ref.shape[1] // QBLK
    mask = causal_mask()
    for at in reversed(range(blocks)):
        cols = slice(at * QBLK, (at + 1) * QBLK)
        queries, out_grad = heads_of(query_ref, cols), heads_of(out_grad_ref, cols)
        grad_dot = jnp.sum(
            out_grad.astype(jnp.float32) * heads_of(out_ref, cols).astype(jnp.float32),
            axis=0,
            keepdims=True,
        )
        log_sum = jnp.concatenate([lse_ref[0, j : j + 1, cols] for j in range(GROUP)], axis=1)
        query_grad = 0.0
        for k in range(at + 1):
            own = slice(k * QBLK, (k + 1) * QBLK)
            weights_now = jnp.exp(mul_nn(key_rows[own], queries) - log_sum)
            if k == at:
                weights_now = jnp.where(mask, weights_now, 0.0)
            weights_grad = mul_nn(value_rows[own], out_grad)
            score_grad = (weights_now * (weights_grad - grad_dot)).astype(jnp.bfloat16)
            value_part = mul_nt(out_grad, weights_now.astype(jnp.bfloat16))
            key_part = mul_nt(queries, score_grad)
            if at == blocks - 1:
                value_sum[:, own] = value_part
                key_sum[:, own] = key_part
            else:
                value_sum[:, own] += value_part
                key_sum[:, own] += key_part
            query_grad = query_grad + mul_nn(key_ref[:, own], score_grad)
        cosine, sine_part = cos_ref[:, cols] * DH**-0.5, sin_ref[:, cols] * -(DH**-0.5)
        for j in range(GROUP):
            query_grad_ref[j * DH : (j + 1) * DH, cols] = turn(
                query_grad[:, j * QBLK : (j + 1) * QBLK], cosine, sine_part
            ).astype(jnp.bfloat16)
    key_grad_ref[...] = turn(key_sum[...], cos_ref[...], -sin_ref[...]).astype(jnp.bfloat16)
    value_grad_ref[...] = value_sum[...].astype(jnp.bfloat16)


def attend_specs(seq_len):
    query_spec = pl.BlockSpec((GROUP * DH, seq_len), lambda h: (h, 0))
    key_spec = pl.BlockSpec((DH, seq_len), lambda h: (h, 0))
    lse_spec = pl.BlockSpec((1, 8, seq_len), lambda h: (h, 0, 0))
    angle_spec = pl.BlockSpec((DH // 2, seq_len), lambda h: (0, 0))
    return query_spec, key_spec, lse_spec, angle_spec


def attend(length, attn_in, weights, cosine, sine_part):
    seq_len, width = attn_in.shape
    query_spec, key_spec, lse_spec, angle_spec = attend_specs(seq_len)
    head_rows = (GROUP + 2) * DH
    return pl.pallas_call(
        attend_kernel,
        grid=(HK,),
        in_specs=[
            pl.BlockSpec(memory_space=pltpu.SMEM),
            pl.BlockSpec((seq_len, width), lambda h: (0, 0)),
            pl.BlockSpec((1, head_rows, width), lambda h: (h, 0, 0)),
            angle_spec,
            angle_spec,
        ],
        out_specs=[query_spec, key_spec, key_spec, query_spec, lse_spec],
        out_shape=[
            jax.ShapeDtypeStruct((HQ * DH, seq_len), jnp.bfloat16),
            jax.ShapeDtypeStruct((HK * DH, seq_len), jnp.bfloat16),
            jax.ShapeDtypeStruct((HK * DH, seq_len), jnp.bfloat16),
            jax.ShapeDtypeStruct((HQ * DH, seq_len), jnp.bfloat16),
            jax.ShapeDtypeStruct((HK, 8, seq_len), jnp.float32),
        ],
        scratch_shapes=[pltpu.VMEM((seq_len, DH), jnp.bfloat16)],
        compiler_params=pltpu.CompilerParams(vmem_limit_bytes=40 * 2**20),
        cost_estimate=pl.CostEstimate(
            flops=20 * 10**9, bytes_accessed=8 * 2**20, transcendentals=6 * 10**6
        ),
        name="attend",
    )(length, attn_in, weights, cosine, sine_part)


def attend_back(queries, keys, values, attended, attended_grad, log_sum, cosine, sine_part):
    seq_len = queries.shape[1]
    query_spec, key_spec, lse_spec, angle_spec = attend_specs(seq_len)
    return pl.pallas_call(
        attend_back_kernel,
        grid=(HK,),
        in_specs=[
            query_spec,
            key_spec,
            key_spec,
            query_spec,
            query_spec,
            lse_spec,
            angle_spec,
            angle_spec,
        ],
        out_specs=[query_spec, key_spec, key_spec],
        out_shape=[
            jax.ShapeDtypeStruct((HQ * DH, seq_len), jnp.bfloat16),
            jax.ShapeDtypeStruct((HK * DH, seq_len), jnp.bfloat16),
            jax.ShapeDtypeStruct((HK * DH, seq_len), jnp.bfloat16),
        ],
        scratch_shapes=[pltpu.VMEM((seq_len, DH), jnp.bfloat16)] * 2
        + [pltpu.VMEM((DH, seq_len), jnp.float32)] * 2,
        compiler_params=pltpu.CompilerParams(vmem_limit_bytes=40 * 2**20),
        cost_estimate=pl.CostEstimate(
            flops=25 * 10**9, bytes_accessed=8 * 2**20, transcendentals=6 * 10**6
        ),
        name="attend_back",
    )(queries, keys, values, attended, attended_grad, log_sum, cosine, sine_part)


def swap(values, axis, bits, count):
    return lax.ppermute(values, axis, [(k, k ^ bits) for k in range(count)])


def pick(values, index, size, axis):
    return lax.dynamic_slice_in_dim(values, index * size, size, axis)


def two(bit, mine, other, axis):
    return jnp.concatenate(
        [jnp.where(bit == 0, mine, other), jnp.where(bit == 0, other, mine)], axis=axis
    )


def sum_over_devices(partial_sum):
    rows, cols = partial_sum.shape
    dp_at, seq_at = lax.axis_index("dp"), lax.axis_index("seq")
    core, plane, near, far = dp_at % 2, dp_at // 2, seq_at % 2, seq_at // 2
    low = lambda v: v.astype(jnp.bfloat16)
    wide = lambda v: v.astype(jnp.float32)
    other = swap(low(pick(partial_sum, 1 - core, rows // 2, 0)), "dp", 1, 8)
    half = pick(partial_sum, core, rows // 2, 0) + wide(other)
    size = rows // 8
    total = pick(half, plane, size, 0)
    for step in (1, 2, 3):
        total = total + wide(swap(low(pick(half, plane ^ step, size, 0)), "dp", 2 * step, 8))
    size = cols // 2
    other = swap(low(pick(total, 1 - near, size, 1)), "seq", 1, 4)
    total = pick(total, near, size, 1) + wide(other)
    size = cols // 4
    other = swap(low(pick(total, 1 - far, size, 1)), "seq", 2, 4)
    total = low(pick(total, far, size, 1) + wide(other))
    total = two(far, total, swap(total, "seq", 2, 4), 1)
    total = two(near, total, swap(total, "seq", 1, 4), 1)
    parts = [total] + [swap(total, "dp", 2 * step, 8) for step in (1, 2, 3)]
    half = []
    for at in range(4):
        piece = parts[3]
        for step in (2, 1, 0):
            piece = jnp.where(plane == at ^ step, parts[step], piece)
        half.append(piece)
    half = jnp.concatenate(half, axis=0)
    return two(core, half, swap(half, "dp", 1, 8), 0).astype(jnp.float32)


def rows_in(values):
    count, block_len, width = values.shape
    seq_at = lax.axis_index("seq")
    whole = jnp.zeros((count * block_len, width), values.dtype)
    for step in range(count):
        chunk = lax.dynamic_index_in_dim(values, (seq_at + step) % count, 0, keepdims=False)
        if step:
            chunk = lax.ppermute(chunk, "seq", [(k, (k + step) % count) for k in range(count)])
        place = (seq_at - step) % count * block_len
        whole = lax.dynamic_update_slice_in_dim(whole, chunk, place, 0)
    return whole


def rows_out(whole, count):
    block_len = whole.shape[0] // count
    seq_at = lax.axis_index("seq")
    values = jnp.zeros((count, block_len, whole.shape[1]), whole.dtype)
    for step in range(count):
        chunk = pick(whole, (seq_at + step) % count, block_len, 0)
        if step:
            chunk = lax.ppermute(chunk, "seq", [(k, (k + step) % count) for k in range(count)])
        values = lax.dynamic_update_slice_in_dim(values, chunk[None], (seq_at - step) % count, 0)
    return values


def local_rows(
    tokens,
    lengths,
    w_query,
    w_key,
    w_value,
    w_out,
    w_gate,
    w_up,
    w_down,
    gain_attn,
    gain_ffn,
    cotangent,
):
    row_count, block_len, model_width = tokens.shape
    seq_len = row_count * block_len
    q_width, kv_width = HQ * DH, HK * DH
    seq_at = lax.axis_index("seq")
    length = lax.dynamic_slice_in_dim(lengths, seq_at, 1)
    positions = jnp.arange(seq_len, dtype=jnp.int32)
    live = positions < length
    half_dim = DH // 2
    frequency = rope_base ** (-jnp.arange(half_dim, dtype=jnp.float32) / half_dim)
    angles = frequency[:, None] * positions.astype(jnp.float32)[None, :]
    cosine, sine_part = jnp.cos(angles), jnp.sin(angles)
    w_heads = jnp.concatenate(
        [
            w_query.T.reshape(HK, GROUP * DH, model_width),
            w_key.T.reshape(HK, DH, model_width),
            w_value.T.reshape(HK, DH, model_width),
        ],
        axis=1,
    )
    w_qkv = jnp.concatenate([w_query, w_key, w_value], axis=1)

    inputs = rows_in(tokens).astype(jnp.float32)
    out_low = rows_in(cotangent)
    attn_norm, attn_pull = jax.vjp(norm_rows, inputs, gain_attn)
    attn_in = attn_norm.astype(jnp.bfloat16)
    queries, keys, values, attended, log_sum = attend(length, attn_in, w_heads, cosine, sine_part)
    residual = inputs + inner_rows(attended, w_out)
    ffn_norm, ffn_pull = jax.vjp(norm_rows, residual, gain_ffn)
    ffn_in = ffn_norm.astype(jnp.bfloat16)
    gate_proj = jnp.dot(ffn_in, w_gate, preferred_element_type=jnp.float32)
    up_proj = jnp.dot(ffn_in, w_up, preferred_element_type=jnp.float32)
    product, swiglu_pull = jax.vjp(
        lambda gate_in, up_in: jax.nn.silu(gate_in) * up_in, gate_proj, up_proj
    )
    hidden = product.astype(jnp.bfloat16)
    branch = jnp.dot(hidden, w_down, preferred_element_type=jnp.float32)
    mixed = rows_out((residual + branch).astype(jnp.bfloat16), row_count)
    out_grad = out_low.astype(jnp.float32)
    w_down_sum = sum_over_devices(inner_rows(out_low, hidden))
    hidden_grad = times_t(out_low, w_down)
    gate_grad, up_grad = swiglu_pull(hidden_grad)
    gate_low = gate_grad.astype(jnp.bfloat16)
    up_low = up_grad.astype(jnp.bfloat16)
    w_gate_sum = sum_over_devices(inner_rows(ffn_in, gate_low))
    w_up_sum = sum_over_devices(inner_rows(ffn_in, up_low))
    ffn_in_grad = times_t(gate_low, w_gate) + times_t(up_low, w_up)
    residual_part, gain_ffn_grad = ffn_pull(ffn_in_grad)
    residual_grad = out_grad + residual_part
    residual_low = residual_grad.astype(jnp.bfloat16)
    w_out_grad = jnp.dot(attended, residual_low, preferred_element_type=jnp.float32)
    attended_grad = jnp.where(live[None, :], times_t(w_out, residual_low), 0.0).astype(
        jnp.bfloat16
    )
    query_low, key_low, value_low = attend_back(
        queries, keys, values, attended, attended_grad, log_sum, cosine, sine_part
    )
    qkv_low = jnp.concatenate([query_low, key_low, value_low], axis=0)
    attn_in_grad = lax.dot_general(
        qkv_low, w_qkv, (((0,), (1,)), ((), ())), preferred_element_type=jnp.float32
    )
    inputs_part, gain_attn_grad = attn_pull(attn_in_grad)
    tokens_grad = rows_out((residual_grad + inputs_part).astype(jnp.bfloat16), row_count)
    w_qkv_grad = lax.dot_general(
        attn_in, qkv_low, (((0,), (1,)), ((), ())), preferred_element_type=jnp.float32
    )
    attn_sum = sum_over_devices(jnp.concatenate([w_qkv_grad, w_out_grad], axis=1))
    gains = jnp.stack([gain_attn_grad, gain_ffn_grad])
    gains_sum = gains
    for bits in (1, 2, 4):
        gains_sum = gains_sum + swap(gains_sum, "dp", bits, 8)
    for bits in (1, 2):
        gains_sum = gains_sum + swap(gains_sum, "seq", bits, 4)
    return (
        mixed,
        tokens_grad,
        attn_sum[:, :q_width],
        attn_sum[:, q_width : q_width + kv_width],
        attn_sum[:, q_width + kv_width : q_width + 2 * kv_width],
        attn_sum[:, q_width + 2 * kv_width :],
        w_gate_sum,
        w_up_sum,
        w_down_sum.T,
        gains_sum[0],
        gains_sum[1],
    )


def solution(mesh):
    whole_rows = mesh.shape["dp"] == 8 and mesh.shape["seq"] == 4
    return jax.shard_map(
        local_rows if whole_rows else local_general,
        mesh=mesh,
        in_specs=(
            P("dp", "seq", None),
            P("dp"),
            P(),
            P(),
            P(),
            P(),
            P(),
            P(),
            P(),
            P(),
            P(),
            P("dp", "seq", None),
        ),
        out_specs=(
            P("dp", "seq", None),
            P("dp", "seq", None),
            P(),
            P(),
            P(),
            P(),
            P(),
            P(),
            P(),
            P(),
            P(),
        ),
        check_vma=False,
    )
```

```python
from functools import partial
import math

import jax
import jax.numpy as jnp
from jax import lax
from jax.experimental import pallas as pl
from jax.experimental.pallas import tpu as pltpu
from jax.sharding import PartitionSpec as P

HQ = 9
HK = 3
DH = 64


eps_norm = 1e-05
rope_base = 100000.0
neg_large = -1e30


def norm_rows(values, gain_vec):
    return (
        values * lax.rsqrt(jnp.mean(values * values, axis=-1, keepdims=True) + eps_norm) * gain_vec
    )


def rotate(values, positions, turn_sign):
    half_dim = values.shape[-1] // 2
    frequency = rope_base ** (-jnp.arange(half_dim, dtype=jnp.float32) / half_dim)
    angles = turn_sign * positions.astype(jnp.float32)[:, None] * frequency[None, :]
    cosine = jnp.cos(angles)[:, None, :]
    sine_part = jnp.sin(angles)[:, None, :]
    first_half = values[..., :half_dim]
    second_half = values[..., half_dim:]
    return jnp.concatenate(
        [
            first_half * cosine - second_half * sine_part,
            second_half * cosine + first_half * sine_part,
        ],
        axis=-1,
    )


def inner_rows(left, right):
    return lax.dot_general(
        left, right, (((0,), (0,)), ((), ())), preferred_element_type=jnp.float32
    )


def times_t(left, right):
    return lax.dot_general(
        left, right, (((1,), (1,)), ((), ())), preferred_element_type=jnp.float32
    )


def fold_piece(block_len, step_fn, carry, pieces):
    piece_count = pieces.shape[1] // block_len

    def inner_step(index_step, state):
        part_piece = lax.dynamic_slice_in_dim(pieces, index_step * block_len, block_len, 1)
        return step_fn(state, part_piece, index_step * block_len)

    return lax.fori_loop(0, piece_count, inner_step, carry)


def local_general(
    tokens,
    lengths,
    w_query,
    w_key,
    w_value,
    w_out,
    w_gate,
    w_up,
    w_down,
    gain_attn,
    gain_ffn,
    cotangent,
):
    row_count, block_len, model_width = tokens.shape
    group_size = HQ // HK
    kv_width = HK * DH
    score_scale = 1.0 / math.sqrt(DH)
    seq_devices = lax.axis_size("seq")
    my_start = lax.axis_index("seq") * block_len
    positions = my_start + jnp.arange(block_len, dtype=jnp.int32)
    longest = jnp.max(lengths)
    live_rows = positions[None, :] < lengths[:, None]
    query_active = my_start < longest
    inputs = tokens.reshape(-1, model_width).astype(jnp.float32)
    attn_norm, attn_pull = jax.vjp(norm_rows, inputs, gain_attn)
    attn_in = attn_norm.astype(jnp.bfloat16)
    query_pre = jnp.dot(attn_in, w_query, preferred_element_type=jnp.float32)
    query_heads = rotate(query_pre.reshape(row_count, block_len, HQ, DH), positions, 1.0).astype(
        jnp.bfloat16
    )
    query_heads = query_heads.reshape(row_count, block_len, HK, group_size, DH)
    key_pre = jnp.dot(attn_in, w_key, preferred_element_type=jnp.float32)
    key_heads = rotate(key_pre.reshape(row_count, block_len, HK, DH), positions, 1.0).astype(
        jnp.bfloat16
    )
    value_heads = jnp.dot(attn_in, w_value, preferred_element_type=jnp.float32).astype(jnp.bfloat16)
    key_value = jnp.concatenate(
        [
            key_heads.reshape(row_count, block_len, kv_width),
            value_heads.reshape(row_count, block_len, kv_width),
        ],
        axis=-1,
    )

    def allowed_for(piece_start):
        key_pos = piece_start + jnp.arange(block_len, dtype=jnp.int32)
        causal = key_pos[None, None, :] <= positions[None, :, None]
        inside = key_pos[None, None, :] < lengths[:, None, None]
        return causal & inside

    def needed_for(piece_start):
        return (piece_start <= my_start) & (piece_start < longest) & query_active

    def split_piece(pieces):
        key_part = pieces[..., :kv_width].reshape(row_count, block_len, HK, DH)
        value_part = pieces[..., kv_width:].reshape(row_count, block_len, HK, DH)
        return (key_part, value_part)

    def forward_block(carry, pieces, piece_start):

        def forward_compute_block(state):
            row_max, row_total, weighted = state
            key_part, value_part = split_piece(pieces)
            scores = (
                jnp.einsum(
                    "rqhgd,rkhd->rhgqk", query_heads, key_part, preferred_element_type=jnp.float32
                )
                * score_scale
            )
            allowed = allowed_for(piece_start)[:, None, None]
            scores = jnp.where(allowed, scores, neg_large)
            new_max = jnp.maximum(row_max, jnp.max(scores, axis=-1))
            shrink = jnp.exp(row_max - new_max)
            exp_scores = jnp.where(allowed, jnp.exp(scores - new_max[..., None]), 0.0)
            row_total = row_total * shrink + jnp.sum(exp_scores, axis=-1)
            update = jnp.einsum(
                "rhgqk,rkhd->rqhgd",
                exp_scores.astype(jnp.bfloat16),
                value_part,
                preferred_element_type=jnp.float32,
            )
            weighted = weighted * jnp.moveaxis(shrink, 3, 1)[..., None] + update
            return (new_max, row_total, weighted)

        return lax.cond(needed_for(piece_start), forward_compute_block, lambda state: state, carry)

    stat_shape = (row_count, HK, group_size, block_len)
    forward_init = (
        jnp.full(stat_shape, neg_large, jnp.float32),
        jnp.zeros(stat_shape, jnp.float32),
        jnp.zeros((row_count, block_len, HK, group_size, DH), jnp.float32),
    )
    forward_state = fold_piece(
        block_len, forward_block, forward_init, lax.all_gather(key_value, "seq", axis=1, tiled=True)
    )
    row_max, row_total, weighted = forward_state
    safe_total = jnp.where(row_total > 0, row_total, 1.0)
    attn_heads = weighted / jnp.moveaxis(safe_total, 3, 1)[..., None]
    attn_heads = jnp.where(live_rows[:, :, None, None, None], attn_heads, 0.0)
    log_sum = jnp.where(live_rows[:, None, None, :], row_max + jnp.log(safe_total), 0.0)
    attn_low = attn_heads.reshape(-1, HQ * DH).astype(jnp.bfloat16)
    residual = inputs + jnp.dot(attn_low, w_out, preferred_element_type=jnp.float32)
    ffn_norm, ffn_pull = jax.vjp(norm_rows, residual, gain_ffn)
    ffn_in = ffn_norm.astype(jnp.bfloat16)
    gate_proj = jnp.dot(ffn_in, w_gate, preferred_element_type=jnp.float32)
    up_proj = jnp.dot(ffn_in, w_up, preferred_element_type=jnp.float32)
    product, swiglu_pull = jax.vjp(
        lambda gate_in, up_in: jax.nn.silu(gate_in) * up_in, gate_proj, up_proj
    )
    hidden = product.astype(jnp.bfloat16)
    branch = jnp.dot(hidden, w_down, preferred_element_type=jnp.float32)
    mixed = (residual + branch).astype(jnp.bfloat16).reshape(row_count, block_len, model_width)
    out_low = cotangent.reshape(-1, model_width)
    out_grad = out_low.astype(jnp.float32)
    w_down_grad = inner_rows(hidden, out_low)
    hidden_grad = times_t(out_low, w_down)
    gate_grad, up_grad = swiglu_pull(hidden_grad)
    gate_low = gate_grad.astype(jnp.bfloat16)
    up_low = up_grad.astype(jnp.bfloat16)
    w_gate_grad = inner_rows(ffn_in, gate_low)
    w_up_grad = inner_rows(ffn_in, up_low)
    ffn_in_grad = times_t(gate_low, w_gate) + times_t(up_low, w_up)
    residual_part, gain_ffn_grad = ffn_pull(ffn_in_grad)
    residual_grad = out_grad + residual_part
    residual_low = residual_grad.astype(jnp.bfloat16)
    w_out_grad = inner_rows(attn_low, residual_low)
    attended_grad = times_t(residual_low, w_out).reshape(row_count, block_len, HK, group_size, DH)
    attended_grad = jnp.where(live_rows[:, :, None, None, None], attended_grad, 0.0).astype(
        jnp.bfloat16
    )
    grad_dot = jnp.moveaxis(jnp.sum(attended_grad.astype(jnp.float32) * attn_heads, axis=-1), 1, 3)

    def backward_block(with_kv, carry, pieces, piece_start):

        def backward_compute_block(state):
            key_part, value_part = split_piece(pieces)
            scores = (
                jnp.einsum(
                    "rqhgd,rkhd->rhgqk", query_heads, key_part, preferred_element_type=jnp.float32
                )
                * score_scale
            )
            allowed = allowed_for(piece_start)[:, None, None]
            weights_now = jnp.where(allowed, jnp.exp(scores - log_sum[..., None]), 0.0)
            weights_grad = jnp.einsum(
                "rqhgd,rkhd->rhgqk", attended_grad, value_part, preferred_element_type=jnp.float32
            )
            score_grad = (weights_now * (weights_grad - grad_dot[..., None])).astype(jnp.bfloat16)
            query_grad = (
                state[0]
                + jnp.einsum(
                    "rhgqk,rkhd->rqhgd", score_grad, key_part, preferred_element_type=jnp.float32
                )
                * score_scale
            )
            kv_grad = state[1]
            values_grad = jnp.einsum(
                "rhgqk,rqhgd->rkhd",
                weights_now.astype(jnp.bfloat16),
                attended_grad,
                preferred_element_type=jnp.float32,
            )
            keys_grad = (
                jnp.einsum(
                    "rhgqk,rqhgd->rkhd", score_grad, query_heads, preferred_element_type=jnp.float32
                )
                * score_scale
            )
            local_kv = jnp.concatenate(
                [
                    keys_grad.reshape(row_count, block_len, kv_width),
                    values_grad.reshape(row_count, block_len, kv_width),
                ],
                axis=-1,
            )
            current = lax.dynamic_slice_in_dim(kv_grad, piece_start, block_len, 1)
            kv_grad = lax.dynamic_update_slice_in_dim(kv_grad, current + local_kv, piece_start, 1)
            return (query_grad, kv_grad)

        return lax.cond(needed_for(piece_start), backward_compute_block, lambda state: state, carry)

    query_zero = jnp.zeros((row_count, block_len, HK, group_size, DH), jnp.float32)
    backward_init = (
        query_zero,
        jnp.zeros((row_count, block_len * seq_devices, 2 * kv_width), jnp.float32),
    )
    step_back = partial(backward_block, True)
    backward_state = fold_piece(
        block_len, step_back, backward_init, lax.all_gather(key_value, "seq", axis=1, tiled=True)
    )
    query_grad = backward_state[0]
    own_kv_grad = lax.psum_scatter(
        backward_state[1].astype(jnp.bfloat16), "seq", scatter_dimension=1, tiled=True
    ).astype(jnp.float32)
    query_low = (
        rotate(query_grad.reshape(row_count, block_len, HQ, DH), positions, -1.0)
        .astype(jnp.bfloat16)
        .reshape(-1, HQ * DH)
    )
    key_low = (
        rotate(own_kv_grad[..., :kv_width].reshape(row_count, block_len, HK, DH), positions, -1.0)
        .astype(jnp.bfloat16)
        .reshape(-1, kv_width)
    )
    value_low = own_kv_grad[..., kv_width:].astype(jnp.bfloat16).reshape(-1, kv_width)
    w_query_grad = inner_rows(attn_in, query_low)
    w_key_grad = inner_rows(attn_in, key_low)
    w_value_grad = inner_rows(attn_in, value_low)
    attn_in_grad = (
        times_t(query_low, w_query) + times_t(key_low, w_key) + times_t(value_low, w_value)
    )
    inputs_part, gain_attn_grad = attn_pull(attn_in_grad)
    tokens_grad = (
        (residual_grad + inputs_part)
        .astype(jnp.bfloat16)
        .reshape(row_count, block_len, model_width)
    )
    (
        w_query_grad,
        w_key_grad,
        w_value_grad,
        w_out_grad,
        w_gate_grad,
        w_up_grad,
        w_down_grad,
        gain_attn_grad,
        gain_ffn_grad,
    ) = lax.psum(
        (
            w_query_grad,
            w_key_grad,
            w_value_grad,
            w_out_grad,
            w_gate_grad,
            w_up_grad,
            w_down_grad,
            gain_attn_grad,
            gain_ffn_grad,
        ),
        ("dp", "seq"),
    )
    return (
        mixed,
        tokens_grad,
        w_query_grad,
        w_key_grad,
        w_value_grad,
        w_out_grad,
        w_gate_grad,
        w_up_grad,
        w_down_grad,
        gain_attn_grad,
        gain_ffn_grad,
    )


GROUP = HQ // HK
HEAD_ROWS = (GROUP + 2) * DH
SCALE = DH**-0.5
FULL = pl.BlockSpec(memory_space=pltpu.VMEM)
SMEM = pl.BlockSpec(memory_space=pltpu.SMEM)
ANY = pl.BlockSpec(memory_space=pl.ANY)


def shape_of(shape, dtype=jnp.bfloat16):
    return jax.ShapeDtypeStruct(shape, dtype)


def low(values):
    return values.astype(jnp.bfloat16)


def wide(values):
    return values.astype(jnp.float32)


def mul_nt(left, right):
    return lax.dot_general(
        left, right, (((1,), (1,)), ((), ())), preferred_element_type=jnp.float32
    )


def mul_nn(left, right):
    return lax.dot_general(
        left, right, (((1,), (0,)), ((), ())), preferred_element_type=jnp.float32
    )


class Order:
    last = None


def run(
    kernel, name, info, operands, out_shapes, scratch=(), vmem=12, grid=(), in_specs=None, out_specs=None
):
    after = [] if Order.last is None else [Order.last]
    taken = len(operands)

    def body(*refs):
        kernel(*refs[: 1 + taken], *refs[1 + taken + len(after) :])

    many = isinstance(out_shapes, list)
    outs = pl.pallas_call(
        body,
        grid=grid,
        in_specs=[SMEM] + (in_specs or [FULL] * taken) + [ANY] * len(after),
        out_specs=out_specs or ([FULL] * len(out_shapes) if many else FULL),
        scratch_shapes=list(scratch),
        out_shape=out_shapes,
        compiler_params=pltpu.CompilerParams(vmem_limit_bytes=vmem * 2**20),
        cost_estimate=pl.CostEstimate(flops=1000, bytes_accessed=1000, transcendentals=0),
        name=name,
    )(info, *operands, *after)
    Order.last = min(outs, key=lambda v: v.size) if many else outs
    return outs


def whole(*shape):
    return pl.BlockSpec(shape, lambda b: (0,) * len(shape))


def at_block(*shape):
    return pl.BlockSpec((1, *shape), lambda b: (b, *[0] * len(shape)))


def turn(values, cosine, sine_part):
    first_half, second_half = values[: DH // 2], values[DH // 2 :]
    return jnp.concatenate(
        [
            first_half * cosine - second_half * sine_part,
            second_half * cosine + first_half * sine_part,
        ],
        axis=0,
    )


def inverse_rms(values):
    mean = jnp.sum(values * values, axis=0, keepdims=True) * (1.0 / values.shape[0])
    return lax.rsqrt(mean + eps_norm)


def norm_back(values, grad, gain):
    scale = inverse_rms(values)
    turned = grad * gain
    inner = jnp.sum(turned * values, axis=0, keepdims=True) * (1.0 / values.shape[0])
    part = scale * turned - values * (scale * scale * scale * inner)
    return part, grad * values * scale


def gain_of(ref):
    return jnp.concatenate([ref[...], ref[...]], axis=1)


def causal_mask(width):
    key_at = lax.broadcasted_iota(jnp.int32, (width, width), 0)
    query_at = lax.broadcasted_iota(jnp.int32, (width, width), 1)
    return jnp.concatenate([key_at <= query_at] * GROUP, axis=1)


def heads_of(values):
    return jnp.concatenate([values[j * DH : (j + 1) * DH] for j in range(GROUP)], axis=1)


def attend_kernel(
    info,
    row_ref,
    gain_ref,
    weights_ref,
    cos_ref,
    sin_ref,
    attn_in_ref,
    query_ref,
    key_ref,
    value_ref,
    out_ref,
    lse_ref,
    key_rows,
):
    blocks, _, width = row_ref.shape
    gain = gain_of(gain_ref)
    for b in range(blocks):
        values = wide(row_ref[b])
        attn_in_ref[b] = low(values * inverse_rms(values) * gain)
    mask = causal_mask(width)

    def one_head(h, carry):
        for b in range(blocks):
            pre = mul_nn(weights_ref[h], attn_in_ref[b])
            cosine, sine_part = cos_ref[b], sin_ref[b]
            for j in range(GROUP):
                query_ref[h, b, j * DH : (j + 1) * DH] = low(
                    turn(pre[j * DH : (j + 1) * DH], cosine, sine_part) * SCALE
                )
            keys = low(turn(pre[GROUP * DH : (GROUP + 1) * DH], cosine, sine_part))
            key_ref[h, b] = keys
            key_rows[b] = keys.T
            value_ref[h, b] = low(pre[(GROUP + 1) * DH :])
        for b in range(blocks):
            queries = heads_of(query_ref[h, b])
            scores, top = [], None
            for k in range(b + 1):
                part = mul_nn(key_rows[k], queries)
                if k == b:
                    part = jnp.where(mask, part, neg_large)
                scores.append(part)
                part_top = jnp.max(part, axis=0, keepdims=True)
                top = part_top if top is None else jnp.maximum(top, part_top)
            total, weighted = 0.0, 0.0
            for k in range(b + 1):
                weights_now = jnp.exp(scores[k] - top)
                total = total + jnp.sum(weights_now, axis=0, keepdims=True)
                weighted = weighted + mul_nn(value_ref[h, k], low(weights_now))
            weighted = weighted * (1.0 / total)
            log_sum = top + jnp.log(total)
            live = b * width + lax.broadcasted_iota(jnp.int32, (1, width), 1) < info[3]
            for j in range(GROUP):
                mine = slice(j * width, (j + 1) * width)
                out_ref[h, b, j * DH : (j + 1) * DH] = low(jnp.where(live, weighted[:, mine], 0.0))
                lse_ref[h, b, j : j + 1] = log_sum[:, mine]
        return carry

    lax.fori_loop(0, HK, one_head, 0)


def attend(info, row, gain, w_heads, cosine, sine_part):
    blocks, features, width = row.shape
    return run(
        attend_kernel,
        "attend",
        info,
        [row, gain, w_heads, cosine, sine_part],
        [
            shape_of((blocks, features, width)),
            shape_of((HK, blocks, GROUP * DH, width)),
            shape_of((HK, blocks, DH, width)),
            shape_of((HK, blocks, DH, width)),
            shape_of((HK, blocks, GROUP * DH, width)),
            shape_of((HK, blocks, 8, width), jnp.float32),
        ],
        [pltpu.VMEM((blocks, width, DH), jnp.bfloat16)],
        16,
    )


def attend_back_kernel(
    h,
    info,
    query_ref,
    key_ref,
    value_ref,
    out_ref,
    out_grad_ref,
    lse_ref,
    cos_ref,
    sin_ref,
    grad_ref,
    key_rows,
    value_rows,
    key_sum,
    value_sum,
):
    blocks, width = query_ref.shape[1], query_ref.shape[3]
    head = slice(h * GROUP * DH, (h + 1) * GROUP * DH)
    for b in range(blocks):
        key_rows[b] = key_ref[h, b].T
        value_rows[b] = value_ref[h, b].T
    mask = causal_mask(width)
    for b in reversed(range(blocks)):
        queries, out_grad = heads_of(query_ref[h, b]), heads_of(out_grad_ref[b, head])
        grad_dot = jnp.sum(wide(out_grad) * wide(heads_of(out_ref[h, b])), axis=0, keepdims=True)
        log_sum = jnp.concatenate([lse_ref[h, b, j : j + 1] for j in range(GROUP)], axis=1)
        query_grad = 0.0
        for k in range(b + 1):
            weights_now = jnp.exp(mul_nn(key_rows[k], queries) - log_sum)
            if k == b:
                weights_now = jnp.where(mask, weights_now, 0.0)
            weights_grad = mul_nn(value_rows[k], out_grad)
            score_grad = low(weights_now * (weights_grad - grad_dot))
            value_part = mul_nt(out_grad, low(weights_now))
            key_part = mul_nt(queries, score_grad)
            if b == blocks - 1:
                value_sum[k] = value_part
                key_sum[k] = key_part
            else:
                value_sum[k] += value_part
                key_sum[k] += key_part
            query_grad = query_grad + mul_nn(key_ref[h, k], score_grad)
        cosine, sine_part = cos_ref[b], -sin_ref[b]
        for j in range(GROUP):
            grad_ref[b, j * DH : (j + 1) * DH] = low(
                turn(query_grad[:, j * width : (j + 1) * width], cosine * SCALE, sine_part * SCALE)
            )
        grad_ref[b, GROUP * DH : (GROUP + 1) * DH] = low(turn(key_sum[b], cosine, sine_part))
        grad_ref[b, (GROUP + 1) * DH :] = low(value_sum[b])


def attend_back(info, h, queries, keys, values, attended, attended_grad, log_sum, angles):
    _, blocks, _, width = queries.shape
    return run(
        partial(attend_back_kernel, h),
        "attend_back",
        info,
        [queries, keys, values, attended, attended_grad, log_sum, *angles],
        shape_of((blocks, HEAD_ROWS, width)),
        [pltpu.VMEM((blocks, width, DH), jnp.bfloat16)] * 2
        + [pltpu.VMEM((blocks, DH, width), jnp.float32)] * 2,
    )


def lanes_of(ref, rows=slice(None)):
    return jnp.concatenate([ref[b, rows] for b in range(ref.shape[0])], axis=1)


def put_grad(values, ref, at):
    planes, parts, _, rows, cols = ref.shape
    for p in range(planes):
        for z in range(parts):
            ref[p, z, at] = values[p * rows : (p + 1) * rows, z * cols : (z + 1) * cols].astype(
                ref.dtype
            )


CHUNK = 768


def ffn_kernel(
    info,
    row_ref,
    att_ref,
    cot_ref,
    gain_ref,
    w_out_t_ref,
    w_gate_t_ref,
    w_up_t_ref,
    w_down_t_ref,
    w_down_ref,
    w_gate_ref,
    w_up_ref,
    w_out_ref,
    mixed_ref,
    grad_ref,
    low_ref,
    att_grad_ref,
    gain_grad_ref,
    down_send_ref,
    down_keep_ref,
    pair_send_ref,
    pair_keep_ref,
    ffn_ins,
    cots,
    hiddens,
    gates,
    ups,
):
    b = pl.program_id(0)
    width = row_ref.shape[2]
    gain = gain_of(gain_ref)
    attended = jnp.concatenate([att_ref[h, 0] for h in range(HK)], axis=0)
    residual = wide(row_ref[0]) + mul_nn(w_out_t_ref[...], attended)
    ffn_in = low(residual * inverse_rms(residual) * gain)
    ffn_ins[b] = ffn_in
    cot = cot_ref[0]
    cots[b] = cot
    mixed, ffn_in_grad = residual, 0.0
    for at in range(0, hiddens.shape[1], CHUNK):
        part = slice(at, at + CHUNK)
        gate = mul_nn(w_gate_t_ref[part], ffn_in)
        up = mul_nn(w_up_t_ref[part], ffn_in)
        hidden_grad = mul_nn(w_down_ref[part], cot)
        sigmoid = 1.0 / (1.0 + jnp.exp(-gate))
        silu = gate * sigmoid
        hidden = low(silu * up)
        gate_grad = low(hidden_grad * up * (sigmoid + silu * (1.0 - sigmoid)))
        up_grad = low(hidden_grad * silu)
        hiddens[b, part] = hidden
        gates[b, part] = gate_grad
        ups[b, part] = up_grad
        mixed = mixed + mul_nn(w_down_t_ref[:, part], hidden)
        ffn_in_grad = ffn_in_grad + (
            mul_nn(w_gate_ref[:, part], gate_grad) + mul_nn(w_up_ref[:, part], up_grad)
        )
    mixed_ref[0] = low(mixed)
    part, gain_terms = norm_back(residual, ffn_in_grad, gain)
    gain_terms = gain_terms[:, : width // 2] + gain_terms[:, width // 2 :]

    @pl.when(b == 0)
    def _():
        gain_grad_ref[...] = gain_terms

    @pl.when(b > 0)
    def _():
        gain_grad_ref[...] += gain_terms

    grad = wide(cot) + part
    grad_ref[0] = grad
    grad_low = low(grad)
    low_ref[0] = grad_low
    live = b * width + lax.broadcasted_iota(jnp.int32, (1, width), 1) < info[3]
    att_grad_ref[0] = low(jnp.where(live, mul_nn(w_out_ref[...], grad_low), 0.0))

    @pl.when(b == pl.num_programs(0) - 1)
    def _():
        rows = grad_ref.shape[1] // 2
        for half, down_ref, pair_ref in (
            (1 - info[1], down_send_ref, pair_send_ref),
            (info[1], down_keep_ref, pair_keep_ref),
        ):
            own = pl.ds(pl.multiple_of(half * rows, 16), rows)
            left = lanes_of(ffn_ins, own)
            put_grad(mul_nt(left, lanes_of(gates)), pair_ref, 0)
            put_grad(mul_nt(left, lanes_of(ups)), pair_ref, 1)
            put_grad(mul_nt(lanes_of(cots, own), lanes_of(hiddens)), down_ref, 0)


def ffn(info, row, attended, cot, gain, turned, straight):
    blocks, features, width = row.shape
    hidden = turned[1].shape[0]
    block, long = (blocks, features, width), (blocks, hidden, width)
    pieces = lambda count: (4, 4, count, features // 8, hidden // 4)
    return run(
        ffn_kernel,
        "ffn",
        info,
        [row, attended, cot, gain, *turned, *straight],
        [
            shape_of(block),
            shape_of(block, jnp.float32),
            shape_of(block),
            shape_of(block),
            shape_of(gain.shape, jnp.float32),
            shape_of(pieces(1)),
            shape_of(pieces(1), jnp.float32),
            shape_of(pieces(2)),
            shape_of(pieces(2), jnp.float32),
        ],
        [pltpu.VMEM(block, jnp.bfloat16)] * 2 + [pltpu.VMEM(long, jnp.bfloat16)] * 3,
        52,
        (blocks,),
        [
            at_block(features, width),
            pl.BlockSpec((HK, 1, GROUP * DH, width), lambda b: (0, b, 0, 0)),
            at_block(features, width),
            whole(*gain.shape),
            *[FULL] * 8,
        ],
        [
            *[at_block(features, width)] * 4,
            whole(*gain.shape),
            *[whole(*pieces(1))] * 2,
            *[whole(*pieces(2))] * 2,
        ],
    )


PIECE_ROWS = 48
PIECE_COLS = 640


def tokens_back_kernel(
    info, g0_ref, g1_ref, g2_ref, row_ref, grad_ref, gain_ref, w_ref, out_ref, gain_sum
):
    width = row_ref.shape[2]
    gain = gain_of(gain_ref)
    gain_sum[...] = jnp.zeros_like(gain_sum)

    def one_block(b, carry):
        qkv = jnp.concatenate([g0_ref[b], g1_ref[b], g2_ref[b]], axis=0)
        part, gain_terms = norm_back(wide(row_ref[b]), mul_nn(w_ref[...], qkv), gain)
        gain_sum[...] += gain_terms[:, : width // 2] + gain_terms[:, width // 2 :]
        out_ref[b] = low(grad_ref[b] + part)
        return carry

    lax.fori_loop(0, row_ref.shape[0], one_block, 0)


def tokens_back(info, qkv_grads, row, grad, gain, w_heads_t):
    return run(
        tokens_back_kernel,
        "tokens_back",
        info,
        [*qkv_grads, row, grad, gain, w_heads_t],
        [shape_of(row.shape), shape_of(gain.shape, jnp.float32)],
    )


def attn_grad_kernel(
    info, g0_ref, g1_ref, g2_ref, attn_in_ref, att_ref, low_ref, gain1_ref, gain2_ref, *outs
):
    send_ref, keep_ref = outs
    features = attn_in_ref.shape[1]

    def put(values, ref, at, columns=None):
        if columns is None:
            columns = jnp.zeros((values.shape[0], PIECE_COLS - features), jnp.float32)
        for piece in range(values.shape[0] // PIECE_ROWS):
            rows = slice(piece * PIECE_ROWS, (piece + 1) * PIECE_ROWS)
            p, z = (at + piece) // 4, (at + piece) % 4
            ref[p, z, 0, :, :features] = values[rows].astype(ref.dtype)
            ref[p, z, 0, :, features:] = columns[rows].astype(ref.dtype)

    def take(start, size):
        rows = slice(start, start + size)
        return jnp.concatenate([lanes_of(g, rows) for g in (g0_ref, g1_ref, g2_ref)], axis=0)

    def first_half(ref):
        attn_in = lanes_of(attn_in_ref)
        lane = lax.broadcasted_iota(jnp.int32, (features, PIECE_COLS - features), 1)
        gains = jnp.where(
            lane == 0,
            jnp.sum(gain1_ref[...], axis=1, keepdims=True),
            jnp.where(lane == 1, jnp.sum(gain2_ref[...], axis=1, keepdims=True), 0.0),
        )
        put(mul_nt(attn_in, take(0, GROUP * DH)), ref, 0, gains)
        put(mul_nt(take(GROUP * DH, DH), attn_in), ref, features // PIECE_ROWS)

    def second_half(ref):
        put(mul_nt(take((GROUP + 1) * DH, DH), lanes_of(attn_in_ref)), ref, 0)
        attended = jnp.concatenate([lanes_of(att_ref.at[h]) for h in range(HK)], axis=0)
        put(mul_nt(attended, lanes_of(low_ref)), ref, HK * DH // PIECE_ROWS)

    @pl.when(info[1] == 0)
    def _():
        second_half(send_ref)
        first_half(keep_ref)

    @pl.when(info[1] == 1)
    def _():
        first_half(send_ref)
        second_half(keep_ref)


def attn_grad(info, qkv_grads, attn_in, attended, grad_low, gain1, gain2):
    pieces = (4, 4, 1, PIECE_ROWS, PIECE_COLS)
    return run(
        attn_grad_kernel,
        "attn_grad",
        info,
        [*qkv_grads, attn_in, attended, grad_low, gain1, gain2],
        [shape_of(pieces), shape_of(pieces, jnp.float32)],
    )


def bit_of(value, bit):
    return lax.rem(value // (1 << bit), 2)


def plane_at(first, own, other):
    return own + 2 * other if first == 0 else other + 2 * own


def split_plane_kernel(routes, info, keep_ref, in_ref, *outs):
    for k, first in enumerate(routes):
        mine = bit_of(info[2], first)
        send_ref, own_ref = outs[2 * k : 2 * k + 2]
        for t in range(2):
            for z in range(4):
                there, here = plane_at(first, 1 - mine, t), plane_at(first, mine, t)
                send_ref[t, z] = low(keep_ref[there, z, k] + wide(in_ref[there, z, k]))
                own_ref[t, z] = keep_ref[here, z, k] + wide(in_ref[here, z, k])


def split_line_kernel(routes, info, *refs):
    count = len(routes)
    ins, outs = refs[: 2 * count], refs[2 * count :]
    for k, first in enumerate(routes):
        mine = bit_of(info[2], 1 - first)
        keep_ref, in_ref = ins[2 * k : 2 * k + 2]
        send_ref, own_ref = outs[2 * k : 2 * k + 2]
        send_ref[...] = low(keep_ref[1 - mine] + wide(in_ref[1 - mine]))
        own_ref[...] = keep_ref[mine] + wide(in_ref[mine])


def split_near_kernel(routes, info, *refs):
    ins, (send_ref, own_ref) = refs[:-2], refs[-2:]
    near = bit_of(info[0], 0)
    for k in range(len(routes)):
        keep_ref, in_ref = ins[2 * k : 2 * k + 2]
        for t in range(2):
            there, here = 1 - near + 2 * t, near + 2 * t
            send_ref[t, k] = low(keep_ref[there] + wide(in_ref[there]))
            own_ref[t, k] = keep_ref[here] + wide(in_ref[here])


def split_far_kernel(routes, info, keep_ref, in_ref, send_ref, own_ref):
    far = bit_of(info[0], 1)
    send_ref[...] = low(keep_ref[1 - far] + wide(in_ref[1 - far]))
    own_ref[...] = keep_ref[far] + wide(in_ref[far])


def total_kernel(routes, info, keep_ref, in_ref, out_ref):
    out_ref[...] = low(keep_ref[...] + wide(in_ref[...]))


def join_far_kernel(routes, info, own_ref, in_ref, out_ref):
    far = bit_of(info[0], 1)
    out_ref[far] = own_ref[...]
    out_ref[1 - far] = in_ref[...]


def join_near_kernel(routes, info, own_ref, in_ref, *outs):
    near = bit_of(info[0], 0)
    for k in range(len(routes)):
        for t in range(2):
            outs[k][near + 2 * t] = own_ref[t, k]
            outs[k][1 - near + 2 * t] = in_ref[t, k]


def join_line_kernel(routes, info, *refs):
    count = len(routes)
    ins, outs = refs[: 2 * count], refs[2 * count :]
    for k, first in enumerate(routes):
        mine = bit_of(info[2], 1 - first)
        outs[k][mine] = ins[2 * k][...]
        outs[k][1 - mine] = ins[2 * k + 1][...]


def join_plane_kernel(routes, info, *refs):
    ins, out_ref = refs[:-1], refs[-1]
    for k, first in enumerate(routes):
        mine = bit_of(info[2], first)
        own_ref, in_ref = ins[2 * k : 2 * k + 2]
        for t in range(2):
            for z in range(4):
                out_ref[plane_at(first, mine, t), z, k] = own_ref[t, z]
                out_ref[plane_at(first, 1 - mine, t), z, k] = in_ref[t, z]


def swap(values, axis, bits):
    count = 8 if axis == "dp" else 4
    return lax.ppermute(values, axis, [(k, k ^ bits) for k in range(count)])


class Sum:
    def __init__(self, info, send_keep, routes):
        self.info, self.routes = info, routes
        self.send, self.keep = send_keep
        self.piece = self.send.shape[3:]
        self.stage = 0
        self.next = swap(self.send, "dp", 1)

    def call(self, kernel, operands, shapes):
        return run(partial(kernel, self.routes), kernel.__name__[:-7], self.info, operands, shapes)

    def step(self):
        routes, piece = self.routes, tuple(self.piece)
        count = len(routes)
        both = lambda shape: [shape_of(shape), shape_of(shape, jnp.float32)]
        plane = [2 << first for first in routes]
        line = [2 << (1 - first) for first in routes]
        if self.stage == 0:
            self.outs = self.call(
                split_plane_kernel, [self.keep, self.next], both((2, 4, *piece)) * count
            )
            self.next = [swap(self.outs[2 * k], "dp", plane[k]) for k in range(count)]
        elif self.stage in (1, 2):
            operands = []
            for k in range(count):
                operands += [self.outs[2 * k + 1], self.next[k]]
            if self.stage == 1:
                self.outs = self.call(split_line_kernel, operands, both((4, *piece)) * count)
                self.next = [swap(self.outs[2 * k], "dp", line[k]) for k in range(count)]
            else:
                self.outs = self.call(split_near_kernel, operands, both((2, count, *piece)))
                self.next = swap(self.outs[0], "seq", 1)
        elif self.stage == 3:
            self.outs = self.call(
                split_far_kernel, [self.outs[1], self.next], both((count, *piece))
            )
            self.next = swap(self.outs[0], "seq", 2)
        elif self.stage == 4:
            self.outs = self.call(
                total_kernel, [self.outs[1], self.next], shape_of((count, *piece))
            )
            self.next = swap(self.outs, "seq", 2)
        elif self.stage == 5:
            self.outs = self.call(
                join_far_kernel, [self.outs, self.next], shape_of((2, count, *piece))
            )
            self.next = swap(self.outs, "seq", 1)
        elif self.stage == 6:
            self.outs = self.call(
                join_near_kernel, [self.outs, self.next], [shape_of((4, *piece))] * count
            )
            self.next = [swap(self.outs[k], "dp", line[k]) for k in range(count)]
        elif self.stage in (7, 8):
            operands = []
            for k in range(count):
                operands += [self.outs[k], self.next[k]]
            if self.stage == 7:
                self.outs = self.call(
                    join_line_kernel, operands, [shape_of((2, 4, *piece))] * count
                )
                self.next = [swap(self.outs[k], "dp", plane[k]) for k in range(count)]
            else:
                self.outs = self.call(
                    join_plane_kernel, operands, shape_of((4, 4, count, *piece))
                )
                self.next = swap(self.outs, "dp", 1)
        self.stage += 1

    def result(self, kernel, shapes, scratch=()):
        assert self.stage == 9
        return run(kernel, "join", self.info, [self.outs, self.next], shapes, scratch)


def join_wide_kernel(info, own_ref, in_ref, *out_refs):
    planes, parts, _, rows, cols = own_ref.shape
    for ref, core in ((own_ref, info[1]), (in_ref, 1 - info[1])):
        for p in range(planes):
            at = pl.multiple_of(core * (planes * rows) + p * rows, 8)
            for z in range(parts):
                for k, out_ref in enumerate(out_refs):
                    out_ref[pl.ds(at, rows), z * cols : (z + 1) * cols] = wide(ref[p, z, k])


def join_attn_kernel(
    info, own_ref, in_ref, query_ref, key_ref, value_ref, out_ref, gains_ref, total
):
    planes, parts, _, rows, cols = own_ref.shape
    for ref, core in ((own_ref, info[1]), (in_ref, 1 - info[1])):
        for p in range(planes):
            for z in range(parts):
                total[core * (planes * parts) + p * parts + z] = wide(ref[p, z, 0])
    at = 0
    features = query_ref.shape[1]
    for ref in (query_ref, key_ref, value_ref, out_ref):
        for piece in range(ref.shape[0] // rows):
            ref[piece * rows : (piece + 1) * rows] = total[at, :, :features]
            if ref is query_ref:
                gains_ref[piece * rows : (piece + 1) * rows] = total[at, :, cols - 128 :]
            at += 1


def exchange(values):
    return lax.all_to_all(values, "seq", 0, 0)


def local_rows(
    tokens,
    lengths,
    w_query,
    w_key,
    w_value,
    w_out,
    w_gate,
    w_up,
    w_down,
    gain_attn,
    gain_ffn,
    cotangent,
):
    row_count, block_len, model_width = tokens.shape
    kv_width, hidden_width = HK * DH, w_gate.shape[1]
    dp_at, seq_at = lax.axis_index("dp"), lax.axis_index("seq")
    length = lax.dynamic_slice_in_dim(lengths, seq_at, 1)
    info = jnp.concatenate([jnp.stack([seq_at, dp_at % 2, dp_at // 2]).astype(jnp.int32), length])
    Order.last = None
    row = exchange(jnp.swapaxes(tokens, 1, 2))
    Order.last = row

    half_dim = DH // 2
    positions = jnp.arange(row_count * block_len, dtype=jnp.float32).reshape(row_count, 1, -1)
    frequency = rope_base ** (-jnp.arange(half_dim, dtype=jnp.float32) / half_dim)
    angles = frequency[None, :, None] * positions
    angles = (jnp.cos(angles), jnp.sin(angles))
    w_heads = jnp.concatenate(
        [
            w_query.T.reshape(HK, GROUP * DH, model_width),
            w_key.T.reshape(HK, DH, model_width),
            w_value.T.reshape(HK, DH, model_width),
        ],
        axis=1,
    )
    w_heads_t = w_heads.reshape(-1, model_width).T
    gains = [jnp.broadcast_to(g[:, None], (model_width, block_len // 2)) for g in (gain_attn, gain_ffn)]

    cotangent, row, w_heads, *gains, angles = lax.optimization_barrier(
        (jnp.swapaxes(cotangent, 1, 2), row, w_heads, *gains, angles)
    )
    cot = exchange(cotangent)
    attn_in, queries, keys, values, attended, log_sum = attend(info, row, gains[0], w_heads, *angles)
    turned = [w_out, w_gate, w_up]
    *turned, w_down, attended = lax.optimization_barrier((*turned, w_down, attended))
    turned = [w.T for w in (*turned, w_down)]
    mixed, grad, grad_low, attended_grad, gain_ffn_part, *halves = ffn(
        info, row, attended, cot, gains[1], turned, [w_down, w_gate, w_up, w_out]
    )
    down = Sum(info, halves[:2], (1,))
    pair = Sum(info, halves[2:], (0, 1))
    mixed_out = exchange(mixed)
    down.step()
    pair.step()

    def back(h):
        return attend_back(
            info, h, queries, keys, values, attended, attended_grad, log_sum, angles
        )

    qkv_grads = [back(0)]
    down.step()
    qkv_grads.append(back(1))
    pair.step()
    down.step()
    Order.last = mixed_out
    qkv_grads.append(back(2))
    pair.step()
    down.step()
    tokens_grad, gain_attn_part = tokens_back(info, qkv_grads, row, grad, gains[0], w_heads_t)
    tokens_out = exchange(tokens_grad)
    attn = Sum(
        info,
        attn_grad(info, qkv_grads, attn_in, attended, grad_low, gain_attn_part, gain_ffn_part),
        (0,),
    )
    pair.step()
    down.step()
    attn.step()
    pair.step()
    down.step()
    attn.step()
    pair.step()
    down.step()
    attn.step()
    pair.step()
    down.step()
    attn.step()
    pair.step()
    attn.step()
    down.step()
    pair.step()
    attn.step()
    Order.last = tokens_out
    shape = shape_of((model_width, hidden_width), jnp.float32)
    w_down_sum = down.result(join_wide_kernel, [shape])[0]
    attn.step()
    attn.step()
    w_gate_sum, w_up_sum = pair.result(join_wide_kernel, [shape, shape])
    attn.step()
    square = shape_of((model_width, model_width), jnp.float32)
    narrow = shape_of((kv_width, model_width), jnp.float32)
    w_query_sum, w_key_sum, w_value_sum, w_out_sum, gains_sum = attn.result(
        join_attn_kernel,
        [square, narrow, narrow, square, shape_of((model_width, 128), jnp.float32)],
        [pltpu.VMEM((32, 48, 640), jnp.float32)],
    )
    return (
        jnp.swapaxes(mixed_out, 1, 2),
        jnp.swapaxes(tokens_out, 1, 2),
        w_query_sum,
        w_key_sum.T,
        w_value_sum.T,
        w_out_sum,
        w_gate_sum,
        w_up_sum,
        w_down_sum.T,
        gains_sum[:, 64],
        gains_sum[:, 65],
    )


def solution(mesh):
    whole_rows = mesh.shape["dp"] == 8 and mesh.shape["seq"] == 4
    return jax.shard_map(
        local_rows if whole_rows else local_general,
        mesh=mesh,
        in_specs=(
            P("dp", "seq", None),
            P("dp"),
            P(),
            P(),
            P(),
            P(),
            P(),
            P(),
            P(),
            P(),
            P(),
            P("dp", "seq", None),
        ),
        out_specs=(
            P("dp", "seq", None),
            P("dp", "seq", None),
            P(),
            P(),
            P(),
            P(),
            P(),
            P(),
            P(),
            P(),
            P(),
        ),
        check_vma=False,
    )
```

```python
from functools import partial
import math

import jax
import jax.numpy as jnp
from jax import lax
from jax.experimental import pallas as pl
from jax.experimental.pallas import tpu as pltpu
from jax.sharding import PartitionSpec as P

HQ = 9
HK = 3
DH = 64


eps_norm = 1e-05
rope_base = 100000.0
neg_large = -1e30


def norm_rows(values, gain_vec):
    return (
        values * lax.rsqrt(jnp.mean(values * values, axis=-1, keepdims=True) + eps_norm) * gain_vec
    )


def rotate(values, positions, turn_sign):
    half_dim = values.shape[-1] // 2
    frequency = rope_base ** (-jnp.arange(half_dim, dtype=jnp.float32) / half_dim)
    angles = turn_sign * positions.astype(jnp.float32)[:, None] * frequency[None, :]
    cosine = jnp.cos(angles)[:, None, :]
    sine_part = jnp.sin(angles)[:, None, :]
    first_half = values[..., :half_dim]
    second_half = values[..., half_dim:]
    return jnp.concatenate(
        [
            first_half * cosine - second_half * sine_part,
            second_half * cosine + first_half * sine_part,
        ],
        axis=-1,
    )


def inner_rows(left, right):
    return lax.dot_general(
        left, right, (((0,), (0,)), ((), ())), preferred_element_type=jnp.float32
    )


def times_t(left, right):
    return lax.dot_general(
        left, right, (((1,), (1,)), ((), ())), preferred_element_type=jnp.float32
    )


def fold_piece(block_len, step_fn, carry, pieces):
    piece_count = pieces.shape[1] // block_len

    def inner_step(index_step, state):
        part_piece = lax.dynamic_slice_in_dim(pieces, index_step * block_len, block_len, 1)
        return step_fn(state, part_piece, index_step * block_len)

    return lax.fori_loop(0, piece_count, inner_step, carry)


def local_general(
    tokens,
    lengths,
    w_query,
    w_key,
    w_value,
    w_out,
    w_gate,
    w_up,
    w_down,
    gain_attn,
    gain_ffn,
    cotangent,
):
    row_count, block_len, model_width = tokens.shape
    group_size = HQ // HK
    kv_width = HK * DH
    score_scale = 1.0 / math.sqrt(DH)
    seq_devices = lax.axis_size("seq")
    my_start = lax.axis_index("seq") * block_len
    positions = my_start + jnp.arange(block_len, dtype=jnp.int32)
    longest = jnp.max(lengths)
    live_rows = positions[None, :] < lengths[:, None]
    query_active = my_start < longest
    inputs = tokens.reshape(-1, model_width).astype(jnp.float32)
    attn_norm, attn_pull = jax.vjp(norm_rows, inputs, gain_attn)
    attn_in = attn_norm.astype(jnp.bfloat16)
    query_pre = jnp.dot(attn_in, w_query, preferred_element_type=jnp.float32)
    query_heads = rotate(query_pre.reshape(row_count, block_len, HQ, DH), positions, 1.0).astype(
        jnp.bfloat16
    )
    query_heads = query_heads.reshape(row_count, block_len, HK, group_size, DH)
    key_pre = jnp.dot(attn_in, w_key, preferred_element_type=jnp.float32)
    key_heads = rotate(key_pre.reshape(row_count, block_len, HK, DH), positions, 1.0).astype(
        jnp.bfloat16
    )
    value_heads = jnp.dot(attn_in, w_value, preferred_element_type=jnp.float32).astype(jnp.bfloat16)
    key_value = jnp.concatenate(
        [
            key_heads.reshape(row_count, block_len, kv_width),
            value_heads.reshape(row_count, block_len, kv_width),
        ],
        axis=-1,
    )

    def allowed_for(piece_start):
        key_pos = piece_start + jnp.arange(block_len, dtype=jnp.int32)
        causal = key_pos[None, None, :] <= positions[None, :, None]
        inside = key_pos[None, None, :] < lengths[:, None, None]
        return causal & inside

    def needed_for(piece_start):
        return (piece_start <= my_start) & (piece_start < longest) & query_active

    def split_piece(pieces):
        key_part = pieces[..., :kv_width].reshape(row_count, block_len, HK, DH)
        value_part = pieces[..., kv_width:].reshape(row_count, block_len, HK, DH)
        return (key_part, value_part)

    def forward_block(carry, pieces, piece_start):

        def forward_compute_block(state):
            row_max, row_total, weighted = state
            key_part, value_part = split_piece(pieces)
            scores = (
                jnp.einsum(
                    "rqhgd,rkhd->rhgqk", query_heads, key_part, preferred_element_type=jnp.float32
                )
                * score_scale
            )
            allowed = allowed_for(piece_start)[:, None, None]
            scores = jnp.where(allowed, scores, neg_large)
            new_max = jnp.maximum(row_max, jnp.max(scores, axis=-1))
            shrink = jnp.exp(row_max - new_max)
            exp_scores = jnp.where(allowed, jnp.exp(scores - new_max[..., None]), 0.0)
            row_total = row_total * shrink + jnp.sum(exp_scores, axis=-1)
            update = jnp.einsum(
                "rhgqk,rkhd->rqhgd",
                exp_scores.astype(jnp.bfloat16),
                value_part,
                preferred_element_type=jnp.float32,
            )
            weighted = weighted * jnp.moveaxis(shrink, 3, 1)[..., None] + update
            return (new_max, row_total, weighted)

        return lax.cond(needed_for(piece_start), forward_compute_block, lambda state: state, carry)

    stat_shape = (row_count, HK, group_size, block_len)
    forward_init = (
        jnp.full(stat_shape, neg_large, jnp.float32),
        jnp.zeros(stat_shape, jnp.float32),
        jnp.zeros((row_count, block_len, HK, group_size, DH), jnp.float32),
    )
    forward_state = fold_piece(
        block_len, forward_block, forward_init, lax.all_gather(key_value, "seq", axis=1, tiled=True)
    )
    row_max, row_total, weighted = forward_state
    safe_total = jnp.where(row_total > 0, row_total, 1.0)
    attn_heads = weighted / jnp.moveaxis(safe_total, 3, 1)[..., None]
    attn_heads = jnp.where(live_rows[:, :, None, None, None], attn_heads, 0.0)
    log_sum = jnp.where(live_rows[:, None, None, :], row_max + jnp.log(safe_total), 0.0)
    attn_low = attn_heads.reshape(-1, HQ * DH).astype(jnp.bfloat16)
    residual = inputs + jnp.dot(attn_low, w_out, preferred_element_type=jnp.float32)
    ffn_norm, ffn_pull = jax.vjp(norm_rows, residual, gain_ffn)
    ffn_in = ffn_norm.astype(jnp.bfloat16)
    gate_proj = jnp.dot(ffn_in, w_gate, preferred_element_type=jnp.float32)
    up_proj = jnp.dot(ffn_in, w_up, preferred_element_type=jnp.float32)
    product, swiglu_pull = jax.vjp(
        lambda gate_in, up_in: jax.nn.silu(gate_in) * up_in, gate_proj, up_proj
    )
    hidden = product.astype(jnp.bfloat16)
    branch = jnp.dot(hidden, w_down, preferred_element_type=jnp.float32)
    mixed = (residual + branch).astype(jnp.bfloat16).reshape(row_count, block_len, model_width)
    out_low = cotangent.reshape(-1, model_width)
    out_grad = out_low.astype(jnp.float32)
    w_down_grad = inner_rows(hidden, out_low)
    hidden_grad = times_t(out_low, w_down)
    gate_grad, up_grad = swiglu_pull(hidden_grad)
    gate_low = gate_grad.astype(jnp.bfloat16)
    up_low = up_grad.astype(jnp.bfloat16)
    w_gate_grad = inner_rows(ffn_in, gate_low)
    w_up_grad = inner_rows(ffn_in, up_low)
    ffn_in_grad = times_t(gate_low, w_gate) + times_t(up_low, w_up)
    residual_part, gain_ffn_grad = ffn_pull(ffn_in_grad)
    residual_grad = out_grad + residual_part
    residual_low = residual_grad.astype(jnp.bfloat16)
    w_out_grad = inner_rows(attn_low, residual_low)
    attended_grad = times_t(residual_low, w_out).reshape(row_count, block_len, HK, group_size, DH)
    attended_grad = jnp.where(live_rows[:, :, None, None, None], attended_grad, 0.0).astype(
        jnp.bfloat16
    )
    grad_dot = jnp.moveaxis(jnp.sum(attended_grad.astype(jnp.float32) * attn_heads, axis=-1), 1, 3)

    def backward_block(with_kv, carry, pieces, piece_start):

        def backward_compute_block(state):
            key_part, value_part = split_piece(pieces)
            scores = (
                jnp.einsum(
                    "rqhgd,rkhd->rhgqk", query_heads, key_part, preferred_element_type=jnp.float32
                )
                * score_scale
            )
            allowed = allowed_for(piece_start)[:, None, None]
            weights_now = jnp.where(allowed, jnp.exp(scores - log_sum[..., None]), 0.0)
            weights_grad = jnp.einsum(
                "rqhgd,rkhd->rhgqk", attended_grad, value_part, preferred_element_type=jnp.float32
            )
            score_grad = (weights_now * (weights_grad - grad_dot[..., None])).astype(jnp.bfloat16)
            query_grad = (
                state[0]
                + jnp.einsum(
                    "rhgqk,rkhd->rqhgd", score_grad, key_part, preferred_element_type=jnp.float32
                )
                * score_scale
            )
            kv_grad = state[1]
            values_grad = jnp.einsum(
                "rhgqk,rqhgd->rkhd",
                weights_now.astype(jnp.bfloat16),
                attended_grad,
                preferred_element_type=jnp.float32,
            )
            keys_grad = (
                jnp.einsum(
                    "rhgqk,rqhgd->rkhd", score_grad, query_heads, preferred_element_type=jnp.float32
                )
                * score_scale
            )
            local_kv = jnp.concatenate(
                [
                    keys_grad.reshape(row_count, block_len, kv_width),
                    values_grad.reshape(row_count, block_len, kv_width),
                ],
                axis=-1,
            )
            current = lax.dynamic_slice_in_dim(kv_grad, piece_start, block_len, 1)
            kv_grad = lax.dynamic_update_slice_in_dim(kv_grad, current + local_kv, piece_start, 1)
            return (query_grad, kv_grad)

        return lax.cond(needed_for(piece_start), backward_compute_block, lambda state: state, carry)

    query_zero = jnp.zeros((row_count, block_len, HK, group_size, DH), jnp.float32)
    backward_init = (
        query_zero,
        jnp.zeros((row_count, block_len * seq_devices, 2 * kv_width), jnp.float32),
    )
    step_back = partial(backward_block, True)
    backward_state = fold_piece(
        block_len, step_back, backward_init, lax.all_gather(key_value, "seq", axis=1, tiled=True)
    )
    query_grad = backward_state[0]
    own_kv_grad = lax.psum_scatter(
        backward_state[1].astype(jnp.bfloat16), "seq", scatter_dimension=1, tiled=True
    ).astype(jnp.float32)
    query_low = (
        rotate(query_grad.reshape(row_count, block_len, HQ, DH), positions, -1.0)
        .astype(jnp.bfloat16)
        .reshape(-1, HQ * DH)
    )
    key_low = (
        rotate(own_kv_grad[..., :kv_width].reshape(row_count, block_len, HK, DH), positions, -1.0)
        .astype(jnp.bfloat16)
        .reshape(-1, kv_width)
    )
    value_low = own_kv_grad[..., kv_width:].astype(jnp.bfloat16).reshape(-1, kv_width)
    w_query_grad = inner_rows(attn_in, query_low)
    w_key_grad = inner_rows(attn_in, key_low)
    w_value_grad = inner_rows(attn_in, value_low)
    attn_in_grad = (
        times_t(query_low, w_query) + times_t(key_low, w_key) + times_t(value_low, w_value)
    )
    inputs_part, gain_attn_grad = attn_pull(attn_in_grad)
    tokens_grad = (
        (residual_grad + inputs_part)
        .astype(jnp.bfloat16)
        .reshape(row_count, block_len, model_width)
    )
    (
        w_query_grad,
        w_key_grad,
        w_value_grad,
        w_out_grad,
        w_gate_grad,
        w_up_grad,
        w_down_grad,
        gain_attn_grad,
        gain_ffn_grad,
    ) = lax.psum(
        (
            w_query_grad,
            w_key_grad,
            w_value_grad,
            w_out_grad,
            w_gate_grad,
            w_up_grad,
            w_down_grad,
            gain_attn_grad,
            gain_ffn_grad,
        ),
        ("dp", "seq"),
    )
    return (
        mixed,
        tokens_grad,
        w_query_grad,
        w_key_grad,
        w_value_grad,
        w_out_grad,
        w_gate_grad,
        w_up_grad,
        w_down_grad,
        gain_attn_grad,
        gain_ffn_grad,
    )


GROUP = HQ // HK
HEAD_ROWS = (GROUP + 2) * DH
SCALE = DH**-0.5
FULL = pl.BlockSpec(memory_space=pltpu.VMEM)
SMEM = pl.BlockSpec(memory_space=pltpu.SMEM)
ANY = pl.BlockSpec(memory_space=pl.ANY)


def shape_of(shape, dtype=jnp.bfloat16):
    return jax.ShapeDtypeStruct(shape, dtype)


def low(values):
    return values.astype(jnp.bfloat16)


def wide(values):
    return values.astype(jnp.float32)


def mul_nt(left, right):
    return lax.dot_general(
        left, right, (((1,), (1,)), ((), ())), preferred_element_type=jnp.float32
    )


def mul_nn(left, right):
    return lax.dot_general(
        left, right, (((1,), (0,)), ((), ())), preferred_element_type=jnp.float32
    )


class Order:
    last = None
    also = ()


def run(
    kernel, name, info, operands, out_shapes, scratch=(), vmem=12, grid=(), in_specs=None, out_specs=None
):
    after = [*([] if Order.last is None else [Order.last]), *Order.also]
    Order.also = ()
    taken = len(operands)

    def body(*refs):
        kernel(*refs[: 1 + taken], *refs[1 + taken + len(after) :])

    many = isinstance(out_shapes, list)
    outs = pl.pallas_call(
        body,
        grid=grid,
        in_specs=[SMEM] + (in_specs or [FULL] * taken) + [ANY] * len(after),
        out_specs=out_specs or ([FULL] * len(out_shapes) if many else FULL),
        scratch_shapes=list(scratch),
        out_shape=out_shapes,
        compiler_params=pltpu.CompilerParams(vmem_limit_bytes=vmem * 2**20),
        cost_estimate=pl.CostEstimate(flops=1000, bytes_accessed=1000, transcendentals=0),
        name=name,
    )(info, *operands, *after)
    Order.last = min(outs, key=lambda v: v.size) if many else outs
    return outs


def whole(*shape):
    return pl.BlockSpec(shape, lambda b: (0,) * len(shape))


def at_block(*shape):
    return pl.BlockSpec((1, *shape), lambda b: (b, *[0] * len(shape)))


def turn(values, cosine, sine_part):
    first_half, second_half = values[: DH // 2], values[DH // 2 :]
    return jnp.concatenate(
        [
            first_half * cosine - second_half * sine_part,
            second_half * cosine + first_half * sine_part,
        ],
        axis=0,
    )


def inverse_rms(values):
    mean = jnp.sum(values * values, axis=0, keepdims=True) * (1.0 / values.shape[0])
    return lax.rsqrt(mean + eps_norm)


def norm_back(values, grad, gain):
    scale = inverse_rms(values)
    turned = grad * gain
    inner = jnp.sum(turned * values, axis=0, keepdims=True) * (1.0 / values.shape[0])
    part = scale * turned - values * (scale * scale * scale * inner)
    return part, grad * values * scale


def gain_of(ref):
    return jnp.concatenate([ref[...], ref[...]], axis=1)


def causal_mask(width):
    key_at = lax.broadcasted_iota(jnp.int32, (width, width), 0)
    query_at = lax.broadcasted_iota(jnp.int32, (width, width), 1)
    return jnp.concatenate([key_at <= query_at] * GROUP, axis=1)


def heads_of(values):
    return jnp.concatenate([values[j * DH : (j + 1) * DH] for j in range(GROUP)], axis=1)


def attend_kernel(
    info,
    row_ref,
    gain_ref,
    weights_ref,
    cos_ref,
    sin_ref,
    attn_in_ref,
    query_ref,
    key_ref,
    value_ref,
    out_ref,
    lse_ref,
    key_rows,
):
    blocks, _, width = row_ref.shape

    @pl.when(pl.program_id(0) == 0)
    def _():
        gain = gain_of(gain_ref)
        for b in range(blocks):
            values = wide(row_ref[b])
            attn_in_ref[b] = low(values * inverse_rms(values) * gain)

    mask = causal_mask(width)
    for b in range(blocks):
        pre = mul_nn(weights_ref[0], attn_in_ref[b])
        cosine, sine_part = cos_ref[b], sin_ref[b]
        for j in range(GROUP):
            query_ref[0, b, j * DH : (j + 1) * DH] = low(
                turn(pre[j * DH : (j + 1) * DH], cosine, sine_part) * SCALE
            )
        keys = low(turn(pre[GROUP * DH : (GROUP + 1) * DH], cosine, sine_part))
        key_ref[0, b] = keys
        key_rows[b] = keys.T
        value_ref[0, b] = low(pre[(GROUP + 1) * DH :])
    for b in range(blocks):
        queries = heads_of(query_ref[0, b])
        scores, top = [], None
        for k in range(b + 1):
            part = mul_nn(key_rows[k], queries)
            if k == b:
                part = jnp.where(mask, part, neg_large)
            scores.append(part)
            part_top = jnp.max(part, axis=0, keepdims=True)
            top = part_top if top is None else jnp.maximum(top, part_top)
        total, weighted = 0.0, 0.0
        for k in range(b + 1):
            weights_now = jnp.exp(scores[k] - top)
            total = total + jnp.sum(weights_now, axis=0, keepdims=True)
            weighted = weighted + mul_nn(value_ref[0, k], low(weights_now))
        weighted = weighted * (1.0 / total)
        log_sum = top + jnp.log(total)
        live = b * width + lax.broadcasted_iota(jnp.int32, (1, width), 1) < info[3]
        for j in range(GROUP):
            mine = slice(j * width, (j + 1) * width)
            out_ref[0, b, j * DH : (j + 1) * DH] = low(jnp.where(live, weighted[:, mine], 0.0))
            lse_ref[0, b, j : j + 1] = log_sum[:, mine]


def attend(info, row, gain, w_heads, cosine, sine_part):
    blocks, features, width = row.shape
    head = lambda rows: pl.BlockSpec((1, blocks, rows, width), lambda h: (h, 0, 0, 0))
    return run(
        attend_kernel,
        "attend",
        info,
        [row, gain, w_heads, cosine, sine_part],
        [
            shape_of((blocks, features, width)),
            shape_of((HK, blocks, GROUP * DH, width)),
            shape_of((HK, blocks, DH, width)),
            shape_of((HK, blocks, DH, width)),
            shape_of((HK, blocks, GROUP * DH, width)),
            shape_of((HK, blocks, 8, width), jnp.float32),
        ],
        [pltpu.VMEM((blocks, width, DH), jnp.bfloat16)],
        32,
        (HK,),
        [
            whole(*row.shape),
            whole(*gain.shape),
            pl.BlockSpec((1, HEAD_ROWS, features), lambda h: (h, 0, 0)),
            whole(*cosine.shape),
            whole(*cosine.shape),
        ],
        [whole(*row.shape), *[head(rows) for rows in (GROUP * DH, DH, DH, GROUP * DH, 8)]],
    )


def attend_back_kernel(
    info,
    query_ref,
    key_ref,
    value_ref,
    out_ref,
    out_grad_ref,
    lse_ref,
    cos_ref,
    sin_ref,
    grad_ref,
    key_rows,
    value_rows,
    key_sum,
    value_sum,
):
    blocks, width = query_ref.shape[1], query_ref.shape[3]
    for b in range(blocks):
        key_rows[b] = key_ref[0, b].T
        value_rows[b] = value_ref[0, b].T
    mask = causal_mask(width)
    for b in reversed(range(blocks)):
        queries, out_grad = heads_of(query_ref[0, b]), heads_of(out_grad_ref[b])
        grad_dot = jnp.sum(wide(out_grad) * wide(heads_of(out_ref[0, b])), axis=0, keepdims=True)
        log_sum = jnp.concatenate([lse_ref[0, b, j : j + 1] for j in range(GROUP)], axis=1)
        query_grad = 0.0
        for k in range(b + 1):
            weights_now = jnp.exp(mul_nn(key_rows[k], queries) - log_sum)
            if k == b:
                weights_now = jnp.where(mask, weights_now, 0.0)
            weights_grad = mul_nn(value_rows[k], out_grad)
            score_grad = low(weights_now * (weights_grad - grad_dot))
            value_part = mul_nt(out_grad, low(weights_now))
            key_part = mul_nt(queries, score_grad)
            if b == blocks - 1:
                value_sum[k] = value_part
                key_sum[k] = key_part
            else:
                value_sum[k] += value_part
                key_sum[k] += key_part
            query_grad = query_grad + mul_nn(key_ref[0, k], score_grad)
        cosine, sine_part = cos_ref[b], -sin_ref[b]
        for j in range(GROUP):
            grad_ref[b, j * DH : (j + 1) * DH] = low(
                turn(query_grad[:, j * width : (j + 1) * width], cosine * SCALE, sine_part * SCALE)
            )
        grad_ref[b, GROUP * DH : (GROUP + 1) * DH] = low(turn(key_sum[b], cosine, sine_part))
        grad_ref[b, (GROUP + 1) * DH :] = low(value_sum[b])


def attend_back(info, h, queries, keys, values, attended, attended_grad, log_sum, angles):
    _, blocks, _, width = queries.shape
    head = lambda rows: pl.BlockSpec((1, blocks, rows, width), lambda s: (h, 0, 0, 0))
    angle = whole(*angles[0].shape)
    return run(
        attend_back_kernel,
        "attend_back",
        info,
        [queries, keys, values, attended, attended_grad, log_sum, *angles],
        shape_of((blocks, HEAD_ROWS, width)),
        [pltpu.VMEM((blocks, width, DH), jnp.bfloat16)] * 2
        + [pltpu.VMEM((blocks, DH, width), jnp.float32)] * 2,
        16,
        (1,),
        [
            *[head(rows) for rows in (GROUP * DH, DH, DH, GROUP * DH)],
            pl.BlockSpec((blocks, GROUP * DH, width), lambda s: (0, h, 0)),
            head(8),
            angle,
            angle,
        ],
        whole(blocks, HEAD_ROWS, width),
    )


def lanes_of(ref, rows=slice(None)):
    return jnp.concatenate([ref[b, rows] for b in range(ref.shape[0])], axis=1)


def put_grad(values, ref, at):
    planes, parts, _, rows, cols = ref.shape
    for p in range(planes):
        for z in range(parts):
            ref[p, z, at] = values[p * rows : (p + 1) * rows, z * cols : (z + 1) * cols].astype(
                ref.dtype
            )


CHUNK = 768


def ffn_kernel(
    info,
    row_ref,
    att_ref,
    cot_ref,
    in1_ref,
    in2_ref,
    in3_ref,
    gain_ref,
    w_out_t_ref,
    w_gate_t_ref,
    w_up_t_ref,
    w_down_t_ref,
    w_down_ref,
    w_gate_ref,
    w_up_ref,
    w_out_ref,
    mixed_ref,
    grad_ref,
    low_ref,
    att_grad_ref,
    gain_grad_ref,
    send_ref,
    keep_ref,
    ffn_ins,
    cots,
    hiddens,
    gates,
    ups,
):
    b = pl.program_id(0)
    width = row_ref.shape[2]
    gain = gain_of(gain_ref)
    attended = jnp.concatenate([att_ref[h, 0] for h in range(HK)], axis=0)
    residual = wide(row_ref[0]) + mul_nn(w_out_t_ref[...], attended)
    ffn_in = low(residual * inverse_rms(residual) * gain)
    ffn_ins[b] = ffn_in
    from_step = lax.rem(info[0] + 4 - b, 4)

    @pl.when(from_step == 0)
    def _():
        cots[b] = cot_ref[b]

    for step, ref in ((1, in1_ref), (2, in2_ref), (3, in3_ref)):

        @pl.when(from_step == step)
        def _():
            cots[b] = ref[...]

    cot = cots[b]
    mixed, ffn_in_grad = residual, 0.0
    for at in range(0, hiddens.shape[1], CHUNK):
        part = slice(at, at + CHUNK)
        gate = mul_nn(w_gate_t_ref[part], ffn_in)
        up = mul_nn(w_up_t_ref[part], ffn_in)
        hidden_grad = mul_nn(w_down_ref[part], cot)
        sigmoid = 1.0 / (1.0 + jnp.exp(-gate))
        silu = gate * sigmoid
        hidden = low(silu * up)
        gate_grad = low(hidden_grad * up * (sigmoid + silu * (1.0 - sigmoid)))
        up_grad = low(hidden_grad * silu)
        hiddens[b, part] = hidden
        gates[b, part] = gate_grad
        ups[b, part] = up_grad
        mixed = mixed + mul_nn(w_down_t_ref[:, part], hidden)
        ffn_in_grad = ffn_in_grad + (
            mul_nn(w_gate_ref[:, part], gate_grad) + mul_nn(w_up_ref[:, part], up_grad)
        )
    mixed_ref[0] = low(mixed)
    part, gain_terms = norm_back(residual, ffn_in_grad, gain)
    gain_terms = gain_terms[:, : width // 2] + gain_terms[:, width // 2 :]

    @pl.when(b == 0)
    def _():
        gain_grad_ref[...] = gain_terms

    @pl.when(b > 0)
    def _():
        gain_grad_ref[...] += gain_terms

    grad = wide(cot) + part
    grad_ref[0] = grad
    grad_low = low(grad)
    low_ref[0] = grad_low
    live = b * width + lax.broadcasted_iota(jnp.int32, (1, width), 1) < info[3]
    att_grad_ref[0] = low(jnp.where(live, mul_nn(w_out_ref[...], grad_low), 0.0))

    @pl.when(b == pl.num_programs(0) - 1)
    def _():
        rows = grad_ref.shape[1] // 2
        for half, ref in ((1 - info[1], send_ref), (info[1], keep_ref)):
            own = pl.ds(pl.multiple_of(half * rows, 16), rows)
            left = lanes_of(ffn_ins, own)
            put_grad(mul_nt(left, lanes_of(gates)), ref, 0)
            put_grad(mul_nt(left, lanes_of(ups)), ref, 1)
            put_grad(mul_nt(lanes_of(cots, own), lanes_of(hiddens)), ref, 2)


def ffn(info, row, attended, cot, arrived, gain, turned, straight):
    blocks, features, width = row.shape
    hidden = turned[1].shape[0]
    block, long = (blocks, features, width), (blocks, hidden, width)
    pieces = (4, 4, 3, features // 8, hidden // 4)
    return run(
        ffn_kernel,
        "ffn",
        info,
        [row, attended, cot, *arrived, gain, *turned, *straight],
        [
            shape_of(block),
            shape_of(block, jnp.float32),
            shape_of(block),
            shape_of(block),
            shape_of(gain.shape, jnp.float32),
            shape_of(pieces),
            shape_of(pieces, jnp.float32),
        ],
        [pltpu.VMEM(block, jnp.bfloat16)] * 2 + [pltpu.VMEM(long, jnp.bfloat16)] * 3,
        52,
        (blocks,),
        [
            at_block(features, width),
            pl.BlockSpec((HK, 1, GROUP * DH, width), lambda b: (0, b, 0, 0)),
            whole(*cot.shape),
            *[whole(features, width)] * 3,
            whole(*gain.shape),
            *[FULL] * 8,
        ],
        [
            *[at_block(features, width)] * 4,
            whole(*gain.shape),
            *[whole(*pieces)] * 2,
        ],
    )


PIECE_ROWS = 48
PIECE_COLS = 640


def tokens_back_kernel(
    info, g0_ref, g1_ref, g2_ref, row_ref, grad_ref, gain_ref, w_ref, out_ref, gain_sum
):
    width = row_ref.shape[2]
    gain = gain_of(gain_ref)
    gain_sum[...] = jnp.zeros_like(gain_sum)

    def one_block(b, carry):
        qkv = jnp.concatenate([g0_ref[b], g1_ref[b], g2_ref[b]], axis=0)
        part, gain_terms = norm_back(wide(row_ref[b]), mul_nn(w_ref[...], qkv), gain)
        gain_sum[...] += gain_terms[:, : width // 2] + gain_terms[:, width // 2 :]
        out_ref[b] = low(grad_ref[b] + part)
        return carry

    lax.fori_loop(0, row_ref.shape[0], one_block, 0)


def tokens_back(info, qkv_grads, row, grad, gain, w_heads_t):
    return run(
        tokens_back_kernel,
        "tokens_back",
        info,
        [*qkv_grads, row, grad, gain, w_heads_t],
        [shape_of(row.shape), shape_of(gain.shape, jnp.float32)],
    )


def attn_grad_kernel(
    info, g0_ref, g1_ref, g2_ref, attn_in_ref, att_ref, low_ref, gain1_ref, gain2_ref, *outs
):
    send_ref, keep_ref = outs
    features = attn_in_ref.shape[1]

    def put(values, ref, at, columns=None):
        if columns is None:
            columns = jnp.zeros((values.shape[0], PIECE_COLS - features), jnp.float32)
        for piece in range(values.shape[0] // PIECE_ROWS):
            rows = slice(piece * PIECE_ROWS, (piece + 1) * PIECE_ROWS)
            p, z = (at + piece) // 4, (at + piece) % 4
            ref[p, z, 0, :, :features] = values[rows].astype(ref.dtype)
            ref[p, z, 0, :, features:] = columns[rows].astype(ref.dtype)

    def take(start, size):
        rows = slice(start, start + size)
        return jnp.concatenate([lanes_of(g, rows) for g in (g0_ref, g1_ref, g2_ref)], axis=0)

    def first_half(ref):
        attn_in = lanes_of(attn_in_ref)
        lane = lax.broadcasted_iota(jnp.int32, (features, PIECE_COLS - features), 1)
        gains = jnp.where(
            lane == 0,
            jnp.sum(gain1_ref[...], axis=1, keepdims=True),
            jnp.where(lane == 1, jnp.sum(gain2_ref[...], axis=1, keepdims=True), 0.0),
        )
        put(mul_nt(attn_in, take(0, GROUP * DH)), ref, 0, gains)
        put(mul_nt(take(GROUP * DH, DH), attn_in), ref, features // PIECE_ROWS)

    def second_half(ref):
        put(mul_nt(take((GROUP + 1) * DH, DH), lanes_of(attn_in_ref)), ref, 0)
        attended = jnp.concatenate([lanes_of(att_ref.at[h]) for h in range(HK)], axis=0)
        put(mul_nt(attended, lanes_of(low_ref)), ref, HK * DH // PIECE_ROWS)

    @pl.when(info[1] == 0)
    def _():
        second_half(send_ref)
        first_half(keep_ref)

    @pl.when(info[1] == 1)
    def _():
        first_half(send_ref)
        second_half(keep_ref)


def attn_grad(info, qkv_grads, attn_in, attended, grad_low, gain1, gain2):
    pieces = (4, 4, 1, PIECE_ROWS, PIECE_COLS)
    return run(
        attn_grad_kernel,
        "attn_grad",
        info,
        [*qkv_grads, attn_in, attended, grad_low, gain1, gain2],
        [shape_of(pieces), shape_of(pieces, jnp.float32)],
    )


def bit_of(value, bit):
    return lax.rem(value // (1 << bit), 2)


def plane_at(first, own, other):
    return own + 2 * other if first == 0 else other + 2 * own


def spot(routes, near, far):
    if len(routes) == 1:
        return 0, near + 2 * far
    return far, near


def split_plane_kernel(routes, info, keep_ref, in_ref, *outs):
    for k, (first, places) in enumerate(routes):
        mine = bit_of(info[2], first)
        send_ref, own_ref = outs[2 * k : 2 * k + 2]
        for t in range(2):
            there, here = plane_at(first, 1 - mine, t), plane_at(first, mine, t)
            for at, z in enumerate(places):
                send_ref[t, at] = low(keep_ref[there, z] + wide(in_ref[there, z]))
                own_ref[t, at] = keep_ref[here, z] + wide(in_ref[here, z])


def split_line_kernel(routes, info, *refs):
    count = len(routes)
    ins, outs = refs[: 2 * count], refs[2 * count :]
    for k, (first, _) in enumerate(routes):
        mine = bit_of(info[2], 1 - first)
        keep_ref, in_ref = ins[2 * k : 2 * k + 2]
        send_ref, own_ref = outs[2 * k : 2 * k + 2]
        send_ref[...] = low(keep_ref[1 - mine] + wide(in_ref[1 - mine]))
        own_ref[...] = keep_ref[mine] + wide(in_ref[mine])


def split_near_kernel(routes, info, *refs):
    ins, (send_ref, own_ref) = refs[:-2], refs[-2:]
    near = bit_of(info[0], 0)
    for far in range(2):
        k, there = spot(routes, 1 - near, far)
        k, here = spot(routes, near, far)
        keep_ref, in_ref = ins[2 * k : 2 * k + 2]
        send_ref[far] = low(keep_ref[there] + wide(in_ref[there]))
        own_ref[far] = keep_ref[here] + wide(in_ref[here])


def split_far_kernel(routes, info, keep_ref, in_ref, send_ref, own_ref):
    far = bit_of(info[0], 1)
    send_ref[...] = low(keep_ref[1 - far] + wide(in_ref[1 - far]))
    own_ref[...] = keep_ref[far] + wide(in_ref[far])


def total_kernel(routes, info, keep_ref, in_ref, out_ref):
    out_ref[...] = low(keep_ref[...] + wide(in_ref[...]))


def join_far_kernel(routes, info, own_ref, in_ref, out_ref):
    far = bit_of(info[0], 1)
    out_ref[far] = own_ref[...]
    out_ref[1 - far] = in_ref[...]


def join_near_kernel(routes, info, own_ref, in_ref, *outs):
    near = bit_of(info[0], 0)
    for far in range(2):
        k, here = spot(routes, near, far)
        k, there = spot(routes, 1 - near, far)
        outs[k][here] = own_ref[far]
        outs[k][there] = in_ref[far]


def join_line_kernel(routes, info, *refs):
    count = len(routes)
    ins, outs = refs[: 2 * count], refs[2 * count :]
    for k, (first, _) in enumerate(routes):
        mine = bit_of(info[2], 1 - first)
        outs[k][mine] = ins[2 * k][...]
        outs[k][1 - mine] = ins[2 * k + 1][...]


def join_plane_kernel(routes, info, *refs):
    ins, out_ref = refs[:-1], refs[-1]
    for k, (first, places) in enumerate(routes):
        mine = bit_of(info[2], first)
        own_ref, in_ref = ins[2 * k : 2 * k + 2]
        for t in range(2):
            for at, z in enumerate(places):
                out_ref[plane_at(first, mine, t), z] = own_ref[t, at]
                out_ref[plane_at(first, 1 - mine, t), z] = in_ref[t, at]


def swap(values, axis, bits):
    count = 8 if axis == "dp" else 4
    return lax.ppermute(values, axis, [(k, k ^ bits) for k in range(count)])


TWO_ROUTES = ((0, (0, 1)), (1, (2, 3)))


class Sum:
    def __init__(self, info, send_keep, routes):
        self.info, self.routes = info, routes
        self.send, self.keep = send_keep
        self.piece = self.send.shape[2:]
        self.stage = 0
        self.next = swap(self.send, "dp", 1)

    def call(self, kernel, operands, shapes):
        return run(partial(kernel, self.routes), kernel.__name__[:-7], self.info, operands, shapes)

    def step(self):
        routes, piece = self.routes, tuple(self.piece)
        count, places = len(routes), len(routes[0][1])
        both = lambda *shape: [shape_of(shape), shape_of(shape, jnp.float32)]
        plane = [2 << first for first, _ in routes]
        line = [2 << (1 - first) for first, _ in routes]
        if self.stage == 0:
            self.outs = self.call(
                split_plane_kernel, [self.keep, self.next], both(2, places, *piece) * count
            )
            self.next = [swap(self.outs[2 * k], "dp", plane[k]) for k in range(count)]
        elif self.stage in (1, 2):
            operands = []
            for k in range(count):
                operands += [self.outs[2 * k + 1], self.next[k]]
            if self.stage == 1:
                self.outs = self.call(split_line_kernel, operands, both(places, *piece) * count)
                self.next = [swap(self.outs[2 * k], "dp", line[k]) for k in range(count)]
            else:
                self.outs = self.call(split_near_kernel, operands, both(2, *piece))
                self.next = swap(self.outs[0], "seq", 1)
        elif self.stage == 3:
            self.outs = self.call(split_far_kernel, [self.outs[1], self.next], both(*piece))
            self.next = swap(self.outs[0], "seq", 2)
        elif self.stage == 4:
            self.outs = self.call(total_kernel, [self.outs[1], self.next], shape_of(piece))
            self.next = swap(self.outs, "seq", 2)
        elif self.stage == 5:
            self.outs = self.call(join_far_kernel, [self.outs, self.next], shape_of((2, *piece)))
            self.next = swap(self.outs, "seq", 1)
        elif self.stage == 6:
            self.outs = self.call(
                join_near_kernel, [self.outs, self.next], [shape_of((places, *piece))] * count
            )
            self.next = [swap(self.outs[k], "dp", line[k]) for k in range(count)]
        elif self.stage in (7, 8):
            operands = []
            for k in range(count):
                operands += [self.outs[k], self.next[k]]
            if self.stage == 7:
                self.outs = self.call(
                    join_line_kernel, operands, [shape_of((2, places, *piece))] * count
                )
                self.next = [swap(self.outs[k], "dp", plane[k]) for k in range(count)]
            else:
                self.outs = self.call(join_plane_kernel, operands, shape_of((4, 4, *piece)))
                self.next = swap(self.outs, "dp", 1)
        self.stage += 1


def add_core_kernel(info, keep_ref, in_ref, own_ref, *out_refs):
    plane = info[2]
    own_ref[...] = keep_ref[plane] + wide(in_ref[plane])
    for step, ref in enumerate(out_refs):
        other = plane ^ (step + 1)
        ref[...] = low(keep_ref[other] + wide(in_ref[other]))


def add_plane_kernel(info, keep_ref, in1_ref, in2_ref, in3_ref, own_ref, *out_refs):
    total = lambda z: (
        (keep_ref[z] + wide(in1_ref[z])) + (wide(in2_ref[z]) + wide(in3_ref[z]))
    )
    own_ref[...] = total(info[0])
    for step, ref in enumerate(out_refs):
        ref[...] = low(total(lax.rem(info[0] + step + 1, 4)))


def add_seq_kernel(info, keep_ref, in1_ref, in2_ref, in3_ref, out_ref):
    out_ref[...] = low(
        (keep_ref[...] + wide(in1_ref[...])) + (wide(in2_ref[...]) + wide(in3_ref[...]))
    )


def join_seq_kernel(info, own_ref, in1_ref, in2_ref, in3_ref, out_ref):
    for step, ref in enumerate((own_ref, in1_ref, in2_ref, in3_ref)):
        out_ref[lax.rem(info[0] + 4 - step, 4)] = ref[...]


def join_chips_kernel(info, own_ref, in1_ref, in2_ref, in3_ref, out_ref):
    for step, ref in enumerate((own_ref, in1_ref, in2_ref, in3_ref)):
        out_ref[info[2] ^ step] = ref[...]


class DirectSum:
    def __init__(self, info, send_keep):
        self.info = info
        self.send, self.keep = send_keep
        self.piece = self.send.shape[2:]
        self.stage = 0
        self.next = [swap(self.send, "dp", 1)]

    def step(self):
        piece = tuple(self.piece)
        line = (4, *piece)
        kernel, shapes = [
            (add_core_kernel, [shape_of(line, jnp.float32)] + [shape_of(line)] * 3),
            (add_plane_kernel, [shape_of(piece, jnp.float32)] + [shape_of(piece)] * 3),
            (add_seq_kernel, shape_of(piece)),
            (join_seq_kernel, shape_of(line)),
            (join_chips_kernel, shape_of((4, *line))),
        ][self.stage]
        first = self.keep if self.stage == 0 else self.outs
        if isinstance(first, list | tuple):
            first = first[0]
        outs = run(kernel, kernel.__name__[:-7], self.info, [first, *self.next], shapes)
        self.outs = outs
        sends = outs[1:] if isinstance(outs, list | tuple) else [outs] * 3
        if self.stage in (0, 3):
            self.next = [swap(v, "dp", 2 * k) for k, v in zip((1, 2, 3), sends)]
        elif self.stage in (1, 2):
            self.next = [shift(v, k) for k, v in zip((1, 2, 3), sends)]
        else:
            self.next = [swap(outs, "dp", 1)]
        self.stage += 1


def join_wide_kernel(info, own_ref, in_ref, *out_refs):
    _, parts, count, rows, cols = own_ref.shape
    for ref, core in ((own_ref, info[1]), (in_ref, 1 - info[1])):
        for z in range(parts):
            for k in range(count):
                out_refs[k][core, 0, :, z * cols : (z + 1) * cols] = wide(ref[0, z, k])


def join_wide(info, own, came):
    _, parts, count, rows, cols = own.shape
    piece = pl.BlockSpec((1, parts, count, rows, cols), lambda p: (p, 0, 0, 0, 0))
    outs = run(
        join_wide_kernel,
        "join",
        info,
        [own, came],
        [shape_of((2, 4, rows, parts * cols), jnp.float32)] * count,
        [],
        32,
        (4,),
        [piece] * 2,
        [pl.BlockSpec((2, 1, rows, parts * cols), lambda p: (0, p, 0, 0))] * count,
    )
    return [v.reshape(8 * rows, parts * cols) for v in outs]


def join_attn_kernel(
    info, own_ref, in_ref, query_ref, key_ref, value_ref, out_ref, gains_ref, total
):
    planes, parts, _, rows, cols = own_ref.shape
    for ref, core in ((own_ref, info[1]), (in_ref, 1 - info[1])):
        for p in range(planes):
            for z in range(parts):
                total[core * (planes * parts) + p * parts + z] = wide(ref[p, z, 0])
    at = 0
    features = query_ref.shape[1]
    for ref in (query_ref, key_ref, value_ref, out_ref):
        for piece in range(ref.shape[0] // rows):
            ref[piece * rows : (piece + 1) * rows] = total[at, :, :features]
            if ref is query_ref:
                gains_ref[piece * rows : (piece + 1) * rows] = total[at, :, cols - 128 :]
            at += 1


def cut_kernel(info, values_ref, *refs):
    outs, sems = refs[:-1], refs[-1]
    copies = [
        pltpu.make_async_copy(values_ref.at[lax.rem(info[0] + step + 1, 4)], out, sems.at[step])
        for step, out in enumerate(outs)
    ]
    for copy in copies:
        copy.start()
    for copy in copies:
        copy.wait()


def cut(info, values):
    return run(
        cut_kernel,
        "cut",
        info,
        [values],
        [shape_of(values.shape[1:])] * 3,
        [pltpu.SemaphoreType.DMA((3,))],
        12,
        (1,),
        [ANY],
        [ANY] * 3,
    )


def shift(values, step):
    return lax.ppermute(values, "seq", [(k, (k + step) % 4) for k in range(4)])


def exchange(values):
    return lax.all_to_all(values, "seq", 0, 0)


def local_rows(
    tokens,
    lengths,
    w_query,
    w_key,
    w_value,
    w_out,
    w_gate,
    w_up,
    w_down,
    gain_attn,
    gain_ffn,
    cotangent,
):
    row_count, block_len, model_width = tokens.shape
    kv_width = HK * DH
    dp_at, seq_at = lax.axis_index("dp"), lax.axis_index("seq")
    length = lax.dynamic_slice_in_dim(lengths, seq_at, 1)
    info = jnp.concatenate([jnp.stack([seq_at, dp_at % 2, dp_at // 2]).astype(jnp.int32), length])
    half_dim = DH // 2
    positions = jnp.arange(row_count * block_len, dtype=jnp.float32).reshape(row_count, 1, -1)
    frequency = rope_base ** (-jnp.arange(half_dim, dtype=jnp.float32) / half_dim)
    angles = frequency[None, :, None] * positions
    angles = (jnp.cos(angles), jnp.sin(angles))
    w_heads = jnp.concatenate(
        [
            w_query.T.reshape(HK, GROUP * DH, model_width),
            w_key.T.reshape(HK, DH, model_width),
            w_value.T.reshape(HK, DH, model_width),
        ],
        axis=1,
    )
    w_heads_t = w_heads.reshape(-1, model_width).T
    gains = [
        jnp.broadcast_to(g[:, None], (model_width, block_len // 2)) for g in (gain_attn, gain_ffn)
    ]
    turned = [w_out.T, w_gate.T, w_up.T, w_down.T]

    row = exchange(jnp.swapaxes(tokens, 1, 2))
    cot, info, w_heads, gains, angles, turned, w_down = lax.optimization_barrier(
        (jnp.swapaxes(cotangent, 1, 2), info, w_heads, gains, angles, turned, w_down)
    )
    Order.last = None
    arrived = [shift(part, s + 1) for s, part in enumerate(cut(info, cot))]
    attn_in, queries, keys, values, attended, log_sum = attend(info, row, gains[0], w_heads, *angles)
    mixed, grad, grad_low, attended_grad, gain_ffn_part, *halves = ffn(
        info, row, attended, cot, arrived, gains[1], turned, [w_down, w_gate, w_up, w_out]
    )
    wide_sum = Sum(info, halves, TWO_ROUTES)

    def back(h):
        return attend_back(
            info, h, queries, keys, values, attended, attended_grad, log_sum, angles
        )

    mixed_out = exchange(mixed)
    wide_sum.step()
    qkv_grads = [back(0), back(1), back(2)]
    wide_sum.step()
    tokens_grad, gain_attn_part = tokens_back(info, qkv_grads, row, grad, gains[0], w_heads_t)
    Order.also = (mixed_out,)
    wide_sum.step()
    attn_sum = DirectSum(
        info,
        attn_grad(info, qkv_grads, attn_in, attended, grad_low, gain_attn_part, gain_ffn_part),
    )
    wide_sum.step()
    attn_sum.step()
    wide_sum.step()
    attn_sum.step()
    wide_sum.step()
    attn_sum.step()
    wide_sum.step()
    attn_sum.step()
    wide_sum.step()
    tokens_grad, Order.last = lax.optimization_barrier((tokens_grad, Order.last))
    tokens_out = exchange(tokens_grad)
    attn_sum.step()
    Order.also = (tokens_out,)
    wide_sum.step()
    w_gate_sum, w_up_sum, w_down_sum = join_wide(info, wide_sum.outs, wide_sum.next)
    square = shape_of((model_width, model_width), jnp.float32)
    narrow = shape_of((kv_width, model_width), jnp.float32)
    w_query_sum, w_key_sum, w_value_sum, w_out_sum, gains_sum = run(
        join_attn_kernel,
        "join",
        info,
        [attn_sum.outs, *attn_sum.next],
        [square, narrow, narrow, square, shape_of((model_width, 128), jnp.float32)],
        [pltpu.VMEM((32, PIECE_ROWS, PIECE_COLS), jnp.float32)],
    )
    return (
        jnp.swapaxes(mixed_out, 1, 2),
        jnp.swapaxes(tokens_out, 1, 2),
        w_query_sum,
        w_key_sum.T,
        w_value_sum.T,
        w_out_sum,
        w_gate_sum,
        w_up_sum,
        w_down_sum.T,
        gains_sum[:, 64],
        gains_sum[:, 65],
    )


def solution(mesh):
    whole_rows = mesh.shape["dp"] == 8 and mesh.shape["seq"] == 4
    return jax.shard_map(
        local_rows if whole_rows else local_general,
        mesh=mesh,
        in_specs=(
            P("dp", "seq", None),
            P("dp"),
            P(),
            P(),
            P(),
            P(),
            P(),
            P(),
            P(),
            P(),
            P(),
            P("dp", "seq", None),
        ),
        out_specs=(
            P("dp", "seq", None),
            P("dp", "seq", None),
            P(),
            P(),
            P(),
            P(),
            P(),
            P(),
            P(),
            P(),
            P(),
        ),
        check_vma=False,
    )
```

```python
from functools import partial
import math

import jax
import jax.numpy as jnp
from jax import lax
from jax.experimental import pallas as pl
from jax.experimental.pallas import tpu as pltpu
from jax.sharding import PartitionSpec as P

HQ = 9
HK = 3
DH = 64


eps_norm = 1e-05
rope_base = 100000.0
neg_large = -1e30


def norm_rows(values, gain_vec):
    return (
        values * lax.rsqrt(jnp.mean(values * values, axis=-1, keepdims=True) + eps_norm) * gain_vec
    )


def rotate(values, positions, turn_sign):
    half_dim = values.shape[-1] // 2
    frequency = rope_base ** (-jnp.arange(half_dim, dtype=jnp.float32) / half_dim)
    angles = turn_sign * positions.astype(jnp.float32)[:, None] * frequency[None, :]
    cosine = jnp.cos(angles)[:, None, :]
    sine_part = jnp.sin(angles)[:, None, :]
    first_half = values[..., :half_dim]
    second_half = values[..., half_dim:]
    return jnp.concatenate(
        [
            first_half * cosine - second_half * sine_part,
            second_half * cosine + first_half * sine_part,
        ],
        axis=-1,
    )


def inner_rows(left, right):
    return lax.dot_general(
        left, right, (((0,), (0,)), ((), ())), preferred_element_type=jnp.float32
    )


def times_t(left, right):
    return lax.dot_general(
        left, right, (((1,), (1,)), ((), ())), preferred_element_type=jnp.float32
    )


def fold_piece(block_len, step_fn, carry, pieces):
    piece_count = pieces.shape[1] // block_len

    def inner_step(index_step, state):
        part_piece = lax.dynamic_slice_in_dim(pieces, index_step * block_len, block_len, 1)
        return step_fn(state, part_piece, index_step * block_len)

    return lax.fori_loop(0, piece_count, inner_step, carry)


def local_general(
    tokens,
    lengths,
    w_query,
    w_key,
    w_value,
    w_out,
    w_gate,
    w_up,
    w_down,
    gain_attn,
    gain_ffn,
    cotangent,
):
    row_count, block_len, model_width = tokens.shape
    group_size = HQ // HK
    kv_width = HK * DH
    score_scale = 1.0 / math.sqrt(DH)
    seq_devices = lax.axis_size("seq")
    my_start = lax.axis_index("seq") * block_len
    positions = my_start + jnp.arange(block_len, dtype=jnp.int32)
    longest = jnp.max(lengths)
    live_rows = positions[None, :] < lengths[:, None]
    query_active = my_start < longest
    inputs = tokens.reshape(-1, model_width).astype(jnp.float32)
    attn_norm, attn_pull = jax.vjp(norm_rows, inputs, gain_attn)
    attn_in = attn_norm.astype(jnp.bfloat16)
    query_pre = jnp.dot(attn_in, w_query, preferred_element_type=jnp.float32)
    query_heads = rotate(query_pre.reshape(row_count, block_len, HQ, DH), positions, 1.0).astype(
        jnp.bfloat16
    )
    query_heads = query_heads.reshape(row_count, block_len, HK, group_size, DH)
    key_pre = jnp.dot(attn_in, w_key, preferred_element_type=jnp.float32)
    key_heads = rotate(key_pre.reshape(row_count, block_len, HK, DH), positions, 1.0).astype(
        jnp.bfloat16
    )
    value_heads = jnp.dot(attn_in, w_value, preferred_element_type=jnp.float32).astype(jnp.bfloat16)
    key_value = jnp.concatenate(
        [
            key_heads.reshape(row_count, block_len, kv_width),
            value_heads.reshape(row_count, block_len, kv_width),
        ],
        axis=-1,
    )

    def allowed_for(piece_start):
        key_pos = piece_start + jnp.arange(block_len, dtype=jnp.int32)
        causal = key_pos[None, None, :] <= positions[None, :, None]
        inside = key_pos[None, None, :] < lengths[:, None, None]
        return causal & inside

    def needed_for(piece_start):
        return (piece_start <= my_start) & (piece_start < longest) & query_active

    def split_piece(pieces):
        key_part = pieces[..., :kv_width].reshape(row_count, block_len, HK, DH)
        value_part = pieces[..., kv_width:].reshape(row_count, block_len, HK, DH)
        return (key_part, value_part)

    def forward_block(carry, pieces, piece_start):

        def forward_compute_block(state):
            row_max, row_total, weighted = state
            key_part, value_part = split_piece(pieces)
            scores = (
                jnp.einsum(
                    "rqhgd,rkhd->rhgqk", query_heads, key_part, preferred_element_type=jnp.float32
                )
                * score_scale
            )
            allowed = allowed_for(piece_start)[:, None, None]
            scores = jnp.where(allowed, scores, neg_large)
            new_max = jnp.maximum(row_max, jnp.max(scores, axis=-1))
            shrink = jnp.exp(row_max - new_max)
            exp_scores = jnp.where(allowed, jnp.exp(scores - new_max[..., None]), 0.0)
            row_total = row_total * shrink + jnp.sum(exp_scores, axis=-1)
            update = jnp.einsum(
                "rhgqk,rkhd->rqhgd",
                exp_scores.astype(jnp.bfloat16),
                value_part,
                preferred_element_type=jnp.float32,
            )
            weighted = weighted * jnp.moveaxis(shrink, 3, 1)[..., None] + update
            return (new_max, row_total, weighted)

        return lax.cond(needed_for(piece_start), forward_compute_block, lambda state: state, carry)

    stat_shape = (row_count, HK, group_size, block_len)
    forward_init = (
        jnp.full(stat_shape, neg_large, jnp.float32),
        jnp.zeros(stat_shape, jnp.float32),
        jnp.zeros((row_count, block_len, HK, group_size, DH), jnp.float32),
    )
    forward_state = fold_piece(
        block_len, forward_block, forward_init, lax.all_gather(key_value, "seq", axis=1, tiled=True)
    )
    row_max, row_total, weighted = forward_state
    safe_total = jnp.where(row_total > 0, row_total, 1.0)
    attn_heads = weighted / jnp.moveaxis(safe_total, 3, 1)[..., None]
    attn_heads = jnp.where(live_rows[:, :, None, None, None], attn_heads, 0.0)
    log_sum = jnp.where(live_rows[:, None, None, :], row_max + jnp.log(safe_total), 0.0)
    attn_low = attn_heads.reshape(-1, HQ * DH).astype(jnp.bfloat16)
    residual = inputs + jnp.dot(attn_low, w_out, preferred_element_type=jnp.float32)
    ffn_norm, ffn_pull = jax.vjp(norm_rows, residual, gain_ffn)
    ffn_in = ffn_norm.astype(jnp.bfloat16)
    gate_proj = jnp.dot(ffn_in, w_gate, preferred_element_type=jnp.float32)
    up_proj = jnp.dot(ffn_in, w_up, preferred_element_type=jnp.float32)
    product, swiglu_pull = jax.vjp(
        lambda gate_in, up_in: jax.nn.silu(gate_in) * up_in, gate_proj, up_proj
    )
    hidden = product.astype(jnp.bfloat16)
    branch = jnp.dot(hidden, w_down, preferred_element_type=jnp.float32)
    mixed = (residual + branch).astype(jnp.bfloat16).reshape(row_count, block_len, model_width)
    out_low = cotangent.reshape(-1, model_width)
    out_grad = out_low.astype(jnp.float32)
    w_down_grad = inner_rows(hidden, out_low)
    hidden_grad = times_t(out_low, w_down)
    gate_grad, up_grad = swiglu_pull(hidden_grad)
    gate_low = gate_grad.astype(jnp.bfloat16)
    up_low = up_grad.astype(jnp.bfloat16)
    w_gate_grad = inner_rows(ffn_in, gate_low)
    w_up_grad = inner_rows(ffn_in, up_low)
    ffn_in_grad = times_t(gate_low, w_gate) + times_t(up_low, w_up)
    residual_part, gain_ffn_grad = ffn_pull(ffn_in_grad)
    residual_grad = out_grad + residual_part
    residual_low = residual_grad.astype(jnp.bfloat16)
    w_out_grad = inner_rows(attn_low, residual_low)
    attended_grad = times_t(residual_low, w_out).reshape(row_count, block_len, HK, group_size, DH)
    attended_grad = jnp.where(live_rows[:, :, None, None, None], attended_grad, 0.0).astype(
        jnp.bfloat16
    )
    grad_dot = jnp.moveaxis(jnp.sum(attended_grad.astype(jnp.float32) * attn_heads, axis=-1), 1, 3)

    def backward_block(with_kv, carry, pieces, piece_start):

        def backward_compute_block(state):
            key_part, value_part = split_piece(pieces)
            scores = (
                jnp.einsum(
                    "rqhgd,rkhd->rhgqk", query_heads, key_part, preferred_element_type=jnp.float32
                )
                * score_scale
            )
            allowed = allowed_for(piece_start)[:, None, None]
            weights_now = jnp.where(allowed, jnp.exp(scores - log_sum[..., None]), 0.0)
            weights_grad = jnp.einsum(
                "rqhgd,rkhd->rhgqk", attended_grad, value_part, preferred_element_type=jnp.float32
            )
            score_grad = (weights_now * (weights_grad - grad_dot[..., None])).astype(jnp.bfloat16)
            query_grad = (
                state[0]
                + jnp.einsum(
                    "rhgqk,rkhd->rqhgd", score_grad, key_part, preferred_element_type=jnp.float32
                )
                * score_scale
            )
            kv_grad = state[1]
            values_grad = jnp.einsum(
                "rhgqk,rqhgd->rkhd",
                weights_now.astype(jnp.bfloat16),
                attended_grad,
                preferred_element_type=jnp.float32,
            )
            keys_grad = (
                jnp.einsum(
                    "rhgqk,rqhgd->rkhd", score_grad, query_heads, preferred_element_type=jnp.float32
                )
                * score_scale
            )
            local_kv = jnp.concatenate(
                [
                    keys_grad.reshape(row_count, block_len, kv_width),
                    values_grad.reshape(row_count, block_len, kv_width),
                ],
                axis=-1,
            )
            current = lax.dynamic_slice_in_dim(kv_grad, piece_start, block_len, 1)
            kv_grad = lax.dynamic_update_slice_in_dim(kv_grad, current + local_kv, piece_start, 1)
            return (query_grad, kv_grad)

        return lax.cond(needed_for(piece_start), backward_compute_block, lambda state: state, carry)

    query_zero = jnp.zeros((row_count, block_len, HK, group_size, DH), jnp.float32)
    backward_init = (
        query_zero,
        jnp.zeros((row_count, block_len * seq_devices, 2 * kv_width), jnp.float32),
    )
    step_back = partial(backward_block, True)
    backward_state = fold_piece(
        block_len, step_back, backward_init, lax.all_gather(key_value, "seq", axis=1, tiled=True)
    )
    query_grad = backward_state[0]
    own_kv_grad = lax.psum_scatter(
        backward_state[1].astype(jnp.bfloat16), "seq", scatter_dimension=1, tiled=True
    ).astype(jnp.float32)
    query_low = (
        rotate(query_grad.reshape(row_count, block_len, HQ, DH), positions, -1.0)
        .astype(jnp.bfloat16)
        .reshape(-1, HQ * DH)
    )
    key_low = (
        rotate(own_kv_grad[..., :kv_width].reshape(row_count, block_len, HK, DH), positions, -1.0)
        .astype(jnp.bfloat16)
        .reshape(-1, kv_width)
    )
    value_low = own_kv_grad[..., kv_width:].astype(jnp.bfloat16).reshape(-1, kv_width)
    w_query_grad = inner_rows(attn_in, query_low)
    w_key_grad = inner_rows(attn_in, key_low)
    w_value_grad = inner_rows(attn_in, value_low)
    attn_in_grad = (
        times_t(query_low, w_query) + times_t(key_low, w_key) + times_t(value_low, w_value)
    )
    inputs_part, gain_attn_grad = attn_pull(attn_in_grad)
    tokens_grad = (
        (residual_grad + inputs_part)
        .astype(jnp.bfloat16)
        .reshape(row_count, block_len, model_width)
    )
    (
        w_query_grad,
        w_key_grad,
        w_value_grad,
        w_out_grad,
        w_gate_grad,
        w_up_grad,
        w_down_grad,
        gain_attn_grad,
        gain_ffn_grad,
    ) = lax.psum(
        (
            w_query_grad,
            w_key_grad,
            w_value_grad,
            w_out_grad,
            w_gate_grad,
            w_up_grad,
            w_down_grad,
            gain_attn_grad,
            gain_ffn_grad,
        ),
        ("dp", "seq"),
    )
    return (
        mixed,
        tokens_grad,
        w_query_grad,
        w_key_grad,
        w_value_grad,
        w_out_grad,
        w_gate_grad,
        w_up_grad,
        w_down_grad,
        gain_attn_grad,
        gain_ffn_grad,
    )


GROUP = HQ // HK
HEAD_ROWS = (GROUP + 2) * DH
SCALE = DH**-0.5
FULL = pl.BlockSpec(memory_space=pltpu.VMEM)
SMEM = pl.BlockSpec(memory_space=pltpu.SMEM)
ANY = pl.BlockSpec(memory_space=pl.ANY)


def shape_of(shape, dtype=jnp.bfloat16):
    return jax.ShapeDtypeStruct(shape, dtype)


def low(values):
    return values.astype(jnp.bfloat16)


def wide(values):
    return values.astype(jnp.float32)


def mul_nt(left, right):
    return lax.dot_general(
        left, right, (((1,), (1,)), ((), ())), preferred_element_type=jnp.float32
    )


def mul_nn(left, right):
    return lax.dot_general(
        left, right, (((1,), (0,)), ((), ())), preferred_element_type=jnp.float32
    )


class Order:
    last = None
    also = ()
    windows = False


def run(
    kernel, name, info, operands, out_shapes, scratch=(), vmem=12, grid=(), in_specs=None, out_specs=None
):
    after = [*([] if Order.last is None else [Order.last]), *Order.also]
    Order.also = ()
    taken = len(operands)

    def body(*refs):
        kernel(*refs[: 1 + taken], *refs[1 + taken + len(after) :])

    many = isinstance(out_shapes, list)
    if Order.windows and not grid:
        grid, vmem = (1,), 60
        in_specs = [once(*v.shape) for v in operands]
        out_specs = [once(*v.shape) for v in out_shapes] if many else once(*out_shapes.shape)
    outs = pl.pallas_call(
        body,
        grid=grid,
        in_specs=[SMEM] + (in_specs or [FULL] * taken) + [ANY] * len(after),
        out_specs=out_specs or ([FULL] * len(out_shapes) if many else FULL),
        scratch_shapes=list(scratch),
        out_shape=out_shapes,
        compiler_params=pltpu.CompilerParams(vmem_limit_bytes=vmem * 2**20),
        cost_estimate=pl.CostEstimate(flops=1000, bytes_accessed=1000, transcendentals=0),
        name=name,
    )(info, *operands, *after)
    Order.last = min(outs, key=lambda v: v.size) if many else outs
    return outs


def whole(*shape):
    return pl.BlockSpec(shape, lambda b: (0,) * len(shape))


def once(*shape):
    return pl.BlockSpec(shape, lambda b: (0,) * len(shape), pipeline_mode=pl.Buffered(1))


def at_block(*shape):
    return pl.BlockSpec((1, *shape), lambda b: (b, *[0] * len(shape)))


def turn(values, cosine, sine_part):
    first_half, second_half = values[: DH // 2], values[DH // 2 :]
    return jnp.concatenate(
        [
            first_half * cosine - second_half * sine_part,
            second_half * cosine + first_half * sine_part,
        ],
        axis=0,
    )


def inverse_rms(values):
    mean = jnp.sum(values * values, axis=0, keepdims=True) * (1.0 / values.shape[0])
    return lax.rsqrt(mean + eps_norm)


def norm_back(values, grad, gain):
    scale = inverse_rms(values)
    turned = grad * gain
    inner = jnp.sum(turned * values, axis=0, keepdims=True) * (1.0 / values.shape[0])
    part = scale * turned - values * (scale * scale * scale * inner)
    return part, grad * values * scale


def gain_of(ref):
    return jnp.concatenate([ref[...], ref[...]], axis=1)


def causal_mask(width):
    key_at = lax.broadcasted_iota(jnp.int32, (width, width), 0)
    query_at = lax.broadcasted_iota(jnp.int32, (width, width), 1)
    return jnp.concatenate([key_at <= query_at] * GROUP, axis=1)


def heads_of(values):
    return jnp.concatenate([values[j * DH : (j + 1) * DH] for j in range(GROUP)], axis=1)


def attend_kernel(
    info,
    row_ref,
    gain_ref,
    weights_ref,
    cos_ref,
    sin_ref,
    attn_in_ref,
    query_ref,
    key_ref,
    value_ref,
    out_ref,
    lse_ref,
    key_rows,
):
    blocks, _, width = row_ref.shape

    @pl.when(pl.program_id(0) == 0)
    def _():
        gain = gain_of(gain_ref)
        for b in range(blocks):
            values = wide(row_ref[b])
            attn_in_ref[b] = low(values * inverse_rms(values) * gain)

    mask = causal_mask(width)
    for b in range(blocks):
        pre = mul_nn(weights_ref[0], attn_in_ref[b])
        cosine, sine_part = cos_ref[b], sin_ref[b]
        for j in range(GROUP):
            query_ref[0, b, j * DH : (j + 1) * DH] = low(
                turn(pre[j * DH : (j + 1) * DH], cosine, sine_part) * SCALE
            )
        keys = low(turn(pre[GROUP * DH : (GROUP + 1) * DH], cosine, sine_part))
        key_ref[0, b] = keys
        key_rows[b] = keys.T
        value_ref[0, b] = low(pre[(GROUP + 1) * DH :])
    for b in range(blocks):
        queries = heads_of(query_ref[0, b])
        scores, top = [], None
        for k in range(b + 1):
            part = mul_nn(key_rows[k], queries)
            if k == b:
                part = jnp.where(mask, part, neg_large)
            scores.append(part)
            part_top = jnp.max(part, axis=0, keepdims=True)
            top = part_top if top is None else jnp.maximum(top, part_top)
        total, weighted = 0.0, 0.0
        for k in range(b + 1):
            weights_now = jnp.exp(scores[k] - top)
            total = total + jnp.sum(weights_now, axis=0, keepdims=True)
            weighted = weighted + mul_nn(value_ref[0, k], low(weights_now))
        weighted = weighted * (1.0 / total)
        log_sum = top + jnp.log(total)
        live = b * width + lax.broadcasted_iota(jnp.int32, (1, width), 1) < info[3]
        for j in range(GROUP):
            mine = slice(j * width, (j + 1) * width)
            out_ref[0, b, j * DH : (j + 1) * DH] = low(jnp.where(live, weighted[:, mine], 0.0))
            lse_ref[0, b, j : j + 1] = log_sum[:, mine]


def attend(info, row, gain, w_heads, cosine, sine_part):
    blocks, features, width = row.shape
    head = lambda rows: pl.BlockSpec((1, blocks, rows, width), lambda h: (h, 0, 0, 0))
    return run(
        attend_kernel,
        "attend",
        info,
        [row, gain, w_heads, cosine, sine_part],
        [
            shape_of((blocks, features, width)),
            shape_of((HK, blocks, GROUP * DH, width)),
            shape_of((HK, blocks, DH, width)),
            shape_of((HK, blocks, DH, width)),
            shape_of((HK, blocks, GROUP * DH, width)),
            shape_of((HK, blocks, 8, width), jnp.float32),
        ],
        [pltpu.VMEM((blocks, width, DH), jnp.bfloat16)],
        60,
        (HK,),
        [
            whole(*row.shape),
            whole(*gain.shape),
            pl.BlockSpec((1, HEAD_ROWS, features), lambda h: (h, 0, 0)),
            whole(*cosine.shape),
            whole(*cosine.shape),
        ],
        [whole(*row.shape), *[head(rows) for rows in (GROUP * DH, DH, DH, GROUP * DH, 8)]],
    )


def lanes_of(ref, rows=slice(None)):
    return jnp.concatenate([ref[b, rows] for b in range(ref.shape[0])], axis=1)


def put_grad(values, ref, at):
    planes, parts, _, rows, cols = ref.shape
    for p in range(planes):
        for z in range(parts):
            ref[p, z, at] = values[p * rows : (p + 1) * rows, z * cols : (z + 1) * cols].astype(
                ref.dtype
            )


CHUNK = 768


def ffn_kernel(
    info,
    row_ref,
    att_ref,
    cot_ref,
    in1_ref,
    in2_ref,
    in3_ref,
    gain_ref,
    w_out_t_ref,
    w_gate_t_ref,
    w_up_t_ref,
    w_down_t_ref,
    w_down_ref,
    w_gate_ref,
    w_up_ref,
    w_out_ref,
    mixed_ref,
    grad_ref,
    low_ref,
    att_grad_ref,
    gain_grad_ref,
    send_ref,
    keep_ref,
    ffn_ins,
    cots,
    hiddens,
    gates,
    ups,
):
    b = pl.program_id(0)
    width = row_ref.shape[2]
    gain = gain_of(gain_ref)
    attended = jnp.concatenate([att_ref[h, 0] for h in range(HK)], axis=0)
    residual = wide(row_ref[0]) + mul_nn(w_out_t_ref[...], attended)
    ffn_in = low(residual * inverse_rms(residual) * gain)
    ffn_ins[b] = ffn_in
    from_step = lax.rem(info[0] + 4 - b, 4)

    @pl.when(from_step == 0)
    def _():
        cots[b] = cot_ref[b]

    for step, ref in ((1, in1_ref), (2, in2_ref), (3, in3_ref)):

        @pl.when(from_step == step)
        def _():
            cots[b] = ref[...]

    cot = cots[b]
    mixed, ffn_in_grad = residual, 0.0
    for at in range(0, hiddens.shape[1], CHUNK):
        part = slice(at, at + CHUNK)
        gate = mul_nn(w_gate_t_ref[part], ffn_in)
        up = mul_nn(w_up_t_ref[part], ffn_in)
        hidden_grad = mul_nn(w_down_ref[part], cot)
        sigmoid = 1.0 / (1.0 + jnp.exp(-gate))
        silu = gate * sigmoid
        hidden = low(silu * up)
        gate_grad = low(hidden_grad * up * (sigmoid + silu * (1.0 - sigmoid)))
        up_grad = low(hidden_grad * silu)
        hiddens[b, part] = hidden
        gates[b, part] = gate_grad
        ups[b, part] = up_grad
        mixed = mixed + mul_nn(w_down_t_ref[:, part], hidden)
        ffn_in_grad = ffn_in_grad + (
            mul_nn(w_gate_ref[:, part], gate_grad) + mul_nn(w_up_ref[:, part], up_grad)
        )
    mixed_ref[0] = low(mixed)
    part, gain_terms = norm_back(residual, ffn_in_grad, gain)
    gain_terms = gain_terms[:, : width // 2] + gain_terms[:, width // 2 :]

    @pl.when(b == 0)
    def _():
        gain_grad_ref[...] = gain_terms

    @pl.when(b > 0)
    def _():
        gain_grad_ref[...] += gain_terms

    grad = wide(cot) + part
    grad_ref[0] = grad
    grad_low = low(grad)
    low_ref[0] = grad_low
    live = b * width + lax.broadcasted_iota(jnp.int32, (1, width), 1) < info[3]
    att_grad_ref[0] = low(jnp.where(live, mul_nn(w_out_ref[...], grad_low), 0.0))

    @pl.when(b == pl.num_programs(0) - 1)
    def _():
        rows = grad_ref.shape[1] // 2
        for half, ref in ((1 - info[1], send_ref), (info[1], keep_ref)):
            own = pl.ds(pl.multiple_of(half * rows, 16), rows)
            left = lanes_of(ffn_ins, own)
            put_grad(mul_nt(left, lanes_of(gates)), ref, 0)
            put_grad(mul_nt(left, lanes_of(ups)), ref, 1)
            put_grad(mul_nt(lanes_of(cots, own), lanes_of(hiddens)), ref, 2)


def ffn(info, row, attended, cot, arrived, gain, turned, straight):
    blocks, features, width = row.shape
    hidden = turned[1].shape[0]
    block, long = (blocks, features, width), (blocks, hidden, width)
    pieces = (4, 4, 3, features // 8, hidden // 4)
    return run(
        ffn_kernel,
        "ffn",
        info,
        [row, attended, cot, *arrived, gain, *turned, *straight],
        [
            shape_of(block),
            shape_of(block, jnp.float32),
            shape_of(block),
            shape_of(block),
            shape_of(gain.shape, jnp.float32),
            shape_of(pieces),
            shape_of(pieces),
        ],
        [pltpu.VMEM(block, jnp.bfloat16)] * 2 + [pltpu.VMEM(long, jnp.bfloat16)] * 3,
        52,
        (blocks,),
        [
            at_block(features, width),
            pl.BlockSpec((HK, 1, GROUP * DH, width), lambda b: (0, b, 0, 0)),
            whole(*cot.shape),
            *[whole(features, width)] * 3,
            whole(*gain.shape),
            *[FULL] * 8,
        ],
        [
            *[at_block(features, width)] * 4,
            whole(*gain.shape),
            *[whole(*pieces)] * 2,
        ],
    )


PIECE_ROWS = 48
PIECE_COLS = 640


def attend_back(refs, grad_ref, scratch):
    query_ref, key_ref, value_ref, out_ref, out_grad_ref, lse_ref, cos_ref, sin_ref = refs
    key_rows, value_rows, key_sum, value_sum = scratch
    blocks, width = query_ref.shape[1], query_ref.shape[3]
    for b in range(blocks):
        key_rows[b] = key_ref[0, b].T
        value_rows[b] = value_ref[0, b].T
    mask = causal_mask(width)
    for b in reversed(range(blocks)):
        queries, out_grad = heads_of(query_ref[0, b]), heads_of(out_grad_ref[b])
        grad_dot = jnp.sum(wide(out_grad) * wide(heads_of(out_ref[0, b])), axis=0, keepdims=True)
        log_sum = jnp.concatenate([lse_ref[0, b, j : j + 1] for j in range(GROUP)], axis=1)
        query_grad = 0.0
        for k in range(b + 1):
            weights_now = jnp.exp(mul_nn(key_rows[k], queries) - log_sum)
            if k == b:
                weights_now = jnp.where(mask, weights_now, 0.0)
            weights_grad = mul_nn(value_rows[k], out_grad)
            score_grad = low(weights_now * (weights_grad - grad_dot))
            value_part = mul_nt(out_grad, low(weights_now))
            key_part = mul_nt(queries, score_grad)
            if b == blocks - 1:
                value_sum[k] = value_part
                key_sum[k] = key_part
            else:
                value_sum[k] += value_part
                key_sum[k] += key_part
            query_grad = query_grad + mul_nn(key_ref[0, k], score_grad)
        cosine, sine_part = cos_ref[b], -sin_ref[b]
        for j in range(GROUP):
            grad_ref[b, j * DH : (j + 1) * DH] = low(
                turn(query_grad[:, j * width : (j + 1) * width], cosine * SCALE, sine_part * SCALE)
            )
        grad_ref[b, GROUP * DH : (GROUP + 1) * DH] = low(turn(key_sum[b], cosine, sine_part))
        grad_ref[b, (GROUP + 1) * DH :] = low(value_sum[b])


def back_kernel(info, *refs):
    heads, refs = refs[:8], refs[8:]
    (gain_ref, gain_ffn_ref), far, refs = refs[:2], refs[2:8], refs[8:]
    (out_ref, send_ref, keep_ref), refs = refs[:3], refs[3:]
    qkv_ref, gain_sum, scratch, near, sems = refs[0], refs[1], refs[2:6], refs[6:12], refs[12]
    row_ref, grad_ref, w_ref, attn_in_ref, att_ref, low_ref = near
    h = pl.program_id(0)
    copies = [
        pltpu.make_async_copy(there, here, sems.at[k])
        for k, (there, here) in enumerate(zip(far, near))
    ]

    @pl.when(h == 0)
    def _():
        for copy in copies:
            copy.start()

    attend_back(heads, qkv_ref.at[h], scratch)

    @pl.when(h == HK - 1)
    def _():
        for copy in copies:
            copy.wait()
        tokens_back(row_ref, grad_ref, gain_ref, w_ref, qkv_ref, out_ref, gain_sum)
        first = lambda ref: attn_grad_first(qkv_ref, attn_in_ref, gain_sum, gain_ffn_ref, ref)
        second = lambda ref: attn_grad_second(qkv_ref, attn_in_ref, att_ref, low_ref, ref)

        @pl.when(info[1] == 0)
        def _():
            second(send_ref)
            first(keep_ref)

        @pl.when(info[1] == 1)
        def _():
            first(send_ref)
            second(keep_ref)


def tokens_back(row_ref, grad_ref, gain_ref, w_ref, qkv_ref, out_ref, gain_sum):
    width = row_ref.shape[2]
    gain = gain_of(gain_ref)
    gain_sum[...] = jnp.zeros_like(gain_sum)

    def one_block(b, carry):
        qkv = jnp.concatenate([qkv_ref[h, b] for h in range(HK)], axis=0)
        part, gain_terms = norm_back(wide(row_ref[b]), mul_nn(w_ref[...], qkv), gain)
        gain_sum[...] += gain_terms[:, : width // 2] + gain_terms[:, width // 2 :]
        out_ref[b] = low(grad_ref[b] + part)
        return carry

    lax.fori_loop(0, row_ref.shape[0], one_block, 0)


def put_rows(values, ref, at, columns=None):
    features = values.shape[1]
    if columns is None:
        columns = jnp.zeros((values.shape[0], PIECE_COLS - features), jnp.float32)
    for piece in range(values.shape[0] // PIECE_ROWS):
        rows = slice(piece * PIECE_ROWS, (piece + 1) * PIECE_ROWS)
        p, z = (at + piece) // 4, (at + piece) % 4
        ref[p, z, 0, :, :features] = values[rows].astype(ref.dtype)
        ref[p, z, 0, :, features:] = columns[rows].astype(ref.dtype)


def take_rows(qkv_ref, start, size):
    rows = slice(start, start + size)
    return jnp.concatenate([lanes_of(qkv_ref.at[h], rows) for h in range(HK)], axis=0)


def attn_grad_first(qkv_ref, attn_in_ref, gain1_ref, gain2_ref, ref):
    attn_in = lanes_of(attn_in_ref)
    features = attn_in.shape[0]
    lane = lax.broadcasted_iota(jnp.int32, (features, PIECE_COLS - features), 1)
    gains = jnp.where(
        lane == 0,
        jnp.sum(gain1_ref[...], axis=1, keepdims=True),
        jnp.where(lane == 1, jnp.sum(gain2_ref[...], axis=1, keepdims=True), 0.0),
    )
    put_rows(mul_nt(attn_in, take_rows(qkv_ref, 0, GROUP * DH)), ref, 0, gains)
    keys = take_rows(qkv_ref, GROUP * DH, DH)
    put_rows(mul_nt(keys, attn_in), ref, features // PIECE_ROWS)


def attn_grad_second(qkv_ref, attn_in_ref, att_ref, low_ref, ref):
    values = take_rows(qkv_ref, (GROUP + 1) * DH, DH)
    put_rows(mul_nt(values, lanes_of(attn_in_ref)), ref, 0)
    attended = jnp.concatenate([lanes_of(att_ref.at[h]) for h in range(HK)], axis=0)
    put_rows(mul_nt(attended, lanes_of(low_ref)), ref, HK * DH // PIECE_ROWS)


def back(info, heads, attended_grad, log_sum, angles, gains, rest):
    queries, keys, values, attended = heads
    row = rest[0]
    _, blocks, _, width = queries.shape
    head = lambda rows: pl.BlockSpec((1, blocks, rows, width), lambda h: (h, 0, 0, 0))
    angle = once(*angles[0].shape)
    pieces = (4, 4, 1, PIECE_ROWS, PIECE_COLS)
    return run(
        back_kernel,
        "back",
        info,
        [queries, keys, values, attended, attended_grad, log_sum, *angles, *gains, *rest],
        [shape_of(row.shape), shape_of(pieces), shape_of(pieces)],
        [
            pltpu.VMEM((HK, blocks, HEAD_ROWS, width), jnp.bfloat16),
            pltpu.VMEM(gains[0].shape, jnp.float32),
        ]
        + [pltpu.VMEM((blocks, width, DH), jnp.bfloat16)] * 2
        + [pltpu.VMEM((blocks, DH, width), jnp.float32)] * 2
        + [pltpu.VMEM(v.shape, v.dtype) for v in rest]
        + [pltpu.SemaphoreType.DMA((6,))],
        60,
        (HK,),
        [
            *[head(rows) for rows in (GROUP * DH, DH, DH, GROUP * DH)],
            pl.BlockSpec((blocks, GROUP * DH, width), lambda h: (0, h, 0)),
            head(8),
            angle,
            angle,
            *[once(*g.shape) for g in gains],
            *[ANY] * 6,
        ],
        [whole(*row.shape), whole(*pieces), whole(*pieces)],
    )


def bit_of(value, bit):
    return lax.rem(value // (1 << bit), 2)


def plane_at(first, own, other):
    return own + 2 * other if first == 0 else other + 2 * own


def spot(routes, near, far):
    if len(routes) == 1:
        return 0, near + 2 * far
    return far, near


def split_plane_kernel(routes, info, keep_ref, in_ref, *outs):
    for k, (first, places) in enumerate(routes):
        mine = bit_of(info[2], first)
        send_ref, own_ref = outs[2 * k : 2 * k + 2]
        for t in range(2):
            there, here = plane_at(first, 1 - mine, t), plane_at(first, mine, t)
            for at, z in enumerate(places):
                send_ref[t, at] = low(wide(keep_ref[there, z]) + wide(in_ref[there, z]))
                own_ref[t, at] = wide(keep_ref[here, z]) + wide(in_ref[here, z])


def split_line_kernel(routes, info, *refs):
    count = len(routes)
    ins, outs = refs[: 2 * count], refs[2 * count :]
    for k, (first, _) in enumerate(routes):
        mine = bit_of(info[2], 1 - first)
        keep_ref, in_ref = ins[2 * k : 2 * k + 2]
        send_ref, own_ref = outs[2 * k : 2 * k + 2]
        send_ref[...] = low(keep_ref[1 - mine] + wide(in_ref[1 - mine]))
        own_ref[...] = keep_ref[mine] + wide(in_ref[mine])


def split_near_kernel(routes, info, *refs):
    ins, (send_ref, own_ref) = refs[:-2], refs[-2:]
    near = bit_of(info[0], 0)
    for far in range(2):
        k, there = spot(routes, 1 - near, far)
        k, here = spot(routes, near, far)
        keep_ref, in_ref = ins[2 * k : 2 * k + 2]
        send_ref[far] = low(keep_ref[there] + wide(in_ref[there]))
        own_ref[far] = keep_ref[here] + wide(in_ref[here])


def split_far_kernel(routes, info, keep_ref, in_ref, send_ref, own_ref):
    far = bit_of(info[0], 1)
    send_ref[...] = low(keep_ref[1 - far] + wide(in_ref[1 - far]))
    own_ref[...] = keep_ref[far] + wide(in_ref[far])


def total_kernel(routes, info, keep_ref, in_ref, out_ref):
    out_ref[...] = low(keep_ref[...] + wide(in_ref[...]))


def join_far_kernel(routes, info, own_ref, in_ref, out_ref):
    far = bit_of(info[0], 1)
    out_ref[far] = own_ref[...]
    out_ref[1 - far] = in_ref[...]


def join_near_kernel(routes, info, own_ref, in_ref, *outs):
    near = bit_of(info[0], 0)
    for far in range(2):
        k, here = spot(routes, near, far)
        k, there = spot(routes, 1 - near, far)
        outs[k][here] = own_ref[far]
        outs[k][there] = in_ref[far]


def join_line_kernel(routes, info, *refs):
    count = len(routes)
    ins, outs = refs[: 2 * count], refs[2 * count :]
    for k, (first, _) in enumerate(routes):
        mine = bit_of(info[2], 1 - first)
        outs[k][mine] = ins[2 * k][...]
        outs[k][1 - mine] = ins[2 * k + 1][...]


def join_plane_kernel(routes, info, *refs):
    ins, out_ref = refs[:-1], refs[-1]
    for k, (first, places) in enumerate(routes):
        mine = bit_of(info[2], first)
        own_ref, in_ref = ins[2 * k : 2 * k + 2]
        for t in range(2):
            for at, z in enumerate(places):
                out_ref[plane_at(first, mine, t), z] = own_ref[t, at]
                out_ref[plane_at(first, 1 - mine, t), z] = in_ref[t, at]


def swap(values, axis, bits):
    count = 8 if axis == "dp" else 4
    return lax.ppermute(values, axis, [(k, k ^ bits) for k in range(count)])


TWO_ROUTES = ((0, (0, 1)), (1, (2, 3)))


class Sum:
    def __init__(self, info, send_keep, routes):
        self.info, self.routes = info, routes
        self.send, self.keep = send_keep
        self.piece = self.send.shape[2:]
        self.stage = 0
        self.next = swap(self.send, "dp", 1)

    def call(self, kernel, operands, shapes):
        return run(partial(kernel, self.routes), kernel.__name__[:-7], self.info, operands, shapes)

    def step(self):
        routes, piece = self.routes, tuple(self.piece)
        count, places = len(routes), len(routes[0][1])
        both = lambda *shape: [shape_of(shape), shape_of(shape, jnp.float32)]
        plane = [2 << first for first, _ in routes]
        line = [2 << (1 - first) for first, _ in routes]
        if self.stage == 0:
            self.outs = self.call(
                split_plane_kernel, [self.keep, self.next], both(2, places, *piece) * count
            )
            self.next = [swap(self.outs[2 * k], "dp", plane[k]) for k in range(count)]
        elif self.stage in (1, 2):
            operands = []
            for k in range(count):
                operands += [self.outs[2 * k + 1], self.next[k]]
            if self.stage == 1:
                self.outs = self.call(split_line_kernel, operands, both(places, *piece) * count)
                self.next = [swap(self.outs[2 * k], "dp", line[k]) for k in range(count)]
            else:
                self.outs = self.call(split_near_kernel, operands, both(2, *piece))
                self.next = swap(self.outs[0], "seq", 1)
        elif self.stage == 3:
            self.outs = self.call(split_far_kernel, [self.outs[1], self.next], both(*piece))
            self.next = swap(self.outs[0], "seq", 2)
        elif self.stage == 4:
            self.outs = self.call(total_kernel, [self.outs[1], self.next], shape_of(piece))
            self.next = swap(self.outs, "seq", 2)
        elif self.stage == 5:
            self.outs = self.call(join_far_kernel, [self.outs, self.next], shape_of((2, *piece)))
            self.next = swap(self.outs, "seq", 1)
        elif self.stage == 6:
            self.outs = self.call(
                join_near_kernel, [self.outs, self.next], [shape_of((places, *piece))] * count
            )
            self.next = [swap(self.outs[k], "dp", line[k]) for k in range(count)]
        elif self.stage in (7, 8):
            operands = []
            for k in range(count):
                operands += [self.outs[k], self.next[k]]
            if self.stage == 7:
                self.outs = self.call(
                    join_line_kernel, operands, [shape_of((2, places, *piece))] * count
                )
                self.next = [swap(self.outs[k], "dp", plane[k]) for k in range(count)]
            else:
                self.outs = self.call(join_plane_kernel, operands, shape_of((4, 4, *piece)))
                self.next = swap(self.outs, "dp", 1)
        self.stage += 1


def add_core_kernel(info, keep_ref, in_ref, own_ref, *out_refs):
    plane = info[2]
    own_ref[...] = wide(keep_ref[plane]) + wide(in_ref[plane])
    for step, ref in enumerate(out_refs):
        other = plane ^ (step + 1)
        ref[...] = low(wide(keep_ref[other]) + wide(in_ref[other]))


def add_plane_kernel(info, keep_ref, in1_ref, in2_ref, in3_ref, own_ref, *out_refs):
    total = lambda z: (
        (keep_ref[z] + wide(in1_ref[z])) + (wide(in2_ref[z]) + wide(in3_ref[z]))
    )
    own_ref[...] = total(info[0])
    for step, ref in enumerate(out_refs):
        ref[...] = low(total(lax.rem(info[0] + step + 1, 4)))


def add_seq_kernel(info, keep_ref, in1_ref, in2_ref, in3_ref, out_ref):
    out_ref[...] = low(
        (keep_ref[...] + wide(in1_ref[...])) + (wide(in2_ref[...]) + wide(in3_ref[...]))
    )


def join_seq_kernel(info, own_ref, in1_ref, in2_ref, in3_ref, out_ref):
    for step, ref in enumerate((own_ref, in1_ref, in2_ref, in3_ref)):
        out_ref[lax.rem(info[0] + 4 - step, 4)] = ref[...]


def join_chips_kernel(info, own_ref, in1_ref, in2_ref, in3_ref, out_ref):
    for step, ref in enumerate((own_ref, in1_ref, in2_ref, in3_ref)):
        out_ref[info[2] ^ step] = ref[...]


class DirectSum:
    def __init__(self, info, send_keep):
        self.info = info
        self.send, self.keep = send_keep
        self.piece = self.send.shape[2:]
        self.stage = 0
        self.next = [swap(self.send, "dp", 1)]

    def step(self):
        piece = tuple(self.piece)
        line = (4, *piece)
        kernel, shapes = [
            (add_core_kernel, [shape_of(line, jnp.float32)] + [shape_of(line)] * 3),
            (add_plane_kernel, [shape_of(piece, jnp.float32)] + [shape_of(piece)] * 3),
            (add_seq_kernel, shape_of(piece)),
            (join_seq_kernel, shape_of(line)),
            (join_chips_kernel, shape_of((4, *line))),
        ][self.stage]
        first = self.keep if self.stage == 0 else self.outs
        if isinstance(first, list | tuple):
            first = first[0]
        outs = run(kernel, kernel.__name__[:-7], self.info, [first, *self.next], shapes)
        self.outs = outs
        sends = outs[1:] if isinstance(outs, list | tuple) else [outs] * 3
        if self.stage in (0, 3):
            self.next = [swap(v, "dp", 2 * k) for k, v in zip((1, 2, 3), sends)]
        elif self.stage in (1, 2):
            self.next = [shift(v, k) for k, v in zip((1, 2, 3), sends)]
        else:
            self.next = [swap(outs, "dp", 1)]
        self.stage += 1


def join_wide_kernel(info, own_ref, in_ref, *out_refs):
    _, parts, count, rows, cols = own_ref.shape
    for ref, core in ((own_ref, info[1]), (in_ref, 1 - info[1])):
        for z in range(parts):
            for k in range(count):
                out_refs[k][core, 0, :, z * cols : (z + 1) * cols] = wide(ref[0, z, k])


def join_wide(info, own, came):
    _, parts, count, rows, cols = own.shape
    piece = pl.BlockSpec((1, parts, count, rows, cols), lambda p: (p, 0, 0, 0, 0))
    outs = run(
        join_wide_kernel,
        "join",
        info,
        [own, came],
        [shape_of((2, 4, rows, parts * cols), jnp.float32)] * count,
        [],
        16,
        (4,),
        [piece] * 2,
        [pl.BlockSpec((2, 1, rows, parts * cols), lambda p: (0, p, 0, 0))] * count,
    )
    return [v.reshape(8 * rows, parts * cols) for v in outs]


def join_attn_kernel(
    info, own_ref, in_ref, query_ref, key_ref, value_ref, out_ref, gains_ref, total
):
    planes, parts, _, rows, cols = own_ref.shape
    for ref, core in ((own_ref, info[1]), (in_ref, 1 - info[1])):
        for p in range(planes):
            for z in range(parts):
                total[core * (planes * parts) + p * parts + z] = wide(ref[p, z, 0])
    at = 0
    features = query_ref.shape[1]
    for ref in (query_ref, key_ref, value_ref, out_ref):
        for piece in range(ref.shape[0] // rows):
            ref[piece * rows : (piece + 1) * rows] = total[at, :, :features]
            if ref is query_ref:
                gains_ref[piece * rows : (piece + 1) * rows] = total[at, :, cols - 128 :]
            at += 1


def cut_kernel(info, values_ref, *refs):
    outs, sems = refs[:-1], refs[-1]
    copies = [
        pltpu.make_async_copy(values_ref.at[lax.rem(info[0] + step + 1, 4)], out, sems.at[step])
        for step, out in enumerate(outs)
    ]
    for copy in copies:
        copy.start()
    for copy in copies:
        copy.wait()


def cut(info, values):
    return run(
        cut_kernel,
        "cut",
        info,
        [values],
        [shape_of(values.shape[1:])] * 3,
        [pltpu.SemaphoreType.DMA((3,))],
        12,
        (1,),
        [ANY],
        [ANY] * 3,
    )


def shift(values, step):
    return lax.ppermute(values, "seq", [(k, (k + step) % 4) for k in range(4)])


def place_kernel(info, in_ref, out_ref):
    out_ref[...] = in_ref[...]


def place(info, values):
    return run(place_kernel, "place", info, [values], shape_of(values.shape))


def exchange(values):
    return lax.all_to_all(values, "seq", 0, 0)


def local_rows(
    tokens,
    lengths,
    w_query,
    w_key,
    w_value,
    w_out,
    w_gate,
    w_up,
    w_down,
    gain_attn,
    gain_ffn,
    cotangent,
):
    row_count, block_len, model_width = tokens.shape
    kv_width = HK * DH
    dp_at, seq_at = lax.axis_index("dp"), lax.axis_index("seq")
    length = lax.dynamic_slice_in_dim(lengths, seq_at, 1)
    info = jnp.concatenate([jnp.stack([seq_at, dp_at % 2, dp_at // 2]).astype(jnp.int32), length])
    half_dim = DH // 2
    positions = jnp.arange(row_count * block_len, dtype=jnp.float32).reshape(row_count, 1, -1)
    frequency = rope_base ** (-jnp.arange(half_dim, dtype=jnp.float32) / half_dim)
    angles = frequency[None, :, None] * positions
    angles = (jnp.cos(angles), jnp.sin(angles))
    w_heads = jnp.concatenate(
        [
            w_query.T.reshape(HK, GROUP * DH, model_width),
            w_key.T.reshape(HK, DH, model_width),
            w_value.T.reshape(HK, DH, model_width),
        ],
        axis=1,
    )
    w_heads_t = w_heads.reshape(-1, model_width).T
    gains = [
        jnp.broadcast_to(g[:, None], (model_width, block_len // 2)) for g in (gain_attn, gain_ffn)
    ]
    turned = [w_out.T, w_gate.T, w_up.T, w_down.T]

    row = exchange(jnp.swapaxes(tokens, 1, 2))
    cot, info, w_heads, w_heads_t, gains, angles, turned, w_down = lax.optimization_barrier(
        (
            jnp.swapaxes(cotangent, 1, 2),
            info,
            w_heads,
            w_heads_t,
            gains,
            angles,
            turned,
            w_down,
        )
    )
    Order.last, Order.also, Order.windows = None, (), False
    arrived = [shift(part, s + 1) for s, part in enumerate(cut(info, cot))]
    attn_in, queries, keys, values, attended, log_sum = attend(info, row, gains[0], w_heads, *angles)
    mixed, grad, grad_low, attended_grad, gain_ffn_part, *halves = ffn(
        info, row, attended, cot, arrived, gains[1], turned, [w_down, w_gate, w_up, w_out]
    )
    wide_sum = Sum(info, halves, TWO_ROUTES)
    Order.windows = True

    mixed_out = exchange(mixed)
    wide_sum.step()
    tokens_grad, *halves = back(
        info,
        (queries, keys, values, attended),
        attended_grad,
        log_sum,
        angles,
        (gains[0], gain_ffn_part),
        (row, grad, w_heads_t, attn_in, attended, grad_low),
    )
    wide_sum.step()
    Order.windows = False
    halves, Order.last = lax.optimization_barrier((halves, Order.last))
    attn_sum = DirectSum(info, halves)
    attn_sum.step()
    Order.also = (mixed_out,)
    wide_sum.step()
    wide_sum.step()
    attn_sum.step()
    wide_sum.step()
    attn_sum.step()
    wide_sum.step()
    attn_sum.step()
    wide_sum.step()
    tokens_grad, Order.last = lax.optimization_barrier((tokens_grad, Order.last))
    tokens_out = exchange(tokens_grad)
    Order.windows = True
    wide_sum.step()
    attn_sum.step()
    square = shape_of((model_width, model_width), jnp.float32)
    narrow = shape_of((kv_width, model_width), jnp.float32)
    shapes = [square, narrow, narrow, square, shape_of((model_width, 128), jnp.float32)]
    w_query_sum, w_key_sum, w_value_sum, w_out_sum, gains_sum = run(
        join_attn_kernel,
        "join",
        info,
        [attn_sum.outs, *attn_sum.next],
        shapes,
        [pltpu.VMEM((32, PIECE_ROWS, PIECE_COLS), jnp.float32)],
        24,
        (1,),
        [once(*attn_sum.outs.shape)] * 2,
        [once(*v.shape) for v in shapes],
    )
    mixed_out = place(info, mixed_out)
    Order.also = (tokens_out,)
    wide_sum.step()
    tokens_out = place(info, tokens_out)
    w_gate_sum, w_up_sum, w_down_sum = join_wide(info, wide_sum.outs, wide_sum.next)
    return (
        jnp.swapaxes(mixed_out, 1, 2),
        jnp.swapaxes(tokens_out, 1, 2),
        w_query_sum,
        w_key_sum.T,
        w_value_sum.T,
        w_out_sum,
        w_gate_sum,
        w_up_sum,
        w_down_sum.T,
        gains_sum[:, 64],
        gains_sum[:, 65],
    )


def solution(mesh):
    whole_rows = mesh.shape["dp"] == 8 and mesh.shape["seq"] == 4
    return jax.shard_map(
        local_rows if whole_rows else local_general,
        mesh=mesh,
        in_specs=(
            P("dp", "seq", None),
            P("dp"),
            P(),
            P(),
            P(),
            P(),
            P(),
            P(),
            P(),
            P(),
            P(),
            P("dp", "seq", None),
        ),
        out_specs=(
            P("dp", "seq", None),
            P("dp", "seq", None),
            P(),
            P(),
            P(),
            P(),
            P(),
            P(),
            P(),
            P(),
            P(),
        ),
        check_vma=False,
    )
```

```python
from functools import partial
import math

import jax
import jax.numpy as jnp
from jax import lax
from jax.experimental import pallas as pl
from jax.experimental.pallas import tpu as pltpu
from jax.sharding import PartitionSpec as P

HQ = 9
HK = 3
DH = 64


eps_norm = 1e-05
rope_base = 100000.0
neg_large = -1e30


def norm_rows(values, gain_vec):
    return (
        values * lax.rsqrt(jnp.mean(values * values, axis=-1, keepdims=True) + eps_norm) * gain_vec
    )


def rotate(values, positions, turn_sign):
    half_dim = values.shape[-1] // 2
    frequency = rope_base ** (-jnp.arange(half_dim, dtype=jnp.float32) / half_dim)
    angles = turn_sign * positions.astype(jnp.float32)[:, None] * frequency[None, :]
    cosine = jnp.cos(angles)[:, None, :]
    sine_part = jnp.sin(angles)[:, None, :]
    first_half = values[..., :half_dim]
    second_half = values[..., half_dim:]
    return jnp.concatenate(
        [
            first_half * cosine - second_half * sine_part,
            second_half * cosine + first_half * sine_part,
        ],
        axis=-1,
    )


def inner_rows(left, right):
    return lax.dot_general(
        left, right, (((0,), (0,)), ((), ())), preferred_element_type=jnp.float32
    )


def times_t(left, right):
    return lax.dot_general(
        left, right, (((1,), (1,)), ((), ())), preferred_element_type=jnp.float32
    )


def fold_piece(block_len, step_fn, carry, pieces):
    piece_count = pieces.shape[1] // block_len

    def inner_step(index_step, state):
        part_piece = lax.dynamic_slice_in_dim(pieces, index_step * block_len, block_len, 1)
        return step_fn(state, part_piece, index_step * block_len)

    return lax.fori_loop(0, piece_count, inner_step, carry)


def local_general(
    tokens,
    lengths,
    w_query,
    w_key,
    w_value,
    w_out,
    w_gate,
    w_up,
    w_down,
    gain_attn,
    gain_ffn,
    cotangent,
):
    row_count, block_len, model_width = tokens.shape
    group_size = HQ // HK
    kv_width = HK * DH
    score_scale = 1.0 / math.sqrt(DH)
    seq_devices = lax.axis_size("seq")
    my_start = lax.axis_index("seq") * block_len
    positions = my_start + jnp.arange(block_len, dtype=jnp.int32)
    longest = jnp.max(lengths)
    live_rows = positions[None, :] < lengths[:, None]
    query_active = my_start < longest
    inputs = tokens.reshape(-1, model_width).astype(jnp.float32)
    attn_norm, attn_pull = jax.vjp(norm_rows, inputs, gain_attn)
    attn_in = attn_norm.astype(jnp.bfloat16)
    query_pre = jnp.dot(attn_in, w_query, preferred_element_type=jnp.float32)
    query_heads = rotate(query_pre.reshape(row_count, block_len, HQ, DH), positions, 1.0).astype(
        jnp.bfloat16
    )
    query_heads = query_heads.reshape(row_count, block_len, HK, group_size, DH)
    key_pre = jnp.dot(attn_in, w_key, preferred_element_type=jnp.float32)
    key_heads = rotate(key_pre.reshape(row_count, block_len, HK, DH), positions, 1.0).astype(
        jnp.bfloat16
    )
    value_heads = jnp.dot(attn_in, w_value, preferred_element_type=jnp.float32).astype(jnp.bfloat16)
    key_value = jnp.concatenate(
        [
            key_heads.reshape(row_count, block_len, kv_width),
            value_heads.reshape(row_count, block_len, kv_width),
        ],
        axis=-1,
    )

    def allowed_for(piece_start):
        key_pos = piece_start + jnp.arange(block_len, dtype=jnp.int32)
        causal = key_pos[None, None, :] <= positions[None, :, None]
        inside = key_pos[None, None, :] < lengths[:, None, None]
        return causal & inside

    def needed_for(piece_start):
        return (piece_start <= my_start) & (piece_start < longest) & query_active

    def split_piece(pieces):
        key_part = pieces[..., :kv_width].reshape(row_count, block_len, HK, DH)
        value_part = pieces[..., kv_width:].reshape(row_count, block_len, HK, DH)
        return (key_part, value_part)

    def forward_block(carry, pieces, piece_start):

        def forward_compute_block(state):
            row_max, row_total, weighted = state
            key_part, value_part = split_piece(pieces)
            scores = (
                jnp.einsum(
                    "rqhgd,rkhd->rhgqk", query_heads, key_part, preferred_element_type=jnp.float32
                )
                * score_scale
            )
            allowed = allowed_for(piece_start)[:, None, None]
            scores = jnp.where(allowed, scores, neg_large)
            new_max = jnp.maximum(row_max, jnp.max(scores, axis=-1))
            shrink = jnp.exp(row_max - new_max)
            exp_scores = jnp.where(allowed, jnp.exp(scores - new_max[..., None]), 0.0)
            row_total = row_total * shrink + jnp.sum(exp_scores, axis=-1)
            update = jnp.einsum(
                "rhgqk,rkhd->rqhgd",
                exp_scores.astype(jnp.bfloat16),
                value_part,
                preferred_element_type=jnp.float32,
            )
            weighted = weighted * jnp.moveaxis(shrink, 3, 1)[..., None] + update
            return (new_max, row_total, weighted)

        return lax.cond(needed_for(piece_start), forward_compute_block, lambda state: state, carry)

    stat_shape = (row_count, HK, group_size, block_len)
    forward_init = (
        jnp.full(stat_shape, neg_large, jnp.float32),
        jnp.zeros(stat_shape, jnp.float32),
        jnp.zeros((row_count, block_len, HK, group_size, DH), jnp.float32),
    )
    forward_state = fold_piece(
        block_len, forward_block, forward_init, lax.all_gather(key_value, "seq", axis=1, tiled=True)
    )
    row_max, row_total, weighted = forward_state
    safe_total = jnp.where(row_total > 0, row_total, 1.0)
    attn_heads = weighted / jnp.moveaxis(safe_total, 3, 1)[..., None]
    attn_heads = jnp.where(live_rows[:, :, None, None, None], attn_heads, 0.0)
    log_sum = jnp.where(live_rows[:, None, None, :], row_max + jnp.log(safe_total), 0.0)
    attn_low = attn_heads.reshape(-1, HQ * DH).astype(jnp.bfloat16)
    residual = inputs + jnp.dot(attn_low, w_out, preferred_element_type=jnp.float32)
    ffn_norm, ffn_pull = jax.vjp(norm_rows, residual, gain_ffn)
    ffn_in = ffn_norm.astype(jnp.bfloat16)
    gate_proj = jnp.dot(ffn_in, w_gate, preferred_element_type=jnp.float32)
    up_proj = jnp.dot(ffn_in, w_up, preferred_element_type=jnp.float32)
    product, swiglu_pull = jax.vjp(
        lambda gate_in, up_in: jax.nn.silu(gate_in) * up_in, gate_proj, up_proj
    )
    hidden = product.astype(jnp.bfloat16)
    branch = jnp.dot(hidden, w_down, preferred_element_type=jnp.float32)
    mixed = (residual + branch).astype(jnp.bfloat16).reshape(row_count, block_len, model_width)
    out_low = cotangent.reshape(-1, model_width)
    out_grad = out_low.astype(jnp.float32)
    w_down_grad = inner_rows(hidden, out_low)
    hidden_grad = times_t(out_low, w_down)
    gate_grad, up_grad = swiglu_pull(hidden_grad)
    gate_low = gate_grad.astype(jnp.bfloat16)
    up_low = up_grad.astype(jnp.bfloat16)
    w_gate_grad = inner_rows(ffn_in, gate_low)
    w_up_grad = inner_rows(ffn_in, up_low)
    ffn_in_grad = times_t(gate_low, w_gate) + times_t(up_low, w_up)
    residual_part, gain_ffn_grad = ffn_pull(ffn_in_grad)
    residual_grad = out_grad + residual_part
    residual_low = residual_grad.astype(jnp.bfloat16)
    w_out_grad = inner_rows(attn_low, residual_low)
    attended_grad = times_t(residual_low, w_out).reshape(row_count, block_len, HK, group_size, DH)
    attended_grad = jnp.where(live_rows[:, :, None, None, None], attended_grad, 0.0).astype(
        jnp.bfloat16
    )
    grad_dot = jnp.moveaxis(jnp.sum(attended_grad.astype(jnp.float32) * attn_heads, axis=-1), 1, 3)

    def backward_block(with_kv, carry, pieces, piece_start):

        def backward_compute_block(state):
            key_part, value_part = split_piece(pieces)
            scores = (
                jnp.einsum(
                    "rqhgd,rkhd->rhgqk", query_heads, key_part, preferred_element_type=jnp.float32
                )
                * score_scale
            )
            allowed = allowed_for(piece_start)[:, None, None]
            weights_now = jnp.where(allowed, jnp.exp(scores - log_sum[..., None]), 0.0)
            weights_grad = jnp.einsum(
                "rqhgd,rkhd->rhgqk", attended_grad, value_part, preferred_element_type=jnp.float32
            )
            score_grad = (weights_now * (weights_grad - grad_dot[..., None])).astype(jnp.bfloat16)
            query_grad = (
                state[0]
                + jnp.einsum(
                    "rhgqk,rkhd->rqhgd", score_grad, key_part, preferred_element_type=jnp.float32
                )
                * score_scale
            )
            kv_grad = state[1]
            values_grad = jnp.einsum(
                "rhgqk,rqhgd->rkhd",
                weights_now.astype(jnp.bfloat16),
                attended_grad,
                preferred_element_type=jnp.float32,
            )
            keys_grad = (
                jnp.einsum(
                    "rhgqk,rqhgd->rkhd", score_grad, query_heads, preferred_element_type=jnp.float32
                )
                * score_scale
            )
            local_kv = jnp.concatenate(
                [
                    keys_grad.reshape(row_count, block_len, kv_width),
                    values_grad.reshape(row_count, block_len, kv_width),
                ],
                axis=-1,
            )
            current = lax.dynamic_slice_in_dim(kv_grad, piece_start, block_len, 1)
            kv_grad = lax.dynamic_update_slice_in_dim(kv_grad, current + local_kv, piece_start, 1)
            return (query_grad, kv_grad)

        return lax.cond(needed_for(piece_start), backward_compute_block, lambda state: state, carry)

    query_zero = jnp.zeros((row_count, block_len, HK, group_size, DH), jnp.float32)
    backward_init = (
        query_zero,
        jnp.zeros((row_count, block_len * seq_devices, 2 * kv_width), jnp.float32),
    )
    step_back = partial(backward_block, True)
    backward_state = fold_piece(
        block_len, step_back, backward_init, lax.all_gather(key_value, "seq", axis=1, tiled=True)
    )
    query_grad = backward_state[0]
    own_kv_grad = lax.psum_scatter(
        backward_state[1].astype(jnp.bfloat16), "seq", scatter_dimension=1, tiled=True
    ).astype(jnp.float32)
    query_low = (
        rotate(query_grad.reshape(row_count, block_len, HQ, DH), positions, -1.0)
        .astype(jnp.bfloat16)
        .reshape(-1, HQ * DH)
    )
    key_low = (
        rotate(own_kv_grad[..., :kv_width].reshape(row_count, block_len, HK, DH), positions, -1.0)
        .astype(jnp.bfloat16)
        .reshape(-1, kv_width)
    )
    value_low = own_kv_grad[..., kv_width:].astype(jnp.bfloat16).reshape(-1, kv_width)
    w_query_grad = inner_rows(attn_in, query_low)
    w_key_grad = inner_rows(attn_in, key_low)
    w_value_grad = inner_rows(attn_in, value_low)
    attn_in_grad = (
        times_t(query_low, w_query) + times_t(key_low, w_key) + times_t(value_low, w_value)
    )
    inputs_part, gain_attn_grad = attn_pull(attn_in_grad)
    tokens_grad = (
        (residual_grad + inputs_part)
        .astype(jnp.bfloat16)
        .reshape(row_count, block_len, model_width)
    )
    (
        w_query_grad,
        w_key_grad,
        w_value_grad,
        w_out_grad,
        w_gate_grad,
        w_up_grad,
        w_down_grad,
        gain_attn_grad,
        gain_ffn_grad,
    ) = lax.psum(
        (
            w_query_grad,
            w_key_grad,
            w_value_grad,
            w_out_grad,
            w_gate_grad,
            w_up_grad,
            w_down_grad,
            gain_attn_grad,
            gain_ffn_grad,
        ),
        ("dp", "seq"),
    )
    return (
        mixed,
        tokens_grad,
        w_query_grad,
        w_key_grad,
        w_value_grad,
        w_out_grad,
        w_gate_grad,
        w_up_grad,
        w_down_grad,
        gain_attn_grad,
        gain_ffn_grad,
    )


GROUP = HQ // HK
HEAD_ROWS = (GROUP + 2) * DH
SCALE = DH**-0.5
FULL = pl.BlockSpec(memory_space=pltpu.VMEM)
SMEM = pl.BlockSpec(memory_space=pltpu.SMEM)
ANY = pl.BlockSpec(memory_space=pl.ANY)


def shape_of(shape, dtype=jnp.bfloat16):
    return jax.ShapeDtypeStruct(shape, dtype)


def low(values):
    return values.astype(jnp.bfloat16)


def wide(values):
    return values.astype(jnp.float32)


def mul_nt(left, right):
    return lax.dot_general(
        left, right, (((1,), (1,)), ((), ())), preferred_element_type=jnp.float32
    )


def mul_nn(left, right):
    return lax.dot_general(
        left, right, (((1,), (0,)), ((), ())), preferred_element_type=jnp.float32
    )


class Order:
    last = None
    also = ()
    windows = False


def run(
    kernel, name, info, operands, out_shapes, scratch=(), vmem=12, grid=(), in_specs=None, out_specs=None
):
    after = [*([] if Order.last is None else [Order.last]), *Order.also]
    Order.also = ()
    taken = len(operands)

    def body(*refs):
        kernel(*refs[: 1 + taken], *refs[1 + taken + len(after) :])

    many = isinstance(out_shapes, list)
    if Order.windows and not grid:
        grid, vmem = (1,), 60
        in_specs = [once(*v.shape) for v in operands]
        out_specs = [once(*v.shape) for v in out_shapes] if many else once(*out_shapes.shape)
    outs = pl.pallas_call(
        body,
        grid=grid,
        in_specs=[SMEM] + (in_specs or [FULL] * taken) + [ANY] * len(after),
        out_specs=out_specs or ([FULL] * len(out_shapes) if many else FULL),
        scratch_shapes=list(scratch),
        out_shape=out_shapes,
        compiler_params=pltpu.CompilerParams(vmem_limit_bytes=vmem * 2**20),
        cost_estimate=pl.CostEstimate(flops=1000, bytes_accessed=1000, transcendentals=0),
        name=name,
    )(info, *operands, *after)
    Order.last = min(outs, key=lambda v: v.size) if many else outs
    return outs


def whole(*shape):
    return pl.BlockSpec(shape, lambda b: (0,) * len(shape))


def once(*shape):
    return pl.BlockSpec(shape, lambda b: (0,) * len(shape), pipeline_mode=pl.Buffered(1))


def at_block(*shape):
    return pl.BlockSpec((1, *shape), lambda b: (b, *[0] * len(shape)))


def turn(values, cosine, sine_part):
    first_half, second_half = values[: DH // 2], values[DH // 2 :]
    return jnp.concatenate(
        [
            first_half * cosine - second_half * sine_part,
            second_half * cosine + first_half * sine_part,
        ],
        axis=0,
    )


def inverse_rms(values):
    mean = jnp.sum(values * values, axis=0, keepdims=True) * (1.0 / values.shape[0])
    return lax.rsqrt(mean + eps_norm)


def norm_back(values, grad, gain):
    scale = inverse_rms(values)
    turned = grad * gain
    inner = jnp.sum(turned * values, axis=0, keepdims=True) * (1.0 / values.shape[0])
    part = scale * turned - values * (scale * scale * scale * inner)
    return part, grad * values * scale


def gain_of(ref):
    return jnp.concatenate([ref[...], ref[...]], axis=1)


def causal_mask(width):
    key_at = lax.broadcasted_iota(jnp.int32, (width, width), 0)
    query_at = lax.broadcasted_iota(jnp.int32, (width, width), 1)
    return jnp.concatenate([key_at <= query_at] * GROUP, axis=1)


def heads_of(values):
    return jnp.concatenate([values[j * DH : (j + 1) * DH] for j in range(GROUP)], axis=1)


def attend_kernel(
    info,
    row_ref,
    gain_ref,
    weights_ref,
    cos_ref,
    sin_ref,
    attn_in_ref,
    query_ref,
    key_ref,
    value_ref,
    out_ref,
    lse_ref,
    key_rows,
):
    blocks, _, width = row_ref.shape

    @pl.when(pl.program_id(0) == 0)
    def _():
        gain = gain_of(gain_ref)
        for b in range(blocks):
            values = wide(row_ref[b])
            attn_in_ref[b] = low(values * inverse_rms(values) * gain)

    mask = causal_mask(width)
    for b in range(blocks):
        pre = mul_nn(weights_ref[0], attn_in_ref[b])
        cosine, sine_part = cos_ref[b], sin_ref[b]
        for j in range(GROUP):
            query_ref[0, b, j * DH : (j + 1) * DH] = low(
                turn(pre[j * DH : (j + 1) * DH], cosine, sine_part) * SCALE
            )
        keys = low(turn(pre[GROUP * DH : (GROUP + 1) * DH], cosine, sine_part))
        key_ref[0, b] = keys
        key_rows[b] = keys.T
        value_ref[0, b] = low(pre[(GROUP + 1) * DH :])
    for b in range(blocks):
        queries = heads_of(query_ref[0, b])
        scores, top = [], None
        for k in range(b + 1):
            part = mul_nn(key_rows[k], queries)
            if k == b:
                part = jnp.where(mask, part, neg_large)
            scores.append(part)
            part_top = jnp.max(part, axis=0, keepdims=True)
            top = part_top if top is None else jnp.maximum(top, part_top)
        total, weighted = 0.0, 0.0
        for k in range(b + 1):
            weights_now = jnp.exp(scores[k] - top)
            total = total + jnp.sum(weights_now, axis=0, keepdims=True)
            weighted = weighted + mul_nn(value_ref[0, k], low(weights_now))
        weighted = weighted * (1.0 / total)
        log_sum = top + jnp.log(total)
        live = b * width + lax.broadcasted_iota(jnp.int32, (1, width), 1) < info[3]
        for j in range(GROUP):
            mine = slice(j * width, (j + 1) * width)
            out_ref[0, b, j * DH : (j + 1) * DH] = low(jnp.where(live, weighted[:, mine], 0.0))
            lse_ref[0, b, j : j + 1] = log_sum[:, mine]


def attend(info, row, gain, w_heads, cosine, sine_part):
    blocks, features, width = row.shape
    head = lambda rows: pl.BlockSpec((1, blocks, rows, width), lambda h: (h, 0, 0, 0))
    return run(
        attend_kernel,
        "attend",
        info,
        [row, gain, w_heads, cosine, sine_part],
        [
            shape_of((blocks, features, width)),
            shape_of((HK, blocks, GROUP * DH, width)),
            shape_of((HK, blocks, DH, width)),
            shape_of((HK, blocks, DH, width)),
            shape_of((HK, blocks, GROUP * DH, width)),
            shape_of((HK, blocks, 8, width), jnp.float32),
        ],
        [pltpu.VMEM((blocks, width, DH), jnp.bfloat16)],
        60,
        (HK,),
        [
            whole(*row.shape),
            whole(*gain.shape),
            pl.BlockSpec((1, HEAD_ROWS, features), lambda h: (h, 0, 0)),
            whole(*cosine.shape),
            whole(*cosine.shape),
        ],
        [whole(*row.shape), *[head(rows) for rows in (GROUP * DH, DH, DH, GROUP * DH, 8)]],
    )


def lanes_of(ref, rows=slice(None)):
    return jnp.concatenate([ref[b, rows] for b in range(ref.shape[0])], axis=1)


def put_grad(values, ref, at):
    planes, parts, _, rows, cols = ref.shape
    for p in range(planes):
        for z in range(parts):
            ref[p, z, at] = values[p * rows : (p + 1) * rows, z * cols : (z + 1) * cols].astype(
                ref.dtype
            )


CHUNK = 768


def ffn_kernel(
    info,
    row_ref,
    att_ref,
    cot_ref,
    in1_ref,
    in2_ref,
    in3_ref,
    gain_ref,
    w_out_t_ref,
    w_gate_t_ref,
    w_up_t_ref,
    w_down_t_ref,
    w_down_ref,
    w_gate_ref,
    w_up_ref,
    w_out_ref,
    mixed_ref,
    grad_ref,
    low_ref,
    att_grad_ref,
    gain_grad_ref,
    send_ref,
    keep_ref,
    ffn_ins,
    cots,
    hiddens,
    gates,
    ups,
):
    b = pl.program_id(0)
    width = row_ref.shape[2]
    gain = gain_of(gain_ref)
    attended = jnp.concatenate([att_ref[h, 0] for h in range(HK)], axis=0)
    residual = wide(row_ref[0]) + mul_nn(w_out_t_ref[...], attended)
    ffn_in = low(residual * inverse_rms(residual) * gain)
    ffn_ins[b] = ffn_in
    from_step = lax.rem(info[0] + 4 - b, 4)

    @pl.when(from_step == 0)
    def _():
        cots[b] = cot_ref[b]

    for step, ref in ((1, in1_ref), (2, in2_ref), (3, in3_ref)):

        @pl.when(from_step == step)
        def _():
            cots[b] = ref[...]

    cot = cots[b]
    mixed, ffn_in_grad = residual, 0.0
    for at in range(0, hiddens.shape[1], CHUNK):
        part = slice(at, at + CHUNK)
        gate = mul_nn(w_gate_t_ref[part], ffn_in)
        up = mul_nn(w_up_t_ref[part], ffn_in)
        hidden_grad = mul_nn(w_down_ref[part], cot)
        sigmoid = 1.0 / (1.0 + jnp.exp(-gate))
        silu = gate * sigmoid
        hidden = low(silu * up)
        gate_grad = low(hidden_grad * up * (sigmoid + silu * (1.0 - sigmoid)))
        up_grad = low(hidden_grad * silu)
        hiddens[b, part] = hidden
        gates[b, part] = gate_grad
        ups[b, part] = up_grad
        mixed = mixed + mul_nn(w_down_t_ref[:, part], hidden)
        ffn_in_grad = ffn_in_grad + (
            mul_nn(w_gate_ref[:, part], gate_grad) + mul_nn(w_up_ref[:, part], up_grad)
        )
    mixed_ref[0] = low(mixed)
    part, gain_terms = norm_back(residual, ffn_in_grad, gain)
    gain_terms = gain_terms[:, : width // 2] + gain_terms[:, width // 2 :]

    @pl.when(b == 0)
    def _():
        gain_grad_ref[...] = gain_terms

    @pl.when(b > 0)
    def _():
        gain_grad_ref[...] += gain_terms

    grad = wide(cot) + part
    grad_ref[0] = grad
    grad_low = low(grad)
    low_ref[0] = grad_low
    live = b * width + lax.broadcasted_iota(jnp.int32, (1, width), 1) < info[3]
    att_grad_ref[0] = low(jnp.where(live, mul_nn(w_out_ref[...], grad_low), 0.0))

    @pl.when(b == pl.num_programs(0) - 1)
    def _():
        rows = grad_ref.shape[1] // 2
        for half, ref in ((1 - info[1], send_ref), (info[1], keep_ref)):
            own = pl.ds(pl.multiple_of(half * rows, 16), rows)
            left = lanes_of(ffn_ins, own)
            put_grad(mul_nt(left, lanes_of(gates)), ref, 0)
            put_grad(mul_nt(left, lanes_of(ups)), ref, 1)
            put_grad(mul_nt(lanes_of(cots, own), lanes_of(hiddens)), ref, 2)


def ffn(info, row, attended, cot, arrived, gain, turned, straight):
    blocks, features, width = row.shape
    hidden = turned[1].shape[0]
    block, long = (blocks, features, width), (blocks, hidden, width)
    pieces = (4, 4, 3, features // 8, hidden // 4)
    return run(
        ffn_kernel,
        "ffn",
        info,
        [row, attended, cot, *arrived, gain, *turned, *straight],
        [
            shape_of(block),
            shape_of(block, jnp.float32),
            shape_of(block),
            shape_of(block),
            shape_of(gain.shape, jnp.float32),
            shape_of(pieces),
            shape_of(pieces),
        ],
        [pltpu.VMEM(block, jnp.bfloat16)] * 2 + [pltpu.VMEM(long, jnp.bfloat16)] * 3,
        52,
        (blocks,),
        [
            at_block(features, width),
            pl.BlockSpec((HK, 1, GROUP * DH, width), lambda b: (0, b, 0, 0)),
            whole(*cot.shape),
            *[whole(features, width)] * 3,
            whole(*gain.shape),
            *[FULL] * 8,
        ],
        [
            *[at_block(features, width)] * 4,
            whole(*gain.shape),
            *[whole(*pieces)] * 2,
        ],
    )


PIECE_ROWS = 48
PIECE_COLS = 640


def attend_back(refs, grad_ref, scratch):
    query_ref, key_ref, value_ref, out_ref, out_grad_ref, lse_ref, cos_ref, sin_ref = refs
    key_rows, value_rows, key_sum, value_sum = scratch
    blocks, width = query_ref.shape[1], query_ref.shape[3]
    for b in range(blocks):
        key_rows[b] = key_ref[0, b].T
        value_rows[b] = value_ref[0, b].T
    mask = causal_mask(width)
    for b in reversed(range(blocks)):
        queries, out_grad = heads_of(query_ref[0, b]), heads_of(out_grad_ref[b])
        grad_dot = jnp.sum(wide(out_grad) * wide(heads_of(out_ref[0, b])), axis=0, keepdims=True)
        log_sum = jnp.concatenate([lse_ref[0, b, j : j + 1] for j in range(GROUP)], axis=1)
        query_grad = 0.0
        for k in range(b + 1):
            weights_now = jnp.exp(mul_nn(key_rows[k], queries) - log_sum)
            if k == b:
                weights_now = jnp.where(mask, weights_now, 0.0)
            weights_grad = mul_nn(value_rows[k], out_grad)
            score_grad = low(weights_now * (weights_grad - grad_dot))
            value_part = mul_nt(out_grad, low(weights_now))
            key_part = mul_nt(queries, score_grad)
            if b == blocks - 1:
                value_sum[k] = value_part
                key_sum[k] = key_part
            else:
                value_sum[k] += value_part
                key_sum[k] += key_part
            query_grad = query_grad + mul_nn(key_ref[0, k], score_grad)
        cosine, sine_part = cos_ref[b], -sin_ref[b]
        for j in range(GROUP):
            grad_ref[b, j * DH : (j + 1) * DH] = low(
                turn(query_grad[:, j * width : (j + 1) * width], cosine * SCALE, sine_part * SCALE)
            )
        grad_ref[b, GROUP * DH : (GROUP + 1) * DH] = low(turn(key_sum[b], cosine, sine_part))
        grad_ref[b, (GROUP + 1) * DH :] = low(value_sum[b])


def back_kernel(info, *refs):
    heads, refs = refs[:8], refs[8:]
    (gain_ref, gain_ffn_ref), far, refs = refs[:2], refs[2:8], refs[8:]
    (out_ref, send_ref, keep_ref), refs = refs[:3], refs[3:]
    qkv_ref, gain_sum, scratch, near, sems = refs[0], refs[1], refs[2:6], refs[6:12], refs[12]
    row_ref, grad_ref, w_ref, attn_in_ref, att_ref, low_ref = near
    h = pl.program_id(0)
    copies = [
        pltpu.make_async_copy(there, here, sems.at[k])
        for k, (there, here) in enumerate(zip(far, near))
    ]

    @pl.when(h == 0)
    def _():
        for copy in copies:
            copy.start()

    attend_back(heads, qkv_ref.at[h], scratch)

    @pl.when(h == HK - 1)
    def _():
        for copy in copies:
            copy.wait()
        tokens_back(row_ref, grad_ref, gain_ref, w_ref, qkv_ref, out_ref, gain_sum)
        first = lambda ref: attn_grad_first(qkv_ref, attn_in_ref, gain_sum, gain_ffn_ref, ref)
        second = lambda ref: attn_grad_second(qkv_ref, attn_in_ref, att_ref, low_ref, ref)

        @pl.when(info[1] == 0)
        def _():
            second(send_ref)
            first(keep_ref)

        @pl.when(info[1] == 1)
        def _():
            first(send_ref)
            second(keep_ref)


def tokens_back(row_ref, grad_ref, gain_ref, w_ref, qkv_ref, out_ref, gain_sum):
    width = row_ref.shape[2]
    gain = gain_of(gain_ref)
    gain_sum[...] = jnp.zeros_like(gain_sum)

    def one_block(b, carry):
        qkv = jnp.concatenate([qkv_ref[h, b] for h in range(HK)], axis=0)
        part, gain_terms = norm_back(wide(row_ref[b]), mul_nn(w_ref[...], qkv), gain)
        gain_sum[...] += gain_terms[:, : width // 2] + gain_terms[:, width // 2 :]
        out_ref[b] = low(grad_ref[b] + part)
        return carry

    lax.fori_loop(0, row_ref.shape[0], one_block, 0)


def put_rows(values, ref, at, columns=None):
    features = values.shape[1]
    if columns is None:
        columns = jnp.zeros((values.shape[0], PIECE_COLS - features), jnp.float32)
    for piece in range(values.shape[0] // PIECE_ROWS):
        rows = slice(piece * PIECE_ROWS, (piece + 1) * PIECE_ROWS)
        p, z = (at + piece) // 4, (at + piece) % 4
        ref[p, z, 0, :, :features] = values[rows].astype(ref.dtype)
        ref[p, z, 0, :, features:] = columns[rows].astype(ref.dtype)


def take_rows(qkv_ref, start, size):
    rows = slice(start, start + size)
    return jnp.concatenate([lanes_of(qkv_ref.at[h], rows) for h in range(HK)], axis=0)


def attn_grad_first(qkv_ref, attn_in_ref, gain1_ref, gain2_ref, ref):
    attn_in = lanes_of(attn_in_ref)
    features = attn_in.shape[0]
    lane = lax.broadcasted_iota(jnp.int32, (features, PIECE_COLS - features), 1)
    gains = jnp.where(
        lane == 0,
        jnp.sum(gain1_ref[...], axis=1, keepdims=True),
        jnp.where(lane == 1, jnp.sum(gain2_ref[...], axis=1, keepdims=True), 0.0),
    )
    put_rows(mul_nt(attn_in, take_rows(qkv_ref, 0, GROUP * DH)), ref, 0, gains)
    keys = take_rows(qkv_ref, GROUP * DH, DH)
    put_rows(mul_nt(keys, attn_in), ref, features // PIECE_ROWS)


def attn_grad_second(qkv_ref, attn_in_ref, att_ref, low_ref, ref):
    values = take_rows(qkv_ref, (GROUP + 1) * DH, DH)
    put_rows(mul_nt(values, lanes_of(attn_in_ref)), ref, 0)
    attended = jnp.concatenate([lanes_of(att_ref.at[h]) for h in range(HK)], axis=0)
    put_rows(mul_nt(attended, lanes_of(low_ref)), ref, HK * DH // PIECE_ROWS)


def back(info, heads, attended_grad, log_sum, angles, gains, rest):
    queries, keys, values, attended = heads
    row = rest[0]
    _, blocks, _, width = queries.shape
    head = lambda rows: pl.BlockSpec((1, blocks, rows, width), lambda h: (h, 0, 0, 0))
    angle = once(*angles[0].shape)
    pieces = (4, 4, 1, PIECE_ROWS, PIECE_COLS)
    return run(
        back_kernel,
        "back",
        info,
        [queries, keys, values, attended, attended_grad, log_sum, *angles, *gains, *rest],
        [shape_of(row.shape), shape_of(pieces), shape_of(pieces)],
        [
            pltpu.VMEM((HK, blocks, HEAD_ROWS, width), jnp.bfloat16),
            pltpu.VMEM(gains[0].shape, jnp.float32),
        ]
        + [pltpu.VMEM((blocks, width, DH), jnp.bfloat16)] * 2
        + [pltpu.VMEM((blocks, DH, width), jnp.float32)] * 2
        + [pltpu.VMEM(v.shape, v.dtype) for v in rest]
        + [pltpu.SemaphoreType.DMA((6,))],
        60,
        (HK,),
        [
            *[head(rows) for rows in (GROUP * DH, DH, DH, GROUP * DH)],
            pl.BlockSpec((blocks, GROUP * DH, width), lambda h: (0, h, 0)),
            head(8),
            angle,
            angle,
            *[once(*g.shape) for g in gains],
            *[ANY] * 6,
        ],
        [whole(*row.shape), whole(*pieces), whole(*pieces)],
    )


def bit_of(value, bit):
    return lax.rem(value // (1 << bit), 2)


def plane_at(first, own, other):
    return own + 2 * other if first == 0 else other + 2 * own


def spot(routes, near, far):
    if len(routes) == 1:
        return 0, near + 2 * far
    return far, near


def split_plane_kernel(routes, info, keep_ref, in_ref, *outs):
    for k, (first, places) in enumerate(routes):
        mine = bit_of(info[2], first)
        send_ref, own_ref = outs[2 * k : 2 * k + 2]
        for t in range(2):
            there, here = plane_at(first, 1 - mine, t), plane_at(first, mine, t)
            for at, z in enumerate(places):
                send_ref[t, at] = low(wide(keep_ref[there, z]) + wide(in_ref[there, z]))
                own_ref[t, at] = wide(keep_ref[here, z]) + wide(in_ref[here, z])


def split_line_kernel(routes, info, *refs):
    count = len(routes)
    ins, outs = refs[: 2 * count], refs[2 * count :]
    for k, (first, _) in enumerate(routes):
        mine = bit_of(info[2], 1 - first)
        keep_ref, in_ref = ins[2 * k : 2 * k + 2]
        send_ref, own_ref = outs[2 * k : 2 * k + 2]
        send_ref[...] = low(keep_ref[1 - mine] + wide(in_ref[1 - mine]))
        own_ref[...] = keep_ref[mine] + wide(in_ref[mine])


def split_near_kernel(routes, info, *refs):
    ins, (send_ref, own_ref) = refs[:-2], refs[-2:]
    near = bit_of(info[0], 0)
    for far in range(2):
        k, there = spot(routes, 1 - near, far)
        k, here = spot(routes, near, far)
        keep_ref, in_ref = ins[2 * k : 2 * k + 2]
        send_ref[far] = low(keep_ref[there] + wide(in_ref[there]))
        own_ref[far] = keep_ref[here] + wide(in_ref[here])


def split_far_kernel(routes, info, keep_ref, in_ref, send_ref, own_ref):
    far = bit_of(info[0], 1)
    send_ref[...] = low(keep_ref[1 - far] + wide(in_ref[1 - far]))
    own_ref[...] = keep_ref[far] + wide(in_ref[far])


def total_kernel(routes, info, keep_ref, in_ref, out_ref):
    out_ref[...] = low(keep_ref[...] + wide(in_ref[...]))


def join_far_kernel(routes, info, own_ref, in_ref, out_ref):
    far = bit_of(info[0], 1)
    out_ref[far] = own_ref[...]
    out_ref[1 - far] = in_ref[...]


def join_near_kernel(routes, info, own_ref, in_ref, *outs):
    near = bit_of(info[0], 0)
    for far in range(2):
        k, here = spot(routes, near, far)
        k, there = spot(routes, 1 - near, far)
        outs[k][here] = own_ref[far]
        outs[k][there] = in_ref[far]


def join_line_kernel(routes, info, *refs):
    count = len(routes)
    ins, outs = refs[: 2 * count], refs[2 * count :]
    for k, (first, _) in enumerate(routes):
        mine = bit_of(info[2], 1 - first)
        outs[k][mine] = ins[2 * k][...]
        outs[k][1 - mine] = ins[2 * k + 1][...]


def swap(values, axis, bits):
    count = 8 if axis == "dp" else 4
    return lax.ppermute(values, axis, [(k, k ^ bits) for k in range(count)])


TWO_ROUTES = ((0, (0, 1)), (1, (2, 3)))


class Sum:
    def __init__(self, info, send_keep, routes):
        self.info, self.routes = info, routes
        self.send, self.keep = send_keep
        self.piece = self.send.shape[2:]
        self.stage = 0
        self.next = swap(self.send, "dp", 1)

    def call(self, kernel, operands, shapes):
        return run(partial(kernel, self.routes), kernel.__name__[:-7], self.info, operands, shapes)

    def step(self):
        routes, piece = self.routes, tuple(self.piece)
        count, places = len(routes), len(routes[0][1])
        both = lambda *shape: [shape_of(shape), shape_of(shape, jnp.float32)]
        plane = [2 << first for first, _ in routes]
        line = [2 << (1 - first) for first, _ in routes]
        if self.stage == 0:
            self.outs = self.call(
                split_plane_kernel, [self.keep, self.next], both(2, places, *piece) * count
            )
            self.next = [swap(self.outs[2 * k], "dp", plane[k]) for k in range(count)]
        elif self.stage in (1, 2):
            operands = []
            for k in range(count):
                operands += [self.outs[2 * k + 1], self.next[k]]
            if self.stage == 1:
                self.outs = self.call(split_line_kernel, operands, both(places, *piece) * count)
                self.next = [swap(self.outs[2 * k], "dp", line[k]) for k in range(count)]
            else:
                self.outs = self.call(split_near_kernel, operands, both(2, *piece))
                self.next = swap(self.outs[0], "seq", 1)
        elif self.stage == 3:
            self.outs = self.call(split_far_kernel, [self.outs[1], self.next], both(*piece))
            self.next = swap(self.outs[0], "seq", 2)
        elif self.stage == 4:
            self.outs = self.call(total_kernel, [self.outs[1], self.next], shape_of(piece))
            self.next = swap(self.outs, "seq", 2)
        elif self.stage == 5:
            self.outs = self.call(join_far_kernel, [self.outs, self.next], shape_of((2, *piece)))
            self.next = swap(self.outs, "seq", 1)
        elif self.stage == 6:
            self.outs = self.call(
                join_near_kernel, [self.outs, self.next], [shape_of((places, *piece))] * count
            )
            self.next = [swap(self.outs[k], "dp", line[k]) for k in range(count)]
        elif self.stage == 7:
            operands = []
            for k in range(count):
                operands += [self.outs[k], self.next[k]]
            self.outs = self.call(join_line_kernel, operands, [shape_of((2, places, *piece))] * count)
            self.next = [swap(self.outs[k], "dp", plane[k]) for k in range(count)]
        self.stage += 1


def add_core_kernel(info, keep_ref, in_ref, own_ref, *out_refs):
    plane = info[2]
    own_ref[...] = wide(keep_ref[plane]) + wide(in_ref[plane])
    for step, ref in enumerate(out_refs):
        other = plane ^ (step + 1)
        ref[...] = low(wide(keep_ref[other]) + wide(in_ref[other]))


def add_plane_kernel(info, keep_ref, in1_ref, in2_ref, in3_ref, own_ref, *out_refs):
    total = lambda z: (
        (keep_ref[z] + wide(in1_ref[z])) + (wide(in2_ref[z]) + wide(in3_ref[z]))
    )
    own_ref[...] = total(info[0])
    for step, ref in enumerate(out_refs):
        ref[...] = low(total(lax.rem(info[0] + step + 1, 4)))


def add_seq_kernel(info, keep_ref, in1_ref, in2_ref, in3_ref, out_ref):
    out_ref[...] = low(
        (keep_ref[...] + wide(in1_ref[...])) + (wide(in2_ref[...]) + wide(in3_ref[...]))
    )


def join_seq_kernel(info, own_ref, in1_ref, in2_ref, in3_ref, out_ref):
    for step, ref in enumerate((own_ref, in1_ref, in2_ref, in3_ref)):
        out_ref[lax.rem(info[0] + 4 - step, 4)] = ref[...]


def join_chips_kernel(info, own_ref, in1_ref, in2_ref, in3_ref, out_ref):
    for step, ref in enumerate((own_ref, in1_ref, in2_ref, in3_ref)):
        out_ref[info[2] ^ step] = ref[...]


class DirectSum:
    def __init__(self, info, send_keep):
        self.info = info
        self.send, self.keep = send_keep
        self.piece = self.send.shape[2:]
        self.stage = 0
        self.next = [swap(self.send, "dp", 1)]

    def step(self):
        piece = tuple(self.piece)
        line = (4, *piece)
        kernel, shapes = [
            (add_core_kernel, [shape_of(line, jnp.float32)] + [shape_of(line)] * 3),
            (add_plane_kernel, [shape_of(piece, jnp.float32)] + [shape_of(piece)] * 3),
            (add_seq_kernel, shape_of(piece)),
            (join_seq_kernel, shape_of(line)),
            (join_chips_kernel, shape_of((4, *line))),
        ][self.stage]
        first = self.keep if self.stage == 0 else self.outs
        if isinstance(first, list | tuple):
            first = first[0]
        outs = run(kernel, kernel.__name__[:-7], self.info, [first, *self.next], shapes)
        self.outs = outs
        sends = outs[1:] if isinstance(outs, list | tuple) else [outs] * 3
        if self.stage in (0, 3):
            self.next = [swap(v, "dp", 2 * k) for k, v in zip((1, 2, 3), sends)]
        elif self.stage in (1, 2):
            self.next = [shift(v, k) for k, v in zip((1, 2, 3), sends)]
        else:
            self.next = [swap(outs, "dp", 1)]
        self.stage += 1


def join_wide_kernel(routes, info, *refs):
    parts, outs, refs = refs[:8], refs[8:11], refs[11:]
    buffers, sems = refs[:3], refs[3]
    _, _, count, rows, cols = parts[0].shape
    copies = [pltpu.make_async_copy(buffers[w], outs[w], sems.at[w]) for w in range(count)]
    for w in range(count):
        for side in range(4):
            core = info[1] if side < 2 else 1 - info[1]
            for k, (first, places) in enumerate(routes):
                mine = bit_of(info[2], first)
                mine = mine if side % 2 == 0 else 1 - mine
                ref = parts[2 * side + k]
                for t in range(2):
                    p = plane_at(first, mine, t)
                    for at, z in enumerate(places):
                        buffers[w][core, p, :, z * cols : (z + 1) * cols] = wide(ref[t, at, w])
        copies[w].start()
    for copy in copies:
        copy.wait()


def join_wide(info, routes, parts):
    _, _, count, rows, cols = parts[0].shape
    shape = (2, 4, rows, 4 * cols)
    outs = run(
        partial(join_wide_kernel, routes),
        "join",
        info,
        parts,
        [shape_of(shape, jnp.float32)] * count,
        [pltpu.VMEM(shape, jnp.float32)] * count + [pltpu.SemaphoreType.DMA((3,))],
        60,
        (1,),
        [once(*v.shape) for v in parts],
        [ANY] * count,
    )
    return [v.reshape(8 * rows, 4 * cols) for v in outs]


def join_attn_kernel(
    info, own_ref, in_ref, query_ref, key_ref, value_ref, out_ref, gains_ref, total
):
    planes, parts, _, rows, cols = own_ref.shape
    for ref, core in ((own_ref, info[1]), (in_ref, 1 - info[1])):
        for p in range(planes):
            for z in range(parts):
                total[core * (planes * parts) + p * parts + z] = wide(ref[p, z, 0])
    at = 0
    features = query_ref.shape[1]
    for ref in (query_ref, key_ref, value_ref, out_ref):
        for piece in range(ref.shape[0] // rows):
            ref[piece * rows : (piece + 1) * rows] = total[at, :, :features]
            if ref is query_ref:
                gains_ref[piece * rows : (piece + 1) * rows] = total[at, :, cols - 128 :]
            at += 1


def cut_kernel(info, values_ref, *refs):
    outs, sems = refs[:-1], refs[-1]
    copies = [
        pltpu.make_async_copy(values_ref.at[lax.rem(info[0] + step + 1, 4)], out, sems.at[step])
        for step, out in enumerate(outs)
    ]
    for copy in copies:
        copy.start()
    for copy in copies:
        copy.wait()


def cut(info, values):
    return run(
        cut_kernel,
        "cut",
        info,
        [values],
        [shape_of(values.shape[1:])] * 3,
        [pltpu.SemaphoreType.DMA((3,))],
        12,
        (1,),
        [ANY],
        [ANY] * 3,
    )


def shift(values, step):
    return lax.ppermute(values, "seq", [(k, (k + step) % 4) for k in range(4)])


def place_kernel(info, in_ref, out_ref):
    out_ref[...] = in_ref[...]


def place(info, values):
    return run(place_kernel, "place", info, [values], shape_of(values.shape))


def exchange(values):
    return lax.all_to_all(values, "seq", 0, 0)


def local_rows(
    tokens,
    lengths,
    w_query,
    w_key,
    w_value,
    w_out,
    w_gate,
    w_up,
    w_down,
    gain_attn,
    gain_ffn,
    cotangent,
):
    row_count, block_len, model_width = tokens.shape
    kv_width = HK * DH
    dp_at, seq_at = lax.axis_index("dp"), lax.axis_index("seq")
    length = lax.dynamic_slice_in_dim(lengths, seq_at, 1)
    info = jnp.concatenate([jnp.stack([seq_at, dp_at % 2, dp_at // 2]).astype(jnp.int32), length])
    half_dim = DH // 2
    positions = jnp.arange(row_count * block_len, dtype=jnp.float32).reshape(row_count, 1, -1)
    frequency = rope_base ** (-jnp.arange(half_dim, dtype=jnp.float32) / half_dim)
    angles = frequency[None, :, None] * positions
    angles = (jnp.cos(angles), jnp.sin(angles))
    w_heads = jnp.concatenate(
        [
            w_query.T.reshape(HK, GROUP * DH, model_width),
            w_key.T.reshape(HK, DH, model_width),
            w_value.T.reshape(HK, DH, model_width),
        ],
        axis=1,
    )
    w_heads_t = w_heads.reshape(-1, model_width).T
    gains = [
        jnp.broadcast_to(g[:, None], (model_width, block_len // 2)) for g in (gain_attn, gain_ffn)
    ]
    turned = [w_out.T, w_gate.T, w_up.T, w_down.T]

    row = exchange(jnp.swapaxes(tokens, 1, 2))
    cot, info, w_heads, w_heads_t, gains, angles, turned, w_down = lax.optimization_barrier(
        (
            jnp.swapaxes(cotangent, 1, 2),
            info,
            w_heads,
            w_heads_t,
            gains,
            angles,
            turned,
            w_down,
        )
    )
    Order.last, Order.also, Order.windows = None, (), False
    arrived = [shift(part, s + 1) for s, part in enumerate(cut(info, cot))]
    attn_in, queries, keys, values, attended, log_sum = attend(info, row, gains[0], w_heads, *angles)
    mixed, grad, grad_low, attended_grad, gain_ffn_part, *halves = ffn(
        info, row, attended, cot, arrived, gains[1], turned, [w_down, w_gate, w_up, w_out]
    )
    wide_sum = Sum(info, halves, TWO_ROUTES)
    Order.windows = True

    mixed_out = exchange(mixed)
    wide_sum.step()
    tokens_grad, *halves = back(
        info,
        (queries, keys, values, attended),
        attended_grad,
        log_sum,
        angles,
        (gains[0], gain_ffn_part),
        (row, grad, w_heads_t, attn_in, attended, grad_low),
    )
    wide_sum.step()
    Order.windows = False
    halves, Order.last = lax.optimization_barrier((halves, Order.last))
    attn_sum = DirectSum(info, halves)
    attn_sum.step()
    Order.also = (mixed_out,)
    wide_sum.step()
    wide_sum.step()
    attn_sum.step()
    wide_sum.step()
    attn_sum.step()
    wide_sum.step()
    attn_sum.step()
    wide_sum.step()
    tokens_grad, Order.last = lax.optimization_barrier((tokens_grad, Order.last))
    tokens_out = exchange(tokens_grad)
    Order.windows = True
    wide_sum.step()
    near_came = [swap(part, "dp", 1) for part in wide_sum.outs]
    attn_sum.step()
    square = shape_of((model_width, model_width), jnp.float32)
    narrow = shape_of((kv_width, model_width), jnp.float32)
    shapes = [square, narrow, narrow, square, shape_of((model_width, 128), jnp.float32)]
    w_query_sum, w_key_sum, w_value_sum, w_out_sum, gains_sum = run(
        join_attn_kernel,
        "join",
        info,
        [attn_sum.outs, *attn_sum.next],
        shapes,
        [pltpu.VMEM((32, PIECE_ROWS, PIECE_COLS), jnp.float32)],
        24,
        (1,),
        [once(*attn_sum.outs.shape)] * 2,
        [once(*v.shape) for v in shapes],
    )
    Order.also = tuple(near_came)
    mixed_out = place(info, mixed_out)
    far_came = [swap(part, "dp", 1) for part in wide_sum.next]
    Order.also = (tokens_out,)
    tokens_out = place(info, tokens_out)
    w_gate_sum, w_up_sum, w_down_sum = join_wide(
        info, TWO_ROUTES, [*wide_sum.outs, *wide_sum.next, *near_came, *far_came]
    )
    return (
        jnp.swapaxes(mixed_out, 1, 2),
        jnp.swapaxes(tokens_out, 1, 2),
        w_query_sum,
        w_key_sum.T,
        w_value_sum.T,
        w_out_sum,
        w_gate_sum,
        w_up_sum,
        w_down_sum.T,
        gains_sum[:, 64],
        gains_sum[:, 65],
    )


def solution(mesh):
    whole_rows = mesh.shape["dp"] == 8 and mesh.shape["seq"] == 4
    return jax.shard_map(
        local_rows if whole_rows else local_general,
        mesh=mesh,
        in_specs=(
            P("dp", "seq", None),
            P("dp"),
            P(),
            P(),
            P(),
            P(),
            P(),
            P(),
            P(),
            P(),
            P(),
            P("dp", "seq", None),
        ),
        out_specs=(
            P("dp", "seq", None),
            P("dp", "seq", None),
            P(),
            P(),
            P(),
            P(),
            P(),
            P(),
            P(),
            P(),
            P(),
        ),
        check_vma=False,
    )
```

```python
from functools import partial
import math

import jax
import jax.numpy as jnp
from jax import lax
from jax.experimental import pallas as pl
from jax.experimental.pallas import tpu as pltpu
from jax.sharding import PartitionSpec as P

HQ = 9
HK = 3
DH = 64


eps_norm = 1e-05
rope_base = 100000.0
neg_large = -1e30


def norm_rows(values, gain_vec):
    return (
        values * lax.rsqrt(jnp.mean(values * values, axis=-1, keepdims=True) + eps_norm) * gain_vec
    )


def rotate(values, positions, turn_sign):
    half_dim = values.shape[-1] // 2
    frequency = rope_base ** (-jnp.arange(half_dim, dtype=jnp.float32) / half_dim)
    angles = turn_sign * positions.astype(jnp.float32)[:, None] * frequency[None, :]
    cosine = jnp.cos(angles)[:, None, :]
    sine_part = jnp.sin(angles)[:, None, :]
    first_half = values[..., :half_dim]
    second_half = values[..., half_dim:]
    return jnp.concatenate(
        [
            first_half * cosine - second_half * sine_part,
            second_half * cosine + first_half * sine_part,
        ],
        axis=-1,
    )


def inner_rows(left, right):
    return lax.dot_general(
        left, right, (((0,), (0,)), ((), ())), preferred_element_type=jnp.float32
    )


def times_t(left, right):
    return lax.dot_general(
        left, right, (((1,), (1,)), ((), ())), preferred_element_type=jnp.float32
    )


def fold_piece(block_len, step_fn, carry, pieces):
    piece_count = pieces.shape[1] // block_len

    def inner_step(index_step, state):
        part_piece = lax.dynamic_slice_in_dim(pieces, index_step * block_len, block_len, 1)
        return step_fn(state, part_piece, index_step * block_len)

    return lax.fori_loop(0, piece_count, inner_step, carry)


def local_general(
    tokens,
    lengths,
    w_query,
    w_key,
    w_value,
    w_out,
    w_gate,
    w_up,
    w_down,
    gain_attn,
    gain_ffn,
    cotangent,
):
    row_count, block_len, model_width = tokens.shape
    group_size = HQ // HK
    kv_width = HK * DH
    score_scale = 1.0 / math.sqrt(DH)
    seq_devices = lax.axis_size("seq")
    my_start = lax.axis_index("seq") * block_len
    positions = my_start + jnp.arange(block_len, dtype=jnp.int32)
    longest = jnp.max(lengths)
    live_rows = positions[None, :] < lengths[:, None]
    query_active = my_start < longest
    inputs = tokens.reshape(-1, model_width).astype(jnp.float32)
    attn_norm, attn_pull = jax.vjp(norm_rows, inputs, gain_attn)
    attn_in = attn_norm.astype(jnp.bfloat16)
    query_pre = jnp.dot(attn_in, w_query, preferred_element_type=jnp.float32)
    query_heads = rotate(query_pre.reshape(row_count, block_len, HQ, DH), positions, 1.0).astype(
        jnp.bfloat16
    )
    query_heads = query_heads.reshape(row_count, block_len, HK, group_size, DH)
    key_pre = jnp.dot(attn_in, w_key, preferred_element_type=jnp.float32)
    key_heads = rotate(key_pre.reshape(row_count, block_len, HK, DH), positions, 1.0).astype(
        jnp.bfloat16
    )
    value_heads = jnp.dot(attn_in, w_value, preferred_element_type=jnp.float32).astype(jnp.bfloat16)
    key_value = jnp.concatenate(
        [
            key_heads.reshape(row_count, block_len, kv_width),
            value_heads.reshape(row_count, block_len, kv_width),
        ],
        axis=-1,
    )

    def allowed_for(piece_start):
        key_pos = piece_start + jnp.arange(block_len, dtype=jnp.int32)
        causal = key_pos[None, None, :] <= positions[None, :, None]
        inside = key_pos[None, None, :] < lengths[:, None, None]
        return causal & inside

    def needed_for(piece_start):
        return (piece_start <= my_start) & (piece_start < longest) & query_active

    def split_piece(pieces):
        key_part = pieces[..., :kv_width].reshape(row_count, block_len, HK, DH)
        value_part = pieces[..., kv_width:].reshape(row_count, block_len, HK, DH)
        return (key_part, value_part)

    def forward_block(carry, pieces, piece_start):

        def forward_compute_block(state):
            row_max, row_total, weighted = state
            key_part, value_part = split_piece(pieces)
            scores = (
                jnp.einsum(
                    "rqhgd,rkhd->rhgqk", query_heads, key_part, preferred_element_type=jnp.float32
                )
                * score_scale
            )
            allowed = allowed_for(piece_start)[:, None, None]
            scores = jnp.where(allowed, scores, neg_large)
            new_max = jnp.maximum(row_max, jnp.max(scores, axis=-1))
            shrink = jnp.exp(row_max - new_max)
            exp_scores = jnp.where(allowed, jnp.exp(scores - new_max[..., None]), 0.0)
            row_total = row_total * shrink + jnp.sum(exp_scores, axis=-1)
            update = jnp.einsum(
                "rhgqk,rkhd->rqhgd",
                exp_scores.astype(jnp.bfloat16),
                value_part,
                preferred_element_type=jnp.float32,
            )
            weighted = weighted * jnp.moveaxis(shrink, 3, 1)[..., None] + update
            return (new_max, row_total, weighted)

        return lax.cond(needed_for(piece_start), forward_compute_block, lambda state: state, carry)

    stat_shape = (row_count, HK, group_size, block_len)
    forward_init = (
        jnp.full(stat_shape, neg_large, jnp.float32),
        jnp.zeros(stat_shape, jnp.float32),
        jnp.zeros((row_count, block_len, HK, group_size, DH), jnp.float32),
    )
    forward_state = fold_piece(
        block_len, forward_block, forward_init, lax.all_gather(key_value, "seq", axis=1, tiled=True)
    )
    row_max, row_total, weighted = forward_state
    safe_total = jnp.where(row_total > 0, row_total, 1.0)
    attn_heads = weighted / jnp.moveaxis(safe_total, 3, 1)[..., None]
    attn_heads = jnp.where(live_rows[:, :, None, None, None], attn_heads, 0.0)
    log_sum = jnp.where(live_rows[:, None, None, :], row_max + jnp.log(safe_total), 0.0)
    attn_low = attn_heads.reshape(-1, HQ * DH).astype(jnp.bfloat16)
    residual = inputs + jnp.dot(attn_low, w_out, preferred_element_type=jnp.float32)
    ffn_norm, ffn_pull = jax.vjp(norm_rows, residual, gain_ffn)
    ffn_in = ffn_norm.astype(jnp.bfloat16)
    gate_proj = jnp.dot(ffn_in, w_gate, preferred_element_type=jnp.float32)
    up_proj = jnp.dot(ffn_in, w_up, preferred_element_type=jnp.float32)
    product, swiglu_pull = jax.vjp(
        lambda gate_in, up_in: jax.nn.silu(gate_in) * up_in, gate_proj, up_proj
    )
    hidden = product.astype(jnp.bfloat16)
    branch = jnp.dot(hidden, w_down, preferred_element_type=jnp.float32)
    mixed = (residual + branch).astype(jnp.bfloat16).reshape(row_count, block_len, model_width)
    out_low = cotangent.reshape(-1, model_width)
    out_grad = out_low.astype(jnp.float32)
    w_down_grad = inner_rows(hidden, out_low)
    hidden_grad = times_t(out_low, w_down)
    gate_grad, up_grad = swiglu_pull(hidden_grad)
    gate_low = gate_grad.astype(jnp.bfloat16)
    up_low = up_grad.astype(jnp.bfloat16)
    w_gate_grad = inner_rows(ffn_in, gate_low)
    w_up_grad = inner_rows(ffn_in, up_low)
    ffn_in_grad = times_t(gate_low, w_gate) + times_t(up_low, w_up)
    residual_part, gain_ffn_grad = ffn_pull(ffn_in_grad)
    residual_grad = out_grad + residual_part
    residual_low = residual_grad.astype(jnp.bfloat16)
    w_out_grad = inner_rows(attn_low, residual_low)
    attended_grad = times_t(residual_low, w_out).reshape(row_count, block_len, HK, group_size, DH)
    attended_grad = jnp.where(live_rows[:, :, None, None, None], attended_grad, 0.0).astype(
        jnp.bfloat16
    )
    grad_dot = jnp.moveaxis(jnp.sum(attended_grad.astype(jnp.float32) * attn_heads, axis=-1), 1, 3)

    def backward_block(with_kv, carry, pieces, piece_start):

        def backward_compute_block(state):
            key_part, value_part = split_piece(pieces)
            scores = (
                jnp.einsum(
                    "rqhgd,rkhd->rhgqk", query_heads, key_part, preferred_element_type=jnp.float32
                )
                * score_scale
            )
            allowed = allowed_for(piece_start)[:, None, None]
            weights_now = jnp.where(allowed, jnp.exp(scores - log_sum[..., None]), 0.0)
            weights_grad = jnp.einsum(
                "rqhgd,rkhd->rhgqk", attended_grad, value_part, preferred_element_type=jnp.float32
            )
            score_grad = (weights_now * (weights_grad - grad_dot[..., None])).astype(jnp.bfloat16)
            query_grad = (
                state[0]
                + jnp.einsum(
                    "rhgqk,rkhd->rqhgd", score_grad, key_part, preferred_element_type=jnp.float32
                )
                * score_scale
            )
            kv_grad = state[1]
            values_grad = jnp.einsum(
                "rhgqk,rqhgd->rkhd",
                weights_now.astype(jnp.bfloat16),
                attended_grad,
                preferred_element_type=jnp.float32,
            )
            keys_grad = (
                jnp.einsum(
                    "rhgqk,rqhgd->rkhd", score_grad, query_heads, preferred_element_type=jnp.float32
                )
                * score_scale
            )
            local_kv = jnp.concatenate(
                [
                    keys_grad.reshape(row_count, block_len, kv_width),
                    values_grad.reshape(row_count, block_len, kv_width),
                ],
                axis=-1,
            )
            current = lax.dynamic_slice_in_dim(kv_grad, piece_start, block_len, 1)
            kv_grad = lax.dynamic_update_slice_in_dim(kv_grad, current + local_kv, piece_start, 1)
            return (query_grad, kv_grad)

        return lax.cond(needed_for(piece_start), backward_compute_block, lambda state: state, carry)

    query_zero = jnp.zeros((row_count, block_len, HK, group_size, DH), jnp.float32)
    backward_init = (
        query_zero,
        jnp.zeros((row_count, block_len * seq_devices, 2 * kv_width), jnp.float32),
    )
    step_back = partial(backward_block, True)
    backward_state = fold_piece(
        block_len, step_back, backward_init, lax.all_gather(key_value, "seq", axis=1, tiled=True)
    )
    query_grad = backward_state[0]
    own_kv_grad = lax.psum_scatter(
        backward_state[1].astype(jnp.bfloat16), "seq", scatter_dimension=1, tiled=True
    ).astype(jnp.float32)
    query_low = (
        rotate(query_grad.reshape(row_count, block_len, HQ, DH), positions, -1.0)
        .astype(jnp.bfloat16)
        .reshape(-1, HQ * DH)
    )
    key_low = (
        rotate(own_kv_grad[..., :kv_width].reshape(row_count, block_len, HK, DH), positions, -1.0)
        .astype(jnp.bfloat16)
        .reshape(-1, kv_width)
    )
    value_low = own_kv_grad[..., kv_width:].astype(jnp.bfloat16).reshape(-1, kv_width)
    w_query_grad = inner_rows(attn_in, query_low)
    w_key_grad = inner_rows(attn_in, key_low)
    w_value_grad = inner_rows(attn_in, value_low)
    attn_in_grad = (
        times_t(query_low, w_query) + times_t(key_low, w_key) + times_t(value_low, w_value)
    )
    inputs_part, gain_attn_grad = attn_pull(attn_in_grad)
    tokens_grad = (
        (residual_grad + inputs_part)
        .astype(jnp.bfloat16)
        .reshape(row_count, block_len, model_width)
    )
    (
        w_query_grad,
        w_key_grad,
        w_value_grad,
        w_out_grad,
        w_gate_grad,
        w_up_grad,
        w_down_grad,
        gain_attn_grad,
        gain_ffn_grad,
    ) = lax.psum(
        (
            w_query_grad,
            w_key_grad,
            w_value_grad,
            w_out_grad,
            w_gate_grad,
            w_up_grad,
            w_down_grad,
            gain_attn_grad,
            gain_ffn_grad,
        ),
        ("dp", "seq"),
    )
    return (
        mixed,
        tokens_grad,
        w_query_grad,
        w_key_grad,
        w_value_grad,
        w_out_grad,
        w_gate_grad,
        w_up_grad,
        w_down_grad,
        gain_attn_grad,
        gain_ffn_grad,
    )


GROUP = HQ // HK
HEAD_ROWS = (GROUP + 2) * DH
SCALE = DH**-0.5
FULL = pl.BlockSpec(memory_space=pltpu.VMEM)
SMEM = pl.BlockSpec(memory_space=pltpu.SMEM)
ANY = pl.BlockSpec(memory_space=pl.ANY)


def shape_of(shape, dtype=jnp.bfloat16):
    return jax.ShapeDtypeStruct(shape, dtype)


def low(values):
    return values.astype(jnp.bfloat16)


def wide(values):
    return values.astype(jnp.float32)


def mul_nt(left, right):
    return lax.dot_general(
        left, right, (((1,), (1,)), ((), ())), preferred_element_type=jnp.float32
    )


def mul_nn(left, right):
    return lax.dot_general(
        left, right, (((1,), (0,)), ((), ())), preferred_element_type=jnp.float32
    )


class Order:
    last = None
    also = ()
    windows = False


def run(
    kernel, name, info, operands, out_shapes, scratch=(), vmem=12, grid=(), in_specs=None, out_specs=None
):
    after = [*([] if Order.last is None else [Order.last]), *Order.also]
    Order.also = ()
    taken = len(operands)

    def body(*refs):
        kernel(*refs[: 1 + taken], *refs[1 + taken + len(after) :])

    many = isinstance(out_shapes, list)
    if Order.windows and not grid:
        grid, vmem = (1,), 60
        in_specs = [once(*v.shape) for v in operands]
        out_specs = [once(*v.shape) for v in out_shapes] if many else once(*out_shapes.shape)
    outs = pl.pallas_call(
        body,
        grid=grid,
        in_specs=[SMEM] + (in_specs or [FULL] * taken) + [ANY] * len(after),
        out_specs=out_specs or ([FULL] * len(out_shapes) if many else FULL),
        scratch_shapes=list(scratch),
        out_shape=out_shapes,
        compiler_params=pltpu.CompilerParams(vmem_limit_bytes=vmem * 2**20),
        cost_estimate=pl.CostEstimate(flops=1000, bytes_accessed=1000, transcendentals=0),
        name=name,
    )(info, *operands, *after)
    Order.last = min(outs, key=lambda v: v.size) if many else outs
    return outs


def whole(*shape):
    return pl.BlockSpec(shape, lambda b: (0,) * len(shape))


def once(*shape):
    return pl.BlockSpec(shape, lambda b: (0,) * len(shape), pipeline_mode=pl.Buffered(1))


def at_block(*shape):
    return pl.BlockSpec((1, *shape), lambda b: (b, *[0] * len(shape)))


def turn(values, cosine, sine_part):
    first_half, second_half = values[: DH // 2], values[DH // 2 :]
    return jnp.concatenate(
        [
            first_half * cosine - second_half * sine_part,
            second_half * cosine + first_half * sine_part,
        ],
        axis=0,
    )


def inverse_rms(values):
    mean = jnp.sum(values * values, axis=0, keepdims=True) * (1.0 / values.shape[0])
    return lax.rsqrt(mean + eps_norm)


def norm_back(values, grad, gain):
    scale = inverse_rms(values)
    turned = grad * gain
    inner = jnp.sum(turned * values, axis=0, keepdims=True) * (1.0 / values.shape[0])
    part = scale * turned - values * (scale * scale * scale * inner)
    return part, grad * values * scale


def gain_of(ref):
    return jnp.concatenate([ref[...], ref[...]], axis=1)


def causal_mask(width):
    key_at = lax.broadcasted_iota(jnp.int32, (width, width), 0)
    query_at = lax.broadcasted_iota(jnp.int32, (width, width), 1)
    return jnp.concatenate([key_at <= query_at] * GROUP, axis=1)


def heads_of(values):
    return jnp.concatenate([values[j * DH : (j + 1) * DH] for j in range(GROUP)], axis=1)


def attend_kernel(
    info,
    row_ref,
    gain_ref,
    weights_ref,
    cos_ref,
    sin_ref,
    attn_in_ref,
    query_ref,
    key_ref,
    value_ref,
    out_ref,
    lse_ref,
    key_rows,
):
    blocks, _, width = row_ref.shape

    @pl.when(pl.program_id(0) == 0)
    def _():
        gain = gain_of(gain_ref)
        for b in range(blocks):
            values = wide(row_ref[b])
            attn_in_ref[b] = low(values * inverse_rms(values) * gain)

    mask = causal_mask(width)
    for b in range(blocks):
        pre = mul_nn(weights_ref[0], attn_in_ref[b])
        cosine, sine_part = cos_ref[b], sin_ref[b]
        for j in range(GROUP):
            query_ref[0, b, j * DH : (j + 1) * DH] = low(
                turn(pre[j * DH : (j + 1) * DH], cosine, sine_part) * SCALE
            )
        keys = low(turn(pre[GROUP * DH : (GROUP + 1) * DH], cosine, sine_part))
        key_ref[0, b] = keys
        key_rows[b] = keys.T
        value_ref[0, b] = low(pre[(GROUP + 1) * DH :])
    for b in range(blocks):
        queries = heads_of(query_ref[0, b])
        scores, top = [], None
        for k in range(b + 1):
            part = mul_nn(key_rows[k], queries)
            if k == b:
                part = jnp.where(mask, part, neg_large)
            scores.append(part)
            part_top = jnp.max(part, axis=0, keepdims=True)
            top = part_top if top is None else jnp.maximum(top, part_top)
        total, weighted = 0.0, 0.0
        for k in range(b + 1):
            weights_now = jnp.exp(scores[k] - top)
            total = total + jnp.sum(weights_now, axis=0, keepdims=True)
            weighted = weighted + mul_nn(value_ref[0, k], low(weights_now))
        weighted = weighted * (1.0 / total)
        log_sum = top + jnp.log(total)
        live = b * width + lax.broadcasted_iota(jnp.int32, (1, width), 1) < info[3]
        for j in range(GROUP):
            mine = slice(j * width, (j + 1) * width)
            out_ref[0, b, j * DH : (j + 1) * DH] = low(jnp.where(live, weighted[:, mine], 0.0))
            lse_ref[0, b, j : j + 1] = log_sum[:, mine]


def attend(info, row, gain, w_heads, cosine, sine_part):
    blocks, features, width = row.shape
    head = lambda rows: pl.BlockSpec((1, blocks, rows, width), lambda h: (h, 0, 0, 0))
    return run(
        attend_kernel,
        "attend",
        info,
        [row, gain, w_heads, cosine, sine_part],
        [
            shape_of((blocks, features, width)),
            shape_of((HK, blocks, GROUP * DH, width)),
            shape_of((HK, blocks, DH, width)),
            shape_of((HK, blocks, DH, width)),
            shape_of((HK, blocks, GROUP * DH, width)),
            shape_of((HK, blocks, 8, width), jnp.float32),
        ],
        [pltpu.VMEM((blocks, width, DH), jnp.bfloat16)],
        60,
        (HK,),
        [
            whole(*row.shape),
            whole(*gain.shape),
            pl.BlockSpec((1, HEAD_ROWS, features), lambda h: (h, 0, 0)),
            whole(*cosine.shape),
            whole(*cosine.shape),
        ],
        [whole(*row.shape), *[head(rows) for rows in (GROUP * DH, DH, DH, GROUP * DH, 8)]],
    )


def lanes_of(ref, rows=slice(None)):
    return jnp.concatenate([ref[b, rows] for b in range(ref.shape[0])], axis=1)


def put_grad(values, ref, at):
    planes, parts, _, rows, cols = ref.shape
    for p in range(planes):
        for z in range(parts):
            ref[p, z, at] = values[p * rows : (p + 1) * rows, z * cols : (z + 1) * cols].astype(
                ref.dtype
            )


CHUNK = 768


def ffn_kernel(
    info,
    row_ref,
    att_ref,
    cot_ref,
    in1_ref,
    in2_ref,
    in3_ref,
    gain_ref,
    w_out_t_ref,
    w_gate_t_ref,
    w_up_t_ref,
    w_down_t_ref,
    w_down_ref,
    w_gate_ref,
    w_up_ref,
    w_out_ref,
    mixed_ref,
    grad_ref,
    low_ref,
    att_grad_ref,
    gain_grad_ref,
    send_ref,
    keep_ref,
    ffn_ins,
    cots,
    hiddens,
    gates,
    ups,
):
    b = pl.program_id(0)
    width = row_ref.shape[2]
    gain = gain_of(gain_ref)
    attended = jnp.concatenate([att_ref[h, 0] for h in range(HK)], axis=0)
    residual = wide(row_ref[0]) + mul_nn(w_out_t_ref[...], attended)
    ffn_in = low(residual * inverse_rms(residual) * gain)
    ffn_ins[b] = ffn_in
    from_step = lax.rem(info[0] + 4 - b, 4)

    @pl.when(from_step == 0)
    def _():
        cots[b] = cot_ref[b]

    for step, ref in ((1, in1_ref), (2, in2_ref), (3, in3_ref)):

        @pl.when(from_step == step)
        def _():
            cots[b] = ref[...]

    cot = cots[b]
    mixed, ffn_in_grad = residual, 0.0
    for at in range(0, hiddens.shape[1], CHUNK):
        part = slice(at, at + CHUNK)
        gate = mul_nn(w_gate_t_ref[part], ffn_in)
        up = mul_nn(w_up_t_ref[part], ffn_in)
        hidden_grad = mul_nn(w_down_ref[part], cot)
        sigmoid = 1.0 / (1.0 + jnp.exp(-gate))
        silu = gate * sigmoid
        hidden = low(silu * up)
        gate_grad = low(hidden_grad * up * (sigmoid + silu * (1.0 - sigmoid)))
        up_grad = low(hidden_grad * silu)
        hiddens[b, part] = hidden
        gates[b, part] = gate_grad
        ups[b, part] = up_grad
        mixed = mixed + mul_nn(w_down_t_ref[:, part], hidden)
        ffn_in_grad = ffn_in_grad + (
            mul_nn(w_gate_ref[:, part], gate_grad) + mul_nn(w_up_ref[:, part], up_grad)
        )
    mixed_ref[0] = low(mixed)
    part, gain_terms = norm_back(residual, ffn_in_grad, gain)
    gain_terms = gain_terms[:, : width // 2] + gain_terms[:, width // 2 :]

    @pl.when(b == 0)
    def _():
        gain_grad_ref[...] = gain_terms

    @pl.when(b > 0)
    def _():
        gain_grad_ref[...] += gain_terms

    grad = wide(cot) + part
    grad_ref[0] = grad
    grad_low = low(grad)
    low_ref[0] = grad_low
    live = b * width + lax.broadcasted_iota(jnp.int32, (1, width), 1) < info[3]
    att_grad_ref[0] = low(jnp.where(live, mul_nn(w_out_ref[...], grad_low), 0.0))

    @pl.when(b == pl.num_programs(0) - 1)
    def _():
        rows = grad_ref.shape[1] // 2
        for half, ref in ((1 - info[1], send_ref), (info[1], keep_ref)):
            own = pl.ds(pl.multiple_of(half * rows, 16), rows)
            left = lanes_of(ffn_ins, own)
            put_grad(mul_nt(left, lanes_of(gates)), ref, 0)
            put_grad(mul_nt(left, lanes_of(ups)), ref, 1)
            put_grad(mul_nt(lanes_of(cots, own), lanes_of(hiddens)), ref, 2)


def ffn(info, row, attended, cot, arrived, gain, turned, straight):
    blocks, features, width = row.shape
    hidden = turned[1].shape[0]
    block, long = (blocks, features, width), (blocks, hidden, width)
    pieces = (4, 4, 3, features // 8, hidden // 4)
    return run(
        ffn_kernel,
        "ffn",
        info,
        [row, attended, cot, *arrived, gain, *turned, *straight],
        [
            shape_of(block),
            shape_of(block, jnp.float32),
            shape_of(block),
            shape_of(block),
            shape_of(gain.shape, jnp.float32),
            shape_of(pieces),
            shape_of(pieces),
        ],
        [pltpu.VMEM(block, jnp.bfloat16)] * 2 + [pltpu.VMEM(long, jnp.bfloat16)] * 3,
        52,
        (blocks,),
        [
            at_block(features, width),
            pl.BlockSpec((HK, 1, GROUP * DH, width), lambda b: (0, b, 0, 0)),
            whole(*cot.shape),
            *[whole(features, width)] * 3,
            whole(*gain.shape),
            *[FULL] * 8,
        ],
        [
            *[at_block(features, width)] * 4,
            whole(*gain.shape),
            *[whole(*pieces)] * 2,
        ],
    )


PIECE_ROWS = 48
PIECE_COLS = 640


def attend_back(refs, grad_ref, scratch):
    query_ref, key_ref, value_ref, out_ref, out_grad_ref, lse_ref, cos_ref, sin_ref = refs
    key_rows, value_rows, key_sum, value_sum = scratch
    blocks, width = query_ref.shape[1], query_ref.shape[3]
    for b in range(blocks):
        key_rows[b] = key_ref[0, b].T
        value_rows[b] = value_ref[0, b].T
    mask = causal_mask(width)
    for b in reversed(range(blocks)):
        queries, out_grad = heads_of(query_ref[0, b]), heads_of(out_grad_ref[b])
        grad_dot = jnp.sum(wide(out_grad) * wide(heads_of(out_ref[0, b])), axis=0, keepdims=True)
        log_sum = jnp.concatenate([lse_ref[0, b, j : j + 1] for j in range(GROUP)], axis=1)
        query_grad = 0.0
        for k in range(b + 1):
            weights_now = jnp.exp(mul_nn(key_rows[k], queries) - log_sum)
            if k == b:
                weights_now = jnp.where(mask, weights_now, 0.0)
            weights_grad = mul_nn(value_rows[k], out_grad)
            score_grad = low(weights_now * (weights_grad - grad_dot))
            value_part = mul_nt(out_grad, low(weights_now))
            key_part = mul_nt(queries, score_grad)
            if b == blocks - 1:
                value_sum[k] = value_part
                key_sum[k] = key_part
            else:
                value_sum[k] += value_part
                key_sum[k] += key_part
            query_grad = query_grad + mul_nn(key_ref[0, k], score_grad)
        cosine, sine_part = cos_ref[b], -sin_ref[b]
        for j in range(GROUP):
            grad_ref[b, j * DH : (j + 1) * DH] = low(
                turn(query_grad[:, j * width : (j + 1) * width], cosine * SCALE, sine_part * SCALE)
            )
        grad_ref[b, GROUP * DH : (GROUP + 1) * DH] = low(turn(key_sum[b], cosine, sine_part))
        grad_ref[b, (GROUP + 1) * DH :] = low(value_sum[b])


def back_kernel(info, *refs):
    heads, refs = refs[:8], refs[8:]
    (gain_ref, gain_ffn_ref), far, refs = refs[:2], refs[2:8], refs[8:]
    (out_ref, send_ref, keep_ref), refs = refs[:3], refs[3:]
    qkv_ref, gain_sum, scratch, near, sems = refs[0], refs[1], refs[2:6], refs[6:12], refs[12]
    row_ref, grad_ref, w_ref, attn_in_ref, att_ref, low_ref = near
    h = pl.program_id(0)
    copies = [
        pltpu.make_async_copy(there, here, sems.at[k])
        for k, (there, here) in enumerate(zip(far, near))
    ]

    @pl.when(h == 0)
    def _():
        for copy in copies:
            copy.start()

    attend_back(heads, qkv_ref.at[h], scratch)

    @pl.when(h == HK - 1)
    def _():
        for copy in copies:
            copy.wait()
        tokens_back(row_ref, grad_ref, gain_ref, w_ref, qkv_ref, out_ref, gain_sum)
        first = lambda ref: attn_grad_first(qkv_ref, attn_in_ref, gain_sum, gain_ffn_ref, ref)
        second = lambda ref: attn_grad_second(qkv_ref, attn_in_ref, att_ref, low_ref, ref)

        @pl.when(info[1] == 0)
        def _():
            second(send_ref)
            first(keep_ref)

        @pl.when(info[1] == 1)
        def _():
            first(send_ref)
            second(keep_ref)


def tokens_back(row_ref, grad_ref, gain_ref, w_ref, qkv_ref, out_ref, gain_sum):
    width = row_ref.shape[2]
    gain = gain_of(gain_ref)
    gain_sum[...] = jnp.zeros_like(gain_sum)

    def one_block(b, carry):
        qkv = jnp.concatenate([qkv_ref[h, b] for h in range(HK)], axis=0)
        part, gain_terms = norm_back(wide(row_ref[b]), mul_nn(w_ref[...], qkv), gain)
        gain_sum[...] += gain_terms[:, : width // 2] + gain_terms[:, width // 2 :]
        out_ref[b] = low(grad_ref[b] + part)
        return carry

    lax.fori_loop(0, row_ref.shape[0], one_block, 0)


def put_rows(values, ref, at, columns=None):
    features = values.shape[1]
    if columns is None:
        columns = jnp.zeros((values.shape[0], PIECE_COLS - features), jnp.float32)
    for piece in range(values.shape[0] // PIECE_ROWS):
        rows = slice(piece * PIECE_ROWS, (piece + 1) * PIECE_ROWS)
        p, z = (at + piece) // 4, (at + piece) % 4
        ref[p, z, 0, :, :features] = values[rows].astype(ref.dtype)
        ref[p, z, 0, :, features:] = columns[rows].astype(ref.dtype)


def take_rows(qkv_ref, start, size):
    rows = slice(start, start + size)
    return jnp.concatenate([lanes_of(qkv_ref.at[h], rows) for h in range(HK)], axis=0)


def attn_grad_first(qkv_ref, attn_in_ref, gain1_ref, gain2_ref, ref):
    attn_in = lanes_of(attn_in_ref)
    features = attn_in.shape[0]
    lane = lax.broadcasted_iota(jnp.int32, (features, PIECE_COLS - features), 1)
    gains = jnp.where(
        lane == 0,
        jnp.sum(gain1_ref[...], axis=1, keepdims=True),
        jnp.where(lane == 1, jnp.sum(gain2_ref[...], axis=1, keepdims=True), 0.0),
    )
    put_rows(mul_nt(attn_in, take_rows(qkv_ref, 0, GROUP * DH)), ref, 0, gains)
    keys = take_rows(qkv_ref, GROUP * DH, DH)
    put_rows(mul_nt(keys, attn_in), ref, features // PIECE_ROWS)


def attn_grad_second(qkv_ref, attn_in_ref, att_ref, low_ref, ref):
    values = take_rows(qkv_ref, (GROUP + 1) * DH, DH)
    put_rows(mul_nt(values, lanes_of(attn_in_ref)), ref, 0)
    attended = jnp.concatenate([lanes_of(att_ref.at[h]) for h in range(HK)], axis=0)
    put_rows(mul_nt(attended, lanes_of(low_ref)), ref, HK * DH // PIECE_ROWS)


def back(info, heads, attended_grad, log_sum, angles, gains, rest):
    queries, keys, values, attended = heads
    row = rest[0]
    _, blocks, _, width = queries.shape
    head = lambda rows: pl.BlockSpec((1, blocks, rows, width), lambda h: (h, 0, 0, 0))
    angle = once(*angles[0].shape)
    pieces = (4, 4, 1, PIECE_ROWS, PIECE_COLS)
    return run(
        back_kernel,
        "back",
        info,
        [queries, keys, values, attended, attended_grad, log_sum, *angles, *gains, *rest],
        [shape_of(row.shape), shape_of(pieces), shape_of(pieces)],
        [
            pltpu.VMEM((HK, blocks, HEAD_ROWS, width), jnp.bfloat16),
            pltpu.VMEM(gains[0].shape, jnp.float32),
        ]
        + [pltpu.VMEM((blocks, width, DH), jnp.bfloat16)] * 2
        + [pltpu.VMEM((blocks, DH, width), jnp.float32)] * 2
        + [pltpu.VMEM(v.shape, v.dtype) for v in rest]
        + [pltpu.SemaphoreType.DMA((6,))],
        60,
        (HK,),
        [
            *[head(rows) for rows in (GROUP * DH, DH, DH, GROUP * DH)],
            pl.BlockSpec((blocks, GROUP * DH, width), lambda h: (0, h, 0)),
            head(8),
            angle,
            angle,
            *[once(*g.shape) for g in gains],
            *[ANY] * 6,
        ],
        [whole(*row.shape), whole(*pieces), whole(*pieces)],
    )


def bit_of(value, bit):
    return lax.rem(value // (1 << bit), 2)


def plane_at(first, own, other):
    return own + 2 * other if first == 0 else other + 2 * own


def spot(routes, near, far):
    if len(routes) == 1:
        return 0, near + 2 * far
    return far, near


def split_plane_kernel(routes, info, keep_ref, in_ref, *outs):
    for k, (first, places) in enumerate(routes):
        mine = bit_of(info[2], first)
        send_ref, own_ref = outs[2 * k : 2 * k + 2]
        for t in range(2):
            there, here = plane_at(first, 1 - mine, t), plane_at(first, mine, t)
            for at, z in enumerate(places):
                send_ref[t, at] = low(wide(keep_ref[there, z]) + wide(in_ref[there, z]))
                own_ref[t, at] = wide(keep_ref[here, z]) + wide(in_ref[here, z])


def split_line_kernel(routes, info, *refs):
    count = len(routes)
    ins, outs = refs[: 2 * count], refs[2 * count :]
    for k, (first, _) in enumerate(routes):
        mine = bit_of(info[2], 1 - first)
        keep_ref, in_ref = ins[2 * k : 2 * k + 2]
        send_ref, own_ref = outs[2 * k : 2 * k + 2]
        send_ref[...] = low(keep_ref[1 - mine] + wide(in_ref[1 - mine]))
        own_ref[...] = keep_ref[mine] + wide(in_ref[mine])


def split_near_kernel(routes, info, *refs):
    ins, (send_ref, own_ref) = refs[:-2], refs[-2:]
    near = bit_of(info[0], 0)
    for far in range(2):
        k, there = spot(routes, 1 - near, far)
        k, here = spot(routes, near, far)
        keep_ref, in_ref = ins[2 * k : 2 * k + 2]
        send_ref[far] = low(keep_ref[there] + wide(in_ref[there]))
        own_ref[far] = keep_ref[here] + wide(in_ref[here])


def split_far_kernel(routes, info, keep_ref, in_ref, send_ref, own_ref):
    far = bit_of(info[0], 1)
    send_ref[...] = low(keep_ref[1 - far] + wide(in_ref[1 - far]))
    own_ref[...] = keep_ref[far] + wide(in_ref[far])


def total_kernel(routes, info, keep_ref, in_ref, out_ref):
    out_ref[...] = low(keep_ref[...] + wide(in_ref[...]))


def join_far_kernel(routes, info, own_ref, in_ref, out_ref):
    far = bit_of(info[0], 1)
    out_ref[far] = own_ref[...]
    out_ref[1 - far] = in_ref[...]


def join_near_kernel(routes, info, own_ref, in_ref, *outs):
    near = bit_of(info[0], 0)
    for far in range(2):
        k, here = spot(routes, near, far)
        k, there = spot(routes, 1 - near, far)
        outs[k][here] = own_ref[far]
        outs[k][there] = in_ref[far]


def join_line_kernel(routes, info, *refs):
    count = len(routes)
    ins, outs = refs[: 2 * count], refs[2 * count :]
    for k, (first, _) in enumerate(routes):
        mine = bit_of(info[2], 1 - first)
        outs[k][mine] = ins[2 * k][...]
        outs[k][1 - mine] = ins[2 * k + 1][...]


def swap(values, axis, bits):
    count = 8 if axis == "dp" else 4
    return lax.ppermute(values, axis, [(k, k ^ bits) for k in range(count)])


TWO_ROUTES = ((0, (0, 1)), (1, (2, 3)))


class Sum:
    def __init__(self, info, send_keep, routes):
        self.info, self.routes = info, routes
        self.send, self.keep = send_keep
        self.piece = self.send.shape[2:]
        self.stage = 0
        self.next = swap(self.send, "dp", 1)

    def call(self, kernel, operands, shapes):
        return run(partial(kernel, self.routes), kernel.__name__[:-7], self.info, operands, shapes)

    def step(self):
        routes, piece = self.routes, tuple(self.piece)
        count, places = len(routes), len(routes[0][1])
        both = lambda *shape: [shape_of(shape), shape_of(shape, jnp.float32)]
        plane = [2 << first for first, _ in routes]
        line = [2 << (1 - first) for first, _ in routes]
        if self.stage == 0:
            self.outs = self.call(
                split_plane_kernel, [self.keep, self.next], both(2, places, *piece) * count
            )
            self.next = [swap(self.outs[2 * k], "dp", plane[k]) for k in range(count)]
        elif self.stage in (1, 2):
            operands = []
            for k in range(count):
                operands += [self.outs[2 * k + 1], self.next[k]]
            if self.stage == 1:
                self.outs = self.call(split_line_kernel, operands, both(places, *piece) * count)
                self.next = [swap(self.outs[2 * k], "dp", line[k]) for k in range(count)]
            else:
                self.outs = self.call(split_near_kernel, operands, both(2, *piece))
                self.next = swap(self.outs[0], "seq", 1)
        elif self.stage == 3:
            self.outs = self.call(split_far_kernel, [self.outs[1], self.next], both(*piece))
            self.next = swap(self.outs[0], "seq", 2)
        elif self.stage == 4:
            self.outs = self.call(total_kernel, [self.outs[1], self.next], shape_of(piece))
            self.next = swap(self.outs, "seq", 2)
        elif self.stage == 5:
            self.outs = self.call(join_far_kernel, [self.outs, self.next], shape_of((2, *piece)))
            self.next = swap(self.outs, "seq", 1)
        elif self.stage == 6:
            self.outs = self.call(
                join_near_kernel, [self.outs, self.next], [shape_of((places, *piece))] * count
            )
            self.next = [swap(self.outs[k], "dp", line[k]) for k in range(count)]
        elif self.stage == 7:
            operands = []
            for k in range(count):
                operands += [self.outs[k], self.next[k]]
            self.outs = self.call(join_line_kernel, operands, [shape_of((2, places, *piece))] * count)
            self.next = [swap(self.outs[k], "dp", plane[k]) for k in range(count)]
        self.stage += 1


def add_core_kernel(info, keep_ref, in_ref, own_ref, *out_refs):
    plane = info[2]
    own_ref[...] = wide(keep_ref[plane]) + wide(in_ref[plane])
    for step, ref in enumerate(out_refs):
        other = plane ^ (step + 1)
        ref[...] = low(wide(keep_ref[other]) + wide(in_ref[other]))


def add_plane_kernel(info, keep_ref, in1_ref, in2_ref, in3_ref, own_ref, *out_refs):
    total = lambda z: (
        (keep_ref[z] + wide(in1_ref[z])) + (wide(in2_ref[z]) + wide(in3_ref[z]))
    )
    own_ref[...] = total(info[0])
    for step, ref in enumerate(out_refs):
        ref[...] = low(total(lax.rem(info[0] + step + 1, 4)))


def add_seq_kernel(info, keep_ref, in1_ref, in2_ref, in3_ref, out_ref):
    out_ref[...] = low(
        (keep_ref[...] + wide(in1_ref[...])) + (wide(in2_ref[...]) + wide(in3_ref[...]))
    )


def join_seq_kernel(info, own_ref, in1_ref, in2_ref, in3_ref, out_ref):
    for step, ref in enumerate((own_ref, in1_ref, in2_ref, in3_ref)):
        out_ref[lax.rem(info[0] + 4 - step, 4)] = ref[...]


def join_chips_kernel(info, own_ref, in1_ref, in2_ref, in3_ref, out_ref):
    for step, ref in enumerate((own_ref, in1_ref, in2_ref, in3_ref)):
        out_ref[info[2] ^ step] = ref[...]


class DirectSum:
    def __init__(self, info, send_keep):
        self.info = info
        self.send, self.keep = send_keep
        self.piece = self.send.shape[2:]
        self.stage = 0
        self.next = [swap(self.send, "dp", 1)]

    def step(self):
        piece = tuple(self.piece)
        line = (4, *piece)
        kernel, shapes = [
            (add_core_kernel, [shape_of(line, jnp.float32)] + [shape_of(line)] * 3),
            (add_plane_kernel, [shape_of(piece, jnp.float32)] + [shape_of(piece)] * 3),
            (add_seq_kernel, shape_of(piece)),
            (join_seq_kernel, shape_of(line)),
            (join_chips_kernel, shape_of((4, *line))),
        ][self.stage]
        first = self.keep if self.stage == 0 else self.outs
        if isinstance(first, list | tuple):
            first = first[0]
        outs = run(kernel, kernel.__name__[:-7], self.info, [first, *self.next], shapes)
        self.outs = outs
        sends = outs[1:] if isinstance(outs, list | tuple) else [outs] * 3
        if self.stage in (0, 3):
            self.next = [swap(v, "dp", 2 * k) for k, v in zip((1, 2, 3), sends)]
        elif self.stage in (1, 2):
            self.next = [shift(v, k) for k, v in zip((1, 2, 3), sends)]
        else:
            self.next = [swap(outs, "dp", 1)]
        self.stage += 1


def join_wide_kernel(routes, info, *refs):
    parts, outs, refs = refs[:8], refs[8:11], refs[11:]
    buffers, sems = refs[:3], refs[3]
    _, _, count, rows, cols = parts[0].shape
    copies = [pltpu.make_async_copy(buffers[w], outs[w], sems.at[w]) for w in range(count)]
    for w in range(count):
        for side in range(4):
            core = info[1] if side < 2 else 1 - info[1]
            for k, (first, places) in enumerate(routes):
                mine = bit_of(info[2], first)
                mine = mine if side % 2 == 0 else 1 - mine
                ref = parts[2 * side + k]
                for t in range(2):
                    p = plane_at(first, mine, t)
                    for at, z in enumerate(places):
                        buffers[w][core, p, :, z * cols : (z + 1) * cols] = wide(ref[t, at, w])
        copies[w].start()
    for copy in copies:
        copy.wait()


def join_wide(info, routes, parts):
    _, _, count, rows, cols = parts[0].shape
    shape = (2, 4, rows, 4 * cols)
    outs = run(
        partial(join_wide_kernel, routes),
        "join",
        info,
        parts,
        [shape_of(shape, jnp.float32)] * count,
        [pltpu.VMEM(shape, jnp.float32)] * count + [pltpu.SemaphoreType.DMA((3,))],
        60,
        (1,),
        [once(*v.shape) for v in parts],
        [ANY] * count,
    )
    return [v.reshape(8 * rows, 4 * cols) for v in outs]


def join_attn_kernel(
    info, own_ref, in_ref, query_ref, key_ref, value_ref, out_ref, gains_ref, total
):
    planes, parts, _, rows, cols = own_ref.shape
    for ref, core in ((own_ref, info[1]), (in_ref, 1 - info[1])):
        for p in range(planes):
            for z in range(parts):
                total[core * (planes * parts) + p * parts + z] = wide(ref[p, z, 0])
    at = 0
    features = query_ref.shape[1]
    for ref in (query_ref, key_ref, value_ref, out_ref):
        for piece in range(ref.shape[0] // rows):
            ref[piece * rows : (piece + 1) * rows] = total[at, :, :features]
            if ref is query_ref:
                gains_ref[piece * rows : (piece + 1) * rows] = total[at, :, cols - 128 :]
            at += 1


def cut_kernel(info, values_ref, *refs):
    outs, sems = refs[:-1], refs[-1]
    copies = [
        pltpu.make_async_copy(values_ref.at[lax.rem(info[0] + step + 1, 4)], out, sems.at[step])
        for step, out in enumerate(outs)
    ]
    for copy in copies:
        copy.start()
    for copy in copies:
        copy.wait()


def cut(info, values):
    return run(
        cut_kernel,
        "cut",
        info,
        [values],
        [shape_of(values.shape[1:])] * 3,
        [pltpu.SemaphoreType.DMA((3,))],
        12,
        (1,),
        [ANY],
        [ANY] * 3,
    )


def shift(values, step):
    return lax.ppermute(values, "seq", [(k, (k + step) % 4) for k in range(4)])


def place_kernel(info, in_ref, out_ref):
    out_ref[...] = in_ref[...]


def place(info, values):
    return run(place_kernel, "place", info, [values], shape_of(values.shape))


def exchange(values):
    return lax.all_to_all(values, "seq", 0, 0)


def local_rows(
    tokens,
    lengths,
    w_query,
    w_key,
    w_value,
    w_out,
    w_gate,
    w_up,
    w_down,
    gain_attn,
    gain_ffn,
    cotangent,
):
    row_count, block_len, model_width = tokens.shape
    kv_width = HK * DH
    dp_at, seq_at = lax.axis_index("dp"), lax.axis_index("seq")
    length = lax.dynamic_slice_in_dim(lengths, seq_at, 1)
    info = jnp.concatenate([jnp.stack([seq_at, dp_at % 2, dp_at // 2]).astype(jnp.int32), length])
    half_dim = DH // 2
    positions = jnp.arange(row_count * block_len, dtype=jnp.float32).reshape(row_count, 1, -1)
    frequency = rope_base ** (-jnp.arange(half_dim, dtype=jnp.float32) / half_dim)
    angles = frequency[None, :, None] * positions
    angles = (jnp.cos(angles), jnp.sin(angles))
    w_heads = jnp.concatenate(
        [
            w_query.T.reshape(HK, GROUP * DH, model_width),
            w_key.T.reshape(HK, DH, model_width),
            w_value.T.reshape(HK, DH, model_width),
        ],
        axis=1,
    )
    w_heads_t = w_heads.reshape(-1, model_width).T
    gains = [
        jnp.broadcast_to(g[:, None], (model_width, block_len // 2)) for g in (gain_attn, gain_ffn)
    ]
    turned = [w_out.T, w_gate.T, w_up.T, w_down.T]

    row = exchange(jnp.swapaxes(tokens, 1, 2))
    cot, info, w_heads, w_heads_t, gains, angles, turned, w_down = lax.optimization_barrier(
        (
            jnp.swapaxes(cotangent, 1, 2),
            info,
            w_heads,
            w_heads_t,
            gains,
            angles,
            turned,
            w_down,
        )
    )
    Order.last, Order.also, Order.windows = None, (), False
    arrived = [shift(part, s + 1) for s, part in enumerate(cut(info, cot))]
    attn_in, queries, keys, values, attended, log_sum = attend(info, row, gains[0], w_heads, *angles)
    mixed, grad, grad_low, attended_grad, gain_ffn_part, *halves = ffn(
        info, row, attended, cot, arrived, gains[1], turned, [w_down, w_gate, w_up, w_out]
    )
    wide_sum = Sum(info, halves, TWO_ROUTES)
    Order.windows = True

    mixed_out = exchange(mixed)
    wide_sum.step()
    tokens_grad, *halves = back(
        info,
        (queries, keys, values, attended),
        attended_grad,
        log_sum,
        angles,
        (gains[0], gain_ffn_part),
        (row, grad, w_heads_t, attn_in, attended, grad_low),
    )
    wide_sum.step()
    Order.windows = False
    halves, Order.last = lax.optimization_barrier((halves, Order.last))
    attn_sum = DirectSum(info, halves)
    attn_sum.step()
    Order.also = (mixed_out,)
    wide_sum.step()
    wide_sum.step()
    attn_sum.step()
    wide_sum.step()
    attn_sum.step()
    wide_sum.step()
    attn_sum.step()
    wide_sum.step()
    tokens_grad, Order.last = lax.optimization_barrier((tokens_grad, Order.last))
    tokens_out = exchange(tokens_grad)
    Order.windows = True
    wide_sum.step()
    near_came = [swap(part, "dp", 1) for part in wide_sum.outs]
    attn_sum.step()
    square = shape_of((model_width, model_width), jnp.float32)
    narrow = shape_of((kv_width, model_width), jnp.float32)
    shapes = [square, narrow, narrow, square, shape_of((model_width, 128), jnp.float32)]
    w_query_sum, w_key_sum, w_value_sum, w_out_sum, gains_sum = run(
        join_attn_kernel,
        "join",
        info,
        [attn_sum.outs, *attn_sum.next],
        shapes,
        [pltpu.VMEM((32, PIECE_ROWS, PIECE_COLS), jnp.float32)],
        24,
        (1,),
        [once(*attn_sum.outs.shape)] * 2,
        [once(*v.shape) for v in shapes],
    )
    Order.also = tuple(near_came)
    mixed_out = place(info, mixed_out)
    parts, Order.last = lax.optimization_barrier((wide_sum.next, Order.last))
    far_came = [swap(part, "dp", 1) for part in parts]
    Order.also = (tokens_out,)
    tokens_out = place(info, tokens_out)
    w_gate_sum, w_up_sum, w_down_sum = join_wide(
        info, TWO_ROUTES, [*wide_sum.outs, *parts, *near_came, *far_came]
    )
    return (
        jnp.swapaxes(mixed_out, 1, 2),
        jnp.swapaxes(tokens_out, 1, 2),
        w_query_sum,
        w_key_sum.T,
        w_value_sum.T,
        w_out_sum,
        w_gate_sum,
        w_up_sum,
        w_down_sum.T,
        gains_sum[:, 64],
        gains_sum[:, 65],
    )


def solution(mesh):
    whole_rows = mesh.shape["dp"] == 8 and mesh.shape["seq"] == 4
    return jax.shard_map(
        local_rows if whole_rows else local_general,
        mesh=mesh,
        in_specs=(
            P("dp", "seq", None),
            P("dp"),
            P(),
            P(),
            P(),
            P(),
            P(),
            P(),
            P(),
            P(),
            P(),
            P("dp", "seq", None),
        ),
        out_specs=(
            P("dp", "seq", None),
            P("dp", "seq", None),
            P(),
            P(),
            P(),
            P(),
            P(),
            P(),
            P(),
            P(),
            P(),
        ),
        check_vma=False,
    )
```
